256 devices in a mesh: rows: 32 (over x, z), ch: 8 (over y, core).
Axes of the slice: x: 4, y: 4, z: 8, core: 2. Of those that a mesh axis runs over, the one named last changes fastest.
Arguments:
- inputs: bfloat16 [1, 512, 256, 256], P(None, 'rows', 'ch'), may hold values from -44 to 44
- w_expand: bfloat16 [256, 1536], P(None, 'ch'), may hold values from -0.375 to 0.375
- kernel: bfloat16 [9, 1536], P(None, 'ch'), may hold values from -2.390625 to 2.390625
- w_se1: bfloat16 [1536, 64], P('ch'), may hold values from -0.4375 to 0.4375
- w_se2: bfloat16 [64, 1536], P(None, 'ch'), may hold values from -1.5 to 1.5
- w_project: bfloat16 [1536, 256], P('ch'), may hold values from -0.4375 to 0.4375
- cotangent: bfloat16 [1, 512, 256, 256], P(None, 'rows', 'ch'), may hold values from -6 to 6
Outputs:
- output: bfloat16 [1, 512, 256, 256], P(None, 'rows', 'ch')
- d_input: bfloat16 [1, 512, 256, 256], P(None, 'rows', 'ch')
- d_w_expand: float32 [256, 1536], P(None, 'ch')
- d_kernel: float32 [9, 1536], P(None, 'ch')
- d_w_se1: float32 [1536, 64], P('ch')
- d_w_se2: float32 [64, 1536], P(None, 'ch')
- d_w_project: float32 [1536, 256], P('ch')
The draws below stay inside these ranges and needn't reach their ends.
All inputs are finite; a program needn't handle non-finite values.
Results may differ from the reference program's by a relative error of at most 0.028.
Values may be sent and summed in bfloat16 or wider, within the bound.
A program may use at most 64 MiB of HBM per device.

```python
import math
import jax
import jax.numpy as jnp
from jax import lax

C = 256
E = 1536
SE_DIM = 64
BATCH = 1
MAP_W = 256
MAP_H = 512


def draw_inputs(key, part):
    key = jax.random.fold_in(key, 11)
    subkeys = jax.random.split(key, 3)
    full_shape = (BATCH, MAP_H, MAP_W, C)
    rising = 3.0 ** (jnp.arange(MAP_H, dtype=jnp.float32) / max(MAP_H - 1, 1))
    chan_scale = jnp.exp(jax.random.uniform(subkeys[1], (C,), minval=math.log(0.4), maxval=math.log(2.5)))
    row_scale = jnp.exp(jax.random.uniform(subkeys[2], (BATCH, MAP_H, 1, 1), minval=-0.35, maxval=0.35))
    base_vals = jnp.clip(jax.random.normal(subkeys[0], full_shape), -4.0, 4.0)
    values = base_vals * chan_scale * rising[None, :, None, None] * row_scale
    return values.astype(jnp.bfloat16)


def steps_of(rng, dims, cuts, least, largest):
    def one(position, shards_of):
        steps = jax.random.uniform(jax.random.fold_in(jax.random.fold_in(rng, 6), position), (shards_of,), jnp.float32, least / len(cuts), largest / len(cuts))
        return jnp.repeat(jnp.exp(steps), dims[position] // shards_of).reshape((-1,) + (1,) * (len(dims) - position - 1))

    gain = one(*cuts[0])
    for cut in cuts[1:]:
        gain = gain * one(*cut)
    return gain


def bell_draw(rng, extent, deviation, bound, shards=(), held_as=jnp.bfloat16):
    drawn = deviation * jax.random.normal(rng, extent, jnp.float32)
    if shards:
        drawn = drawn * steps_of(rng, extent, shards, -0.22, 0.18)
    return jnp.clip(drawn, -bound, bound).astype(held_as)


def setup_inputs(seed: int = 0) -> dict:
    key_list = jax.random.split(jax.random.key(seed), 8)
    inputs = draw_inputs(jax.random.fold_in(key_list[7], 71), 0)
    w_expand = bell_draw(key_list[1], (C, E), C ** -0.5, 0.375, ((1, 8),))
    kernel = bell_draw(key_list[2], (9, E), 0.4, 2.390625, ((1, 8),))
    w_se1 = bell_draw(key_list[3], (E, SE_DIM), (E // 9) ** -0.5, 0.4375, ((0, 8),))
    w_se2 = bell_draw(key_list[4], (SE_DIM, E), (SE_DIM // 4) ** -0.5, 1.5, ((1, 8),))
    w_project = bell_draw(key_list[5], (E, C), (E // 9) ** -0.5, 0.4375, ((0, 8),))
    cotangent = bell_draw(key_list[6], (BATCH, MAP_H, MAP_W, C), 1.0, 6.0, ((1, 32), (2, 8)))
    return {"inputs": inputs, "w_expand": w_expand, "kernel": kernel, "w_se1": w_se1, "w_se2": w_se2, "w_project": w_project, "cotangent": cotangent}


def silu_slope(values):
    sig = jax.nn.sigmoid(values)
    return sig * (1.0 + values * (1.0 - sig))


def depth_apply(padded, kern, height, width):
    total = jnp.zeros((height, width, padded.shape[2]), jnp.float32)
    for tap_row in range(3):
        for tap_col in range(3):
            window = padded[tap_row:tap_row + height, tap_col:tap_col + width].astype(jnp.float32)
            total = total + kern[3 * tap_row + tap_col] * window
    return total


def tap_sums(grad_depth, padded, height, width):
    grad_vals = grad_depth.astype(jnp.float32)
    parts = []
    for tap_row in range(3):
        for tap_col in range(3):
            window = padded[tap_row:tap_row + height, tap_col:tap_col + width].astype(jnp.float32)
            parts.append(jnp.sum(grad_vals * window, axis=(0, 1)))
    return jnp.stack(parts)


def reference(inputs, w_expand, kernel, w_se1, w_se2, w_project, cotangent):
    highest = lax.Precision.HIGHEST
    height = inputs.shape[1]
    width = inputs.shape[2]
    chans = inputs.shape[3]
    expanded = w_expand.shape[1]
    area = height * width
    kern = kernel.astype(jnp.float32)
    se_down = w_se1.astype(jnp.float32)
    se_up = w_se2.astype(jnp.float32)

    def image_step(totals, pair):
        image, grad_out = pair
        flat_in = image.reshape(-1, chans)
        expand_pre = jnp.dot(flat_in, w_expand, preferred_element_type=jnp.float32).reshape(height, width, expanded)
        act_one = jax.nn.silu(expand_pre).astype(jnp.bfloat16)
        padded_one = jnp.pad(act_one, ((1, 1), (1, 1), (0, 0)))
        depth_pre = depth_apply(padded_one, kern, height, width)
        act_two = jax.nn.silu(depth_pre).astype(jnp.bfloat16)
        pooled = jnp.sum(act_two.astype(jnp.float32), axis=(0, 1)) / area
        squeeze_pre = jnp.dot(pooled, se_down, precision=highest)
        squeeze_act = jax.nn.silu(squeeze_pre)
        gate_vals = jax.nn.sigmoid(jnp.dot(squeeze_act, se_up, precision=highest))
        hidden = (act_two.astype(jnp.float32) * gate_vals).astype(jnp.bfloat16)
        flat_hidden = hidden.reshape(-1, expanded)
        projected = jnp.dot(flat_hidden, w_project, preferred_element_type=jnp.float32).reshape(height, width, chans)
        output = (image.astype(jnp.float32) + projected).astype(jnp.bfloat16)
        flat_grad = grad_out.reshape(-1, chans)
        grad_hidden = jnp.dot(flat_grad, w_project.T, preferred_element_type=jnp.float32).reshape(height, width, expanded)
        grad_project = jnp.dot(flat_hidden.T, flat_grad, preferred_element_type=jnp.float32)
        grad_gate = jnp.sum(grad_hidden * act_two.astype(jnp.float32), axis=(0, 1))
        grad_excite = grad_gate * gate_vals * (1.0 - gate_vals)
        grad_up = jnp.outer(squeeze_act, grad_excite)
        grad_squeeze = jnp.dot(grad_excite, se_up.T, precision=highest) * silu_slope(squeeze_pre)
        grad_down = jnp.outer(pooled, grad_squeeze)
        grad_pooled = jnp.dot(grad_squeeze, se_down.T, precision=highest)
        grad_act_two = grad_hidden * gate_vals + grad_pooled / area
        grad_depth = (grad_act_two * silu_slope(depth_pre)).astype(jnp.bfloat16)
        padded_grad = jnp.pad(grad_depth, ((1, 1), (1, 1), (0, 0)))
        grad_act_one = depth_apply(padded_grad, kern[::-1], height, width)
        grad_kern = tap_sums(grad_depth, padded_one, height, width)
        grad_expand_pre = (grad_act_one * silu_slope(expand_pre)).astype(jnp.bfloat16)
        flat_ge = grad_expand_pre.reshape(-1, expanded)
        grad_expand = jnp.dot(flat_in.T, flat_ge, preferred_element_type=jnp.float32)
        back_in = jnp.dot(flat_ge, w_expand.T, preferred_element_type=jnp.float32).reshape(height, width, chans)
        grad_input = (grad_out.astype(jnp.float32) + back_in).astype(jnp.bfloat16)
        fresh = (grad_expand, grad_kern, grad_down, grad_up, grad_project)
        totals = tuple(old + new for old, new in zip(totals, fresh))
        return totals, (output, grad_input)

    init = (jnp.zeros((chans, expanded), jnp.float32), jnp.zeros((9, expanded), jnp.float32),
            jnp.zeros((expanded, w_se1.shape[1]), jnp.float32), jnp.zeros((w_se1.shape[1], expanded), jnp.float32),
            jnp.zeros((expanded, chans), jnp.float32))
    totals, (output, d_input) = lax.scan(image_step, init, (inputs, cotangent))
    grad_scale = 1.0 / (inputs.shape[0] * height * width) ** 0.5
    return (output, d_input, totals[0] * grad_scale, totals[1] * grad_scale, totals[2] * grad_scale,
            totals[3] * grad_scale, totals[4] * grad_scale)
```

```python
import functools
import math

import jax
import jax.numpy as jnp
from jax import lax
from jax.experimental import pallas as pl
from jax.experimental.pallas import tpu as pltpu
from jax.sharding import PartitionSpec as P

MESH = pl.DeviceIdType.MESH
F32 = jnp.float32
BF16 = jnp.bfloat16

CHIPS_Z = 8
H = 16
W = 32
C = 256
S = 192
PW = 72
NT_DIMS = (((1,), (1,)), ((), ()))
TN_DIMS = (((0,), (0,)), ((), ()))


def split3(row):
    hi = row.astype(BF16).astype(F32)
    mid = (row - hi).astype(BF16).astype(F32)
    low = row - hi - mid
    rest = jnp.zeros((5, row.shape[1]), F32)
    return jnp.concatenate([hi, mid, low, rest], axis=0).astype(BF16)


def sigm(v):
    return 0.5 * jnp.tanh(0.5 * v) + 0.5


def fused(rows_n, ch_n, x_ref, c_ref, w_ref, se_ref, tap_ref,
          out_ref, din_ref, dwe_ref, dwp_ref, dk_ref, vec_ref,
          xsib, csib, rowsend, rowbuf, colsend, colbuf, wbuf, sebuf, tapbuf,
          xf, cf, xs, cs, xnat, cnat, a1, s1, gh, s2, act2, ge, ktile, gacc, dkacc,
          vbuf, zv, xv, cv, gs, ysend, yrecv, zsend, zrecv, xrecv, fsend, frecv,
          dksend, dkyr, dkzr, dkxs, dkxr, dkzs, posend, porecv,
          sib_s, sib_r, row_s, row_r, col_s, col_r, w_s, w_r, se_s, se_r, tap_s, tap_r,
          vz_s, vz_r, vx_s, vx_r, vc_s, vc_r, gy_s, gy_r, gz_s, gz_r, gx_s, gx_r, gf_s, gf_r,
          ky_s, ky_r, kz_s, kz_r, kx_s, kx_r, po_s, po_r):
    zn = CHIPS_Z if rows_n % CHIPS_Z == 0 else 2
    xn = rows_n // zn
    yn = ch_n // 2
    ce = S * yn
    nt = ce // 128
    pairs = yn // 2
    zr = S // (zn // 2)
    row = lax.axis_index("rows")
    ch = lax.axis_index("ch")
    mx, mz = row // zn, lax.rem(row, zn)
    my, mc = ch // 2, lax.rem(ch, 2)
    oc = 1 - mc

    def dev_row(step):
        return lax.rem(row + step + rows_n, rows_n)

    def dev_y(step):
        return lax.rem(my + step + yn, yn)

    def copy(src, dst, ssem, rsem, where):
        return pltpu.make_async_remote_copy(
            src_ref=src, dst_ref=dst, send_sem=ssem, recv_sem=rsem, device_id=where, device_id_type=MESH)

    def at_y(peer):
        return (row, peer * 2 + mc)

    def at_z(peer):
        return (mx * zn + peer, ch)

    def at_x(peer):
        return (peer * zn + mz, ch)

    def at_ch(peer):
        return (row, peer)

    def spread(n, me, at, src, land, ssem, rsem):
        for step in range(1, n):
            peer = lax.rem(me + step, n)
            copy(src(peer), land.at[me], ssem.at[step - 1], rsem.at[me], at(peer)).start()

    def gathered(n, me, at, src, land, ssem, rsem):
        for step in range(1, n):
            peer = lax.rem(me + step, n)
            copy(src(peer), land.at[peer], ssem.at[step - 1], rsem.at[peer], at(peer)).wait()

    barrier = pltpu.get_barrier_semaphore()
    partners = [at_ch(lax.rem(ch + s, ch_n)) for s in range(1, ch_n)]
    partners += [at_z(lax.rem(mz + s, zn)) for s in range(1, zn)]
    partners += [at_x(lax.rem(mx + s, xn)) for s in range(1, xn)]
    partners += [(dev_row(dr), my * 2 + core) for dr in (-1, 1) for core in (0, 1)]
    partners += [(dev_row(dr), dev_y(dy) * 2 + core) for dr in (-1, 0, 1) for dy in (-1, 1) for core in (0, 1)]
    for where in partners:
        pl.semaphore_signal(barrier, inc=1, device_id=where, device_id_type=MESH)

    for d, (lo, edge) in enumerate(((0, 0), (H - 2, H - 1))):
        rowsend[d, 0:2 * W] = x_ref[lo:lo + 2].reshape(2 * W, C)
        rowsend[d, 2 * W:3 * W] = c_ref[edge]
    first = mc * (W - 2)
    ri = lax.broadcasted_iota(jnp.int32, (2 * H, H * W), 0)
    ci = lax.broadcasted_iota(jnp.int32, (2 * H, H * W), 1)
    pick = (ci == (ri & (H - 1)) * W + first + (ri >> 4)).astype(F32).astype(BF16)
    colsend[0:2 * H] = jnp.dot(pick, x_ref[...].reshape(H * W, C), preferred_element_type=F32).astype(BF16)
    ri = lax.broadcasted_iota(jnp.int32, (H, H * W), 0)
    ci = lax.broadcasted_iota(jnp.int32, (H, H * W), 1)
    pick = (ci == ri * W + mc * (W - 1)).astype(F32).astype(BF16)
    colsend[2 * H:3 * H] = jnp.dot(pick, c_ref[...].reshape(H * W, C), preferred_element_type=F32).astype(BF16)

    pl.semaphore_wait(barrier, len(partners))

    sib = (row, my * 2 + oc)
    sib_copies = [copy(x_ref, xsib, sib_s.at[0], sib_r.at[0], sib), copy(c_ref, csib, sib_s.at[1], sib_r.at[1], sib)]
    row_copies = []
    for d, dr in ((0, -1), (1, 1)):
        for core in (0, 1):
            row_copies.append((copy(rowsend.at[d], rowbuf.at[1 - d, mc], row_s.at[d, core], row_r.at[1 - d, mc],
                                    (dev_row(dr), my * 2 + core)),
                               copy(rowsend.at[d], rowbuf.at[1 - d, core], row_s.at[d, core], row_r.at[1 - d, core],
                                    (dev_row(dr), my * 2 + core))))
    col_copies = []
    side = 1 - mc
    for i, dr in enumerate((-1, 0, 1)):
        for core in (0, 1):
            where = (dev_row(dr), dev_y(2 * mc - 1) * 2 + core)
            col_copies.append((copy(colsend, colbuf.at[side, 2 - i], col_s.at[i, core], col_r.at[side, 2 - i], where),
                               copy(colsend, colbuf.at[core, i], col_s.at[i, core], col_r.at[core, i], where)))
    for sent in sib_copies:
        sent.start()
    for sent, _ in row_copies + col_copies:
        sent.start()
    spread(yn, my, at_y, lambda p: tap_ref, tapbuf, tap_s, tap_r)
    spread(yn, my, at_y, lambda p: w_ref, wbuf, w_s, w_r)
    spread(ch_n, ch, at_ch, lambda p: se_ref, sebuf, se_s, se_r)

    wbuf[my] = w_ref[...]
    tapbuf[my] = tap_ref[...]
    sebuf[ch] = se_ref[...]
    mine = pl.ds(pl.multiple_of(mc * W, W), W)
    other = pl.ds(pl.multiple_of(oc * W, W), W)
    xf[2:2 + H, mine] = x_ref[...].astype(F32)
    cf[1:1 + H, mine] = c_ref[...].astype(F32)
    xnat[:, mine] = x_ref[...]
    cnat[:, mine] = c_ref[...]
    for sent in sib_copies:
        sent.wait()
    xf[2:2 + H, other] = xsib[...].astype(F32)
    cf[1:1 + H, other] = csib[...].astype(F32)
    xnat[:, other] = xsib[...]
    cnat[:, other] = csib[...]
    for _, landed in row_copies + col_copies:
        landed.wait()

    top_ok = row > 0
    low_ok = row < rows_n - 1
    left_ok = my > 0
    right_ok = my < yn - 1
    for d, ok in ((0, top_ok), (1, low_ok)):
        for core in (0, 1):
            part = rowbuf[d, core].astype(F32) * jnp.where(ok, 1.0, 0.0)
            xf[(2 + H) * d:(2 + H) * d + 2, W * core:W * core + W] = part[0:2 * W].reshape(2, W, C)
            cf[(1 + H) * d, W * core:W * core + W] = part[2 * W:3 * W]
    cols = colbuf[...].reshape(2 * 3 * 48, C)

    def rim(height, above, left_slot, right_slot):
        shape = (height * 8, 288)
        out_row = lax.broadcasted_iota(jnp.int32, shape, 0)
        src = lax.broadcasted_iota(jnp.int32, shape, 1)
        place = out_row & 7
        at_row = (out_row >> 3) - above
        third = jnp.where(at_row < 0, 0, jnp.where(at_row < H, 1, 2))
        ok = jnp.where(at_row < 0, top_ok.astype(jnp.int32), jnp.where(at_row < H, 1, low_ok.astype(jnp.int32)))
        want = third * 48 + (at_row & (H - 1))
        right_of = jnp.where(place < 4, 1, 0)
        slot = jnp.where(place < 4, right_slot(place), left_slot(place))
        ok = ok * jnp.where(slot < 0, 0, 1) * jnp.where(place < 4, right_ok.astype(jnp.int32), left_ok.astype(jnp.int32))
        want = want + right_of * 144 + slot * 16
        hit = jnp.where(src == want, ok, 0).astype(F32).astype(BF16)
        return jnp.dot(hit, cols, preferred_element_type=F32).reshape(height, 8, C)

    xf[:, 64:72] = rim(H + 4, 2, lambda k: jnp.where(k >= 6, k - 6, -1), lambda k: jnp.where(k < 2, k, -1))
    cf[:, 64:72] = rim(H + 2, 1, lambda k: jnp.where(k == 7, 2, -1), lambda k: jnp.where(k == 0, 2, -1))

    @pl.loop(0, (H + 4) // 2)
    def _(i):
        at = pl.ds(pl.multiple_of(i * 2 * PW, 2 * PW), 2 * PW)
        xs[at] = xf[pl.ds(i * 2, 2)].reshape(2 * PW, C).astype(BF16)

    @pl.loop(0, (H + 2) // 2)
    def _(i):
        at = pl.ds(pl.multiple_of(i * 2 * PW, 2 * PW), 2 * PW)
        cs[at] = cf[pl.ds(i * 2, 2)].reshape(2 * PW, C).astype(BF16)

    gathered(yn, my, at_y, lambda p: tap_ref, tapbuf, tap_s, tap_r)
    wide = jnp.concatenate([tapbuf[q].astype(F32)[:, 0:S] for q in range(yn)], axis=1)
    for t in range(nt):
        ktile[t] = wide[:, 128 * t:128 * t + 128]
    gathered(yn, my, at_y, lambda p: w_ref, wbuf, w_s, w_r)

    for b in range(pairs):
        pair = lax.rem(my // 2 + b, pairs)
        w_exp = wbuf[pl.ds(pair * 2, 2), 0].reshape(2 * S, C)
        w_pro = wbuf[pl.ds(pair * 2, 2), 1].reshape(2 * S, C)

        @pl.loop(0, (H + 4) // 2)
        def _(i):
            at = pl.ds(pl.multiple_of(i * 2 * PW, 2 * PW), 2 * PW)
            pre = lax.dot_general(xs[at], w_exp, NT_DIMS, preferred_element_type=F32)
            sig = sigm(pre)
            act = pre * sig
            slope = sig * (1.0 + (pre - act))
            for t in range(3):
                a1[pair * 3 + t, pl.ds(i * 2, 2)] = act[:, 128 * t:128 * t + 128].reshape(2, PW, 128)
                s1[pair * 3 + t, pl.ds(i * 2, 2)] = slope[:, 128 * t:128 * t + 128].reshape(2, PW, 128)

        @pl.loop(0, (H + 2) // 2)
        def _(i):
            at = pl.ds(pl.multiple_of(i * 2 * PW, 2 * PW), 2 * PW)
            back = lax.dot_general(cs[at], w_pro, NT_DIMS, preferred_element_type=F32)
            for t in range(3):
                gh[pair * 3 + t, pl.ds(i * 2, 2)] = back[:, 128 * t:128 * t + 128].reshape(2, PW, 128)

        @pl.loop(0, 3)
        def _(t3):
            t = pair * 3 + t3
            lanes = pl.ds(pl.multiple_of(t * 128, 128), 128)
            taps = [ktile[t, k:k + 1] for k in range(9)]

            def one_row(i):
                rows = [a1[t, i + r] for r in range(3)]
                parts = [taps[c] * rows[0] + taps[3 + c] * rows[1] + taps[6 + c] * rows[2] for c in range(3)]
                pre = parts[1] + pltpu.roll(parts[0], 1, 0) + pltpu.roll(parts[2], PW - 1, 0)
                sig = sigm(pre)
                act = pre * sig
                s2[t, i] = sig * (1.0 + (pre - act))
                return act[0:64]

            def center(i, sums):
                pool, gate_sum = sums
                act = one_row(i)
                act2[i - 1, :, lanes] = act.astype(BF16)
                pool = pool + jnp.sum(act.reshape(8, 8, 128), axis=0)
                gate_sum = gate_sum + jnp.sum((act * gh[t, i, 0:64]).reshape(8, 8, 128), axis=0)
                return pool, gate_sum

            one_row(0)
            one_row(H + 1)
            zero = jnp.zeros((8, 128), F32)
            pool, gate_sum = lax.fori_loop(1, H + 1, center, (zero, zero))
            vbuf[pl.ds(t, 1)] = jnp.sum(pool, axis=0, keepdims=True)
            vbuf[pl.ds(8 + t, 1)] = jnp.sum(gate_sum, axis=0, keepdims=True)

    for t in range(nt, 8):
        vbuf[t:t + 1] = jnp.zeros((1, 128), F32)
        vbuf[8 + t:9 + t] = jnp.zeros((1, 128), F32)

    spread(zn, mz, at_z, lambda p: vbuf, zv, vz_s, vz_r)
    zv[mz] = vbuf[...]

    def send_rows(g, value):
        ysend[g] = value.reshape(yn, S, C).astype(BF16)
        spread(yn, my, at_y, lambda p: ysend.at[g, p], yrecv.at[g], gy_s.at[g], gy_r.at[g])
        yrecv[g, my] = ysend[g, my]

    def send_z(g):
        gathered(yn, my, at_y, lambda p: ysend.at[g, p], yrecv.at[g], gy_s.at[g], gy_r.at[g])
        total = yrecv[g, 0].astype(F32)
        for q in range(1, yn):
            total = total + yrecv[g, q].astype(F32)
        for q in range(zn):
            zsend[g, q] = total[zr * (q // 2):zr * (q // 2) + zr, 128 * (q % 2):128 * (q % 2) + 128].astype(BF16)
        spread(zn, mz, at_z, lambda p: zsend.at[g, p], zrecv.at[g], gz_s.at[g], gz_r.at[g])
        zrecv[g, mz] = zsend[g, mz]

    def send_x(g):
        gathered(zn, mz, at_z, lambda p: zsend.at[g, p], zrecv.at[g], gz_s.at[g], gz_r.at[g])
        total = zrecv[g, 0].astype(F32)
        for q in range(1, zn):
            total = total + zrecv[g, q].astype(F32)
        fsend[g, 0] = total.astype(BF16)
        spread(xn, mx, at_x, lambda p: fsend.at[g, 0], xrecv.at[g], gx_s.at[g], gx_r.at[g])
        xrecv[g, mx] = fsend[g, 0]

    def send_back(g):
        gathered(xn, mx, at_x, lambda p: fsend.at[g, 0], xrecv.at[g], gx_s.at[g], gx_r.at[g])
        total = xrecv[g, 0].astype(F32)
        for q in range(1, xn):
            total = total + xrecv[g, q].astype(F32)
        fsend[g, 1] = total.astype(BF16)
        spread(zn, mz, at_z, lambda p: fsend.at[g, 1], frecv.at[g], gf_s.at[g], gf_r.at[g])
        frecv[g, mz] = fsend[g, 1]

    def whole(g, into):
        gathered(zn, mz, at_z, lambda p: fsend.at[g, 1], frecv.at[g], gf_s.at[g], gf_r.at[g])
        for q in range(zn):
            into[zr * (q // 2):zr * (q // 2) + zr, 128 * (q % 2):128 * (q % 2) + 128] = frecv[g, q].astype(F32)

    cot_flat = cnat[...].reshape(H * 64, C)
    for t in range(ce // 384):
        gacc[384 * t:384 * t + 384] = lax.dot_general(
            act2[:, :, 384 * t:384 * t + 384].reshape(H * 64, 384), cot_flat, TN_DIMS, preferred_element_type=F32)
    send_rows(0, gacc[...])

    gathered(zn, mz, at_z, lambda p: vbuf, zv, vz_s, vz_r)
    vbuf2 = jnp.sum(zv[...], axis=0)
    xv[mx] = vbuf2
    spread(xn, mx, at_x, lambda p: xv.at[mx], xv, vx_s, vx_r)
    gathered(xn, mx, at_x, lambda p: xv.at[mx], xv, vx_s, vx_r)
    cv[ch] = jnp.sum(xv[...], axis=0)
    spread(ch_n, ch, at_ch, lambda p: cv.at[ch], cv, vc_s, vc_r)
    gathered(ch_n, ch, at_ch, lambda p: cv.at[ch], cv, vc_s, vc_r)
    gathered(ch_n, ch, at_ch, lambda p: se_ref, sebuf, se_s, se_r)

    area = float(rows_n * H * yn * 2 * W)
    pooled, gate_grad, weights = [], [], []
    for core in (0, 1):
        total = cv[core]
        for q in range(1, yn):
            total = total + cv[2 * q + core]
        pooled.append(jnp.concatenate([total[t:t + 1] for t in range(nt)], axis=1) * (1.0 / area))
        gate_grad.append(jnp.concatenate([total[8 + t:9 + t] for t in range(nt)], axis=1))
        weights.append(jnp.concatenate([sebuf[2 * q + core] for q in range(yn)], axis=0))
    half = lax.broadcasted_iota(jnp.int32, (1, 128), 1) < 64

    def down(vectors):
        total = jnp.zeros((1, 128), F32)
        for core in (0, 1):
            total = total + jnp.sum(jnp.dot(split3(vectors[core]), weights[core], preferred_element_type=F32), axis=0, keepdims=True)
        return total

    def up(vector, core):
        return jnp.sum(lax.dot_general(split3(vector), weights[core], NT_DIMS, preferred_element_type=F32), axis=0, keepdims=True)

    squeeze_pre = jnp.where(half, down(pooled), 0.0)
    squeeze_sig = sigm(squeeze_pre)
    squeeze_act = squeeze_pre * squeeze_sig
    shifted = pltpu.roll(jnp.broadcast_to(squeeze_act, (8, 128)), 64, 1)[0:1]
    gates = [sigm(up(shifted, core)) for core in (0, 1)]
    excite = [gate_grad[core] * gates[core] * (1.0 - gates[core]) for core in (0, 1)]
    back = pltpu.roll(jnp.broadcast_to(down(excite), (8, 128)), 64, 1)[0:1]
    squeeze_slope = squeeze_sig * (1.0 + squeeze_pre * (1.0 - squeeze_sig))
    grad_squeeze = jnp.where(half, back * squeeze_slope, 0.0)

    def own(values):
        return jnp.where(mc == 0, values[0], values[1])

    gate = own(gates)
    grad_pool = own([up(grad_squeeze, core) for core in (0, 1)]) * (1.0 / area)
    for t in range(nt):
        gs[0, t:t + 1] = gate[:, 128 * t:128 * t + 128]
        gs[1, t:t + 1] = grad_pool[:, 128 * t:128 * t + 128]
    vec_ref[0:1] = gate
    vec_ref[1:2] = own(pooled)
    vec_ref[2:3] = own(excite)
    small = jnp.concatenate([squeeze_act, grad_squeeze] + [jnp.zeros((1, 128), F32)] * (nt - 2), axis=1)
    vec_ref[3:4] = small
    vec_ref[4:8] = jnp.zeros((4, ce), F32)

    send_z(0)

    @pl.loop(0, H)
    def _(i):
        act2[i] = (act2[i].astype(F32) * gate).astype(BF16)

    def project(source, k, w_all, base, into):
        def part(where):
            rows = source[:, where].reshape(H * W, ce)
            return jnp.dot(rows, w_all, preferred_element_type=F32).reshape(H, W, C)

        posend[k] = part(other).astype(BF16)
        copy(posend.at[k], porecv.at[k], po_s.at[k], po_r.at[k], sib).start()
        into[...] = part(mine)

    def projected(k, base, total, into):
        copy(posend.at[k], porecv.at[k], po_s.at[k], po_r.at[k], sib).wait()
        into[...] = (base[...].astype(F32) + (total[...] + porecv[k].astype(F32))).astype(BF16)

    project(act2, 0, wbuf[:, 1].reshape(ce, C), x_ref, xf.at[0:H, 0:W])
    send_x(0)

    place = lax.broadcasted_iota(jnp.int32, (PW, 128), 0)
    off_left = jnp.where(left_ok, PW, PW - 1)
    off_right = jnp.where(right_ok, 0, 1)
    inside = jnp.where((place < 64) | ((place == 64) & (off_right == 0)) | ((place == PW - 1) & (off_left == PW)), 1.0, 0.0)

    @pl.loop(0, nt)
    def _(t):
        lanes = pl.ds(pl.multiple_of(t * 128, 128), 128)
        taps = [ktile[t, k:k + 1] for k in range(9)]
        gate_t = gs[0, pl.ds(t, 1)]
        pool_t = gs[1, pl.ds(t, 1)]

        @pl.loop(0, H + 2)
        def _(i):
            keep = jnp.where(((i > 0) | top_ok) & ((i < H + 1) | low_ok), 1.0, 0.0)
            gh[t, i] = (gh[t, i] * gate_t + pool_t) * s2[t, i] * (inside * keep)

        def center(i, sums):
            rows = [gh[t, i + r] for r in range(3)]
            parts = [taps[c] * rows[2] + taps[3 + c] * rows[1] + taps[6 + c] * rows[0] for c in range(3)]
            grad = parts[1] + pltpu.roll(parts[0], PW - 1, 0) + pltpu.roll(parts[2], 1, 0)
            full = grad[0:64] * s1[t, i + 2, 0:64]
            ge[i, :, lanes] = full.astype(BF16)
            here = jnp.concatenate([rows[1][0:64], jnp.zeros((8, 128), F32)], axis=0)
            moved = [pltpu.roll(here, PW - 1, 0), here, pltpu.roll(here, 1, 0)]
            fresh = []
            for r in range(3):
                act = a1[t, i + 1 + r]
                for c in range(3):
                    fresh.append(sums[3 * r + c] + jnp.sum((moved[c] * act).reshape(9, 8, 128), axis=0))
            return tuple(fresh)

        sums = lax.fori_loop(0, H, center, (jnp.zeros((8, 128), F32),) * 9)
        dkacc[t] = jnp.concatenate(
            [jnp.sum(part, axis=0, keepdims=True) for part in sums] + [jnp.zeros((7, 128), F32)], axis=0)

    send_back(0)
    x_flat = xnat[...].reshape(H * 64, C)
    for t in range(ce // 384):
        gacc[384 * t:384 * t + 384] = lax.dot_general(
            ge[:, :, 384 * t:384 * t + 384].reshape(H * 64, 384), x_flat, TN_DIMS, preferred_element_type=F32)
    send_rows(1, gacc[...])
    dksend[...] = jnp.concatenate([dkacc[t] for t in range(nt)], axis=1).astype(BF16)
    spread(yn, my, at_y, lambda p: dksend, dkyr, ky_s, ky_r)
    dkyr[my] = dksend[...]
    project(ge, 1, wbuf[:, 0].reshape(ce, C), c_ref, cf.at[0:H, 0:W])

    send_z(1)
    gathered(yn, my, at_y, lambda p: dksend, dkyr, ky_s, ky_r)
    total = dkyr[0].astype(F32)
    for q in range(1, yn):
        total = total + dkyr[q].astype(F32)
    mine_k = total[:, 0:S]
    for q in range(1, yn):
        mine_k = jnp.where(my == q, total[:, S * q:S * q + S], mine_k)
    dkzs[...] = jnp.concatenate([mine_k, jnp.zeros((16, 256 - S), F32)], axis=1).astype(BF16)
    spread(zn, mz, at_z, lambda p: dkzs, dkzr, kz_s, kz_r)
    dkzr[mz] = dkzs[...]
    projected(0, x_ref, xf.at[0:H, 0:W], out_ref)
    whole(0, dwp_ref)
    send_x(1)
    gathered(zn, mz, at_z, lambda p: dkzs, dkzr, kz_s, kz_r)
    total = dkzr[0].astype(F32)
    for q in range(1, zn):
        total = total + dkzr[q].astype(F32)
    dkxs[...] = total.astype(BF16)
    spread(xn, mx, at_x, lambda p: dkxs, dkxr, kx_s, kx_r)
    dkxr[mx] = dkxs[...]
    projected(1, c_ref, cf.at[0:H, 0:W], din_ref)
    send_back(1)
    gathered(xn, mx, at_x, lambda p: dkxs, dkxr, kx_s, kx_r)
    total = dkxr[0].astype(F32)
    for q in range(1, xn):
        total = total + dkxr[q].astype(F32)
    dk_ref[...] = total
    whole(1, dwe_ref)


def per_device(inputs, w_expand, kernel, w_se1, w_se2, w_project, cotangent):
    rows_n, ch_n = lax.axis_size("rows"), lax.axis_size("ch")
    zn = CHIPS_Z if rows_n % CHIPS_Z == 0 else 2
    xn, yn = rows_n // zn, ch_n // 2
    ce = S * yn
    nt = ce // 128
    zr = S // (zn // 2)
    grad_scale = 1.0 / math.sqrt(rows_n * H * ch_n * W)
    weights = jnp.stack([w_expand.T, w_project])
    se = jnp.concatenate([w_se1, w_se2.T], axis=1)
    taps = jnp.pad(kernel, ((0, 7), (0, 256 - S)))
    vmem, dma = pltpu.VMEM, pltpu.SemaphoreType.DMA
    scratch = [
        vmem((H, W, C), BF16), vmem((H, W, C), BF16),
        vmem((2, 3 * W, C), BF16), vmem((2, 2, 3 * W, C), BF16),
        vmem((3 * H, C), BF16), vmem((2, 3, 3 * H, C), BF16),
        vmem((yn, 2, S, C), BF16), vmem((ch_n, S, 128), BF16), vmem((yn, 16, 256), BF16),
        vmem((H + 4, PW, C), F32), vmem((H + 2, PW, C), F32),
        vmem(((H + 4) * PW, C), BF16), vmem(((H + 2) * PW, C), BF16),
        vmem((H, 64, C), BF16), vmem((H, 64, C), BF16),
        vmem((nt, H + 4, PW, 128), F32), vmem((nt, H + 4, PW, 128), F32),
        vmem((nt, H + 2, PW, 128), F32), vmem((nt, H + 2, PW, 128), F32),
        vmem((H, 64, ce), BF16), vmem((H, 64, ce), BF16),
        vmem((nt, 16, 128), F32), vmem((ce, C), F32), vmem((nt, 16, 128), F32),
        vmem((16, 128), F32), vmem((zn, 16, 128), F32), vmem((xn, 16, 128), F32), vmem((ch_n, 16, 128), F32),
        vmem((2, 8, 128), F32),
        vmem((2, yn, S, C), BF16), vmem((2, yn, S, C), BF16),
        vmem((2, zn, zr, 128), BF16), vmem((2, zn, zr, 128), BF16),
        vmem((2, xn, zr, 128), BF16), vmem((2, 2, zr, 128), BF16), vmem((2, zn, zr, 128), BF16),
        vmem((16, ce), BF16), vmem((yn, 16, ce), BF16),
        vmem((zn, 16, 256), BF16), vmem((16, 256), BF16), vmem((xn, 16, 256), BF16), vmem((16, 256), BF16),
        vmem((2, H, W, C), BF16), vmem((2, H, W, C), BF16),
        dma((2,)), dma((2,)), dma((2, 2)), dma((2, 2)), dma((3, 2)), dma((2, 3)),
        dma((yn,)), dma((yn,)), dma((ch_n,)), dma((ch_n,)), dma((yn,)), dma((yn,)),
        dma((zn,)), dma((zn,)), dma((xn,)), dma((xn,)), dma((ch_n,)), dma((ch_n,)),
        dma((2, yn)), dma((2, yn)), dma((2, zn)), dma((2, zn)), dma((2, xn)), dma((2, xn)), dma((2, zn)), dma((2, zn)),
        dma((yn,)), dma((yn,)), dma((zn,)), dma((zn,)), dma((xn,)), dma((xn,)),
        dma((2,)), dma((2,)),
    ]
    in_vmem = pl.BlockSpec(memory_space=pltpu.VMEM)
    output, d_input, d_expand_t, d_project, d_taps, vec = pl.pallas_call(
        functools.partial(fused, rows_n, ch_n),
        out_shape=(
            jax.ShapeDtypeStruct((H, W, C), BF16), jax.ShapeDtypeStruct((H, W, C), BF16),
            jax.ShapeDtypeStruct((S, C), F32), jax.ShapeDtypeStruct((S, C), F32),
            jax.ShapeDtypeStruct((16, 256), F32), jax.ShapeDtypeStruct((8, ce), F32)),
        in_specs=[in_vmem] * 5,
        out_specs=(in_vmem,) * 6,
        scratch_shapes=scratch,
        compiler_params=pltpu.CompilerParams(
            collective_id=0, has_side_effects=True, vmem_limit_bytes=56 * 1024 * 1024),
    )(inputs[0], cotangent[0], weights, se, taps)
    start = (lax.axis_index("ch") // 2) * S
    own = lax.dynamic_slice_in_dim(vec, start, S, axis=1)
    gate, pooled, excite = own[0], own[1], own[2]
    squeeze_act, grad_squeeze = vec[3, 0:64], vec[3, 128:192]
    return (
        output[None], d_input[None], d_expand_t.T * grad_scale, d_taps[0:9, 0:S] * grad_scale,
        jnp.outer(pooled, grad_squeeze) * grad_scale, jnp.outer(squeeze_act, excite) * grad_scale,
        d_project * (gate[:, None] * grad_scale))


def solution(mesh):
    return jax.shard_map(
        per_device,
        mesh=mesh,
        in_specs=(
            P(None, "rows", "ch", None),
            P(None, "ch"),
            P(None, "ch"),
            P("ch", None),
            P(None, "ch"),
            P("ch", None),
            P(None, "rows", "ch", None),
        ),
        out_specs=(
            P(None, "rows", "ch", None),
            P(None, "rows", "ch", None),
            P(None, "ch"),
            P(None, "ch"),
            P("ch", None),
            P(None, "ch"),
            P("ch", None),
        ),
        check_vma=False,
    )
```

```python
import functools
import math

import jax
import jax.numpy as jnp
from jax import lax
from jax.experimental import pallas as pl
from jax.experimental.pallas import tpu as pltpu
from jax.sharding import PartitionSpec as P

MESH = pl.DeviceIdType.MESH
F32 = jnp.float32
BF16 = jnp.bfloat16

CHIPS_Z = 8
H = 16
W = 32
C = 256
S = 192
PW = 72
NT_DIMS = (((1,), (1,)), ((), ()))
TN_DIMS = (((0,), (0,)), ((), ()))


def split3(row):
    hi = row.astype(BF16).astype(F32)
    mid = (row - hi).astype(BF16).astype(F32)
    low = row - hi - mid
    rest = jnp.zeros((5, row.shape[1]), F32)
    return jnp.concatenate([hi, mid, low, rest], axis=0).astype(BF16)


def sigm(v):
    return 0.5 * jnp.tanh(0.5 * v) + 0.5


def pairs3(left, right):
    def three(row):
        hi = row.astype(BF16).astype(F32)
        mid = (row - hi).astype(BF16).astype(F32)
        return hi, mid, row - hi - mid

    a, b = three(left), three(right)
    lefts = jnp.concatenate([a[k] for k in (0, 0, 1, 1, 0, 2, 1, 2)], axis=0).astype(BF16)
    rights = jnp.concatenate([b[k] for k in (0, 1, 0, 1, 2, 0, 2, 1)], axis=0).astype(BF16)
    return lefts, rights


def fused(rows_n, ch_n, scale, x_in, we_ref, tap_ref, se1_ref, se2_ref, wp_ref, c_in,
          out_ref, din_ref, dwe_ref, dk_ref, dse1_ref, dse2_ref, dwp_ref,
          xsib, csib, rowsend, rowbuf, colsend, colbuf, wesend, webuf, wpbuf, sesend, sebuf, tapsend, tapbuf,
          xf, cf, xs, cs, xnat, cnat, a1, s1, gh, s2, act2, ge, ktile, gacc, dkacc,
          vbuf, zv, xv, cv, gs, ysend, yrecv, zsend, zrecv, xrecv, fsend, frecv,
          dksend, dkyr, dkzr, dkxs, dkxr, dkzs, posend, porecv,
          sib_s, sib_r, row_s, row_r, col_s, col_r, we_s, we_r, wp_s, wp_r, se_s, se_r, rel_s, rel_r, tap_s, tap_r,
          vz_s, vz_r, vx_s, vx_r, vc_s, vc_r, gy_s, gy_r, gz_s, gz_r, gx_s, gx_r, gf_s, gf_r,
          ky_s, ky_r, kz_s, kz_r, kx_s, kx_r, po_s, po_r):
    x_ref, c_ref = x_in.at[0], c_in.at[0]
    zn = CHIPS_Z if rows_n % CHIPS_Z == 0 else 2
    xn = rows_n // zn
    yn = ch_n // 2
    ce = S * yn
    nt = ce // 128
    pairs = yn // 2
    zr = S // (zn // 2)
    row = lax.axis_index("rows")
    ch = lax.axis_index("ch")
    mx, mz = row // zn, lax.rem(row, zn)
    my, mc = ch // 2, lax.rem(ch, 2)
    oc = 1 - mc

    def dev_row(step):
        return lax.rem(row + step + rows_n, rows_n)

    def dev_y(step):
        return lax.rem(my + step + yn, yn)

    def copy(src, dst, ssem, rsem, where):
        return pltpu.make_async_remote_copy(
            src_ref=src, dst_ref=dst, send_sem=ssem, recv_sem=rsem, device_id=where, device_id_type=MESH)

    def at_y(peer):
        return (row, peer * 2 + mc)

    def at_z(peer):
        return (mx * zn + peer, ch)

    def at_x(peer):
        return (peer * zn + mz, ch)

    def at_ch(peer):
        return (row, peer)

    def spread(n, me, at, src, land, ssem, rsem):
        for step in range(1, n):
            peer = lax.rem(me + step, n)
            copy(src(peer), land.at[me], ssem.at[step - 1], rsem.at[me], at(peer)).start()

    def gathered(n, me, at, src, land, ssem, rsem):
        for step in range(1, n):
            peer = lax.rem(me + step, n)
            copy(src(peer), land.at[peer], ssem.at[step - 1], rsem.at[peer], at(peer)).wait()

    pair_mine = my // 2
    near = my + 1 - 2 * lax.rem(my, 2)
    far = [lax.rem(pair_mine + b, pairs) * 2 + k for b in range(1, pairs) for k in (0, 1)]

    def to_y(peers, first, src, land, ssem, rsem):
        for k, peer in enumerate(peers):
            copy(src(peer), land.at[my], ssem.at[first + k], rsem.at[my], at_y(peer)).start()

    def from_y(peers, first, src, land, ssem, rsem):
        for k, peer in enumerate(peers):
            copy(src(peer), land.at[peer], ssem.at[first + k], rsem.at[peer], at_y(peer)).wait()

    barrier = pltpu.get_barrier_semaphore()
    partners = [at_ch(lax.rem(ch + s, ch_n)) for s in range(1, ch_n)]
    partners += [at_z(lax.rem(mz + s, zn)) for s in range(1, zn)]
    partners += [at_x(lax.rem(mx + s, xn)) for s in range(1, xn)]
    partners += [(dev_row(dr), my * 2 + core) for dr in (-1, 1) for core in (0, 1)]
    partners += [(dev_row(dr), dev_y(dy) * 2 + core) for dr in (-1, 0, 1) for dy in (-1, 1) for core in (0, 1)]
    for where in partners:
        pl.semaphore_signal(barrier, inc=1, device_id=where, device_id_type=MESH)

    for d, (lo, edge) in enumerate(((0, 0), (H - 2, H - 1))):
        rowsend[d, 0:2 * W] = x_ref[lo:lo + 2].reshape(2 * W, C)
        rowsend[d, 2 * W:3 * W] = c_ref[edge]
    first = mc * (W - 2)
    ri = lax.broadcasted_iota(jnp.int32, (2 * H, H * W), 0)
    ci = lax.broadcasted_iota(jnp.int32, (2 * H, H * W), 1)
    pick = (ci == (ri & (H - 1)) * W + first + (ri >> 4)).astype(F32).astype(BF16)
    colsend[0:2 * H] = jnp.dot(pick, x_ref[...].reshape(H * W, C), preferred_element_type=F32).astype(BF16)
    ri = lax.broadcasted_iota(jnp.int32, (H, H * W), 0)
    ci = lax.broadcasted_iota(jnp.int32, (H, H * W), 1)
    pick = (ci == ri * W + mc * (W - 1)).astype(F32).astype(BF16)
    colsend[2 * H:3 * H] = jnp.dot(pick, c_ref[...].reshape(H * W, C), preferred_element_type=F32).astype(BF16)

    eye = (lax.broadcasted_iota(jnp.int32, (S, S), 0) == lax.broadcasted_iota(jnp.int32, (S, S), 1)).astype(F32).astype(BF16)
    wesend[...] = lax.dot_general(eye, we_ref[...], NT_DIMS, preferred_element_type=F32).astype(BF16)
    se2_t = lax.dot_general(eye, se2_ref[...], NT_DIMS, preferred_element_type=F32)
    sesend[...] = jnp.concatenate([se1_ref[...].astype(F32), se2_t], axis=1).astype(BF16)
    tap_rows = jnp.concatenate([tap_ref[...].astype(F32), jnp.zeros((7, S), F32)], axis=0)
    tapsend[...] = jnp.concatenate([tap_rows, jnp.zeros((16, 256 - S), F32)], axis=1).astype(BF16)

    pl.semaphore_wait(barrier, len(partners))

    sib = (row, my * 2 + oc)
    sib_copies = [copy(x_ref, xsib, sib_s.at[0], sib_r.at[0], sib), copy(c_ref, csib, sib_s.at[1], sib_r.at[1], sib)]
    row_copies = []
    for d, dr in ((0, -1), (1, 1)):
        for core in (0, 1):
            row_copies.append((copy(rowsend.at[d], rowbuf.at[1 - d, mc], row_s.at[d, core], row_r.at[1 - d, mc],
                                    (dev_row(dr), my * 2 + core)),
                               copy(rowsend.at[d], rowbuf.at[1 - d, core], row_s.at[d, core], row_r.at[1 - d, core],
                                    (dev_row(dr), my * 2 + core))))
    col_copies = []
    side = 1 - mc
    for i, dr in enumerate((-1, 0, 1)):
        for core in (0, 1):
            where = (dev_row(dr), dev_y(2 * mc - 1) * 2 + core)
            col_copies.append((copy(colsend, colbuf.at[side, 2 - i], col_s.at[i, core], col_r.at[side, 2 - i], where),
                               copy(colsend, colbuf.at[core, i], col_s.at[i, core], col_r.at[core, i], where)))
    sib_copies[0].start()
    for sent, _ in row_copies + col_copies:
        sent.start()
    to_y([near], 0, lambda p: wesend, webuf, we_s, we_r)
    spread(yn, my, at_y, lambda p: tapsend, tapbuf, tap_s, tap_r)
    sib_copies[1].start()
    to_y(far, 1, lambda p: wesend, webuf, we_s, we_r)
    to_y([near] + far, 0, lambda p: wp_ref, wpbuf, wp_s, wp_r)
    spread(yn, my, at_y, lambda p: sesend, sebuf.at[mc], se_s, se_r)
    relay = copy(sebuf.at[mc], sebuf.at[mc], rel_s.at[0], rel_r.at[mc], sib)
    relayed = copy(sebuf.at[mc], sebuf.at[oc], rel_s.at[0], rel_r.at[oc], sib)

    webuf[my] = wesend[...]
    wpbuf[my] = wp_ref[...]
    tapbuf[my] = tapsend[...]
    sebuf[mc, my] = sesend[...]
    mine = pl.ds(pl.multiple_of(mc * W, W), W)
    other = pl.ds(pl.multiple_of(oc * W, W), W)
    xf[2:2 + H, mine] = x_ref[...].astype(F32)
    cf[1:1 + H, mine] = c_ref[...].astype(F32)
    xnat[:, mine] = x_ref[...]
    cnat[:, mine] = c_ref[...]
    sib_copies[0].wait()
    xf[2:2 + H, other] = xsib[...].astype(F32)
    xnat[:, other] = xsib[...]
    for _, landed in row_copies + col_copies:
        landed.wait()

    top_ok = row > 0
    low_ok = row < rows_n - 1
    left_ok = my > 0
    right_ok = my < yn - 1
    for d, ok in ((0, top_ok), (1, low_ok)):
        for core in (0, 1):
            part = rowbuf[d, core].astype(F32) * jnp.where(ok, 1.0, 0.0)
            xf[(2 + H) * d:(2 + H) * d + 2, W * core:W * core + W] = part[0:2 * W].reshape(2, W, C)
            cf[(1 + H) * d, W * core:W * core + W] = part[2 * W:3 * W]
    cols = colbuf[...].reshape(2 * 3 * 48, C)

    def rim(height, above, left_slot, right_slot):
        shape = (height * 8, 288)
        out_row = lax.broadcasted_iota(jnp.int32, shape, 0)
        src = lax.broadcasted_iota(jnp.int32, shape, 1)
        place = out_row & 7
        at_row = (out_row >> 3) - above
        third = jnp.where(at_row < 0, 0, jnp.where(at_row < H, 1, 2))
        ok = jnp.where(at_row < 0, top_ok.astype(jnp.int32), jnp.where(at_row < H, 1, low_ok.astype(jnp.int32)))
        want = third * 48 + (at_row & (H - 1))
        right_of = jnp.where(place < 4, 1, 0)
        slot = jnp.where(place < 4, right_slot(place), left_slot(place))
        ok = ok * jnp.where(slot < 0, 0, 1) * jnp.where(place < 4, right_ok.astype(jnp.int32), left_ok.astype(jnp.int32))
        want = want + right_of * 144 + slot * 16
        hit = jnp.where(src == want, ok, 0).astype(F32).astype(BF16)
        return jnp.dot(hit, cols, preferred_element_type=F32).reshape(height, 8, C)

    xf[:, 64:72] = rim(H + 4, 2, lambda k: jnp.where(k >= 6, k - 6, -1), lambda k: jnp.where(k < 2, k, -1))

    @pl.loop(0, (H + 4) // 2)
    def _(i):
        at = pl.ds(pl.multiple_of(i * 2 * PW, 2 * PW), 2 * PW)
        xs[at] = xf[pl.ds(i * 2, 2)].reshape(2 * PW, C).astype(BF16)

    gathered(yn, my, at_y, lambda p: tapsend, tapbuf, tap_s, tap_r)
    wide = jnp.concatenate([tapbuf[q].astype(F32)[:, 0:S] for q in range(yn)], axis=1)
    for t in range(nt):
        ktile[t] = wide[:, 128 * t:128 * t + 128]
    from_y([near], 0, lambda p: wesend, webuf, we_s, we_r)

    for b in range(pairs):
        pair = lax.rem(pair_mine + b, pairs)
        if b == 1:
            from_y(far, 1, lambda p: wesend, webuf, we_s, we_r)
        w_exp = webuf[pl.ds(pair * 2, 2)].reshape(2 * S, C)

        @pl.loop(0, (H + 4) // 2)
        def _(i):
            at = pl.ds(pl.multiple_of(i * 2 * PW, 2 * PW), 2 * PW)
            pre = lax.dot_general(xs[at], w_exp, NT_DIMS, preferred_element_type=F32)
            sig = sigm(pre)
            act = pre * sig
            slope = sig * (1.0 + (pre - act))
            for t in range(3):
                a1[pair * 3 + t, pl.ds(i * 2, 2)] = act[:, 128 * t:128 * t + 128].reshape(2, PW, 128)
                s1[pair * 3 + t, pl.ds(i * 2, 2)] = slope[:, 128 * t:128 * t + 128].reshape(2, PW, 128)

        @pl.loop(0, 3)
        def _(t3):
            t = pair * 3 + t3
            lanes = pl.ds(pl.multiple_of(t * 128, 128), 128)
            taps = [ktile[t, k:k + 1] for k in range(9)]

            def one_row(i):
                rows = [a1[t, i + r] for r in range(3)]
                parts = [taps[c] * rows[0] + taps[3 + c] * rows[1] + taps[6 + c] * rows[2] for c in range(3)]
                pre = parts[1] + pltpu.roll(parts[0], 1, 0) + pltpu.roll(parts[2], PW - 1, 0)
                sig = sigm(pre)
                act = pre * sig
                s2[t, i] = sig * (1.0 + (pre - act))
                return act[0:64]

            def center(i, pool):
                act = one_row(i)
                act2[i - 1, :, lanes] = act.astype(BF16)
                return pool + jnp.sum(act.reshape(8, 8, 128), axis=0)

            one_row(0)
            one_row(H + 1)
            pool = lax.fori_loop(1, H + 1, center, jnp.zeros((8, 128), F32))
            vbuf[pl.ds(t, 1)] = jnp.sum(pool, axis=0, keepdims=True)

    sib_copies[1].wait()
    cf[1:1 + H, other] = csib[...].astype(F32)
    cnat[:, other] = csib[...]
    cot_flat = cnat[...].reshape(H * 64, C)
    from_y([near] + far, 0, lambda p: wp_ref, wpbuf, wp_s, wp_r)
    ones = jnp.ones((8, C), F32).astype(BF16)
    for t in range(ce // 384):
        rows = lax.dot_general(
            act2[:, :, 384 * t:384 * t + 384].reshape(H * 64, 384), cot_flat, TN_DIMS, preferred_element_type=F32)
        gacc[384 * t:384 * t + 384] = rows
        prod = rows * wpbuf[2 * t:2 * t + 2].reshape(384, C).astype(F32)
        hi = prod.astype(BF16)
        rest = prod - hi.astype(F32)
        mid = rest.astype(BF16)
        low = (rest - mid.astype(F32)).astype(BF16)
        gate_sum = sum(lax.dot_general(ones, part, NT_DIMS, preferred_element_type=F32) for part in (hi, mid, low))
        for k in range(3):
            vbuf[8 + 3 * t + k:9 + 3 * t + k] = gate_sum[0:1, 128 * k:128 * k + 128]

    for t in range(nt, 8):
        vbuf[t:t + 1] = jnp.zeros((1, 128), F32)
        vbuf[8 + t:9 + t] = jnp.zeros((1, 128), F32)

    spread(zn, mz, at_z, lambda p: vbuf, zv, vz_s, vz_r)
    zv[mz] = vbuf[...]

    def send_rows(g, value):
        ysend[g] = value.reshape(yn, S, C).astype(BF16)
        to_y([near] + far, 0, lambda p: ysend.at[g, p], yrecv.at[g], gy_s.at[g], gy_r.at[g])
        yrecv[g, my] = ysend[g, my]

    def send_z(g):
        from_y([near] + far, 0, lambda p: ysend.at[g, p], yrecv.at[g], gy_s.at[g], gy_r.at[g])
        total = yrecv[g, 0].astype(F32)
        for q in range(1, yn):
            total = total + yrecv[g, q].astype(F32)
        for q in range(zn):
            zsend[g, q] = total[zr * (q // 2):zr * (q // 2) + zr, 128 * (q % 2):128 * (q % 2) + 128].astype(BF16)
        spread(zn, mz, at_z, lambda p: zsend.at[g, p], zrecv.at[g], gz_s.at[g], gz_r.at[g])
        zrecv[g, mz] = zsend[g, mz]

    def send_x(g):
        gathered(zn, mz, at_z, lambda p: zsend.at[g, p], zrecv.at[g], gz_s.at[g], gz_r.at[g])
        total = zrecv[g, 0].astype(F32)
        for q in range(1, zn):
            total = total + zrecv[g, q].astype(F32)
        fsend[g, 0] = total.astype(BF16)
        spread(xn, mx, at_x, lambda p: fsend.at[g, 0], xrecv.at[g], gx_s.at[g], gx_r.at[g])
        xrecv[g, mx] = fsend[g, 0]

    def send_back(g):
        gathered(xn, mx, at_x, lambda p: fsend.at[g, 0], xrecv.at[g], gx_s.at[g], gx_r.at[g])
        total = xrecv[g, 0].astype(F32)
        for q in range(1, xn):
            total = total + xrecv[g, q].astype(F32)
        fsend[g, 1] = total.astype(BF16)
        spread(zn, mz, at_z, lambda p: fsend.at[g, 1], frecv.at[g], gf_s.at[g], gf_r.at[g])
        frecv[g, mz] = fsend[g, 1]

    def whole(g, into):
        gathered(zn, mz, at_z, lambda p: fsend.at[g, 1], frecv.at[g], gf_s.at[g], gf_r.at[g])
        for q in range(zn):
            into[zr * (q // 2):zr * (q // 2) + zr, 128 * (q % 2):128 * (q % 2) + 128] = frecv[g, q].astype(F32)

    send_rows(0, gacc[...])
    gathered(yn, my, at_y, lambda p: sesend, sebuf.at[mc], se_s, se_r)
    relay.start()

    cf[:, 64:72] = rim(H + 2, 1, lambda k: jnp.where(k == 7, 2, -1), lambda k: jnp.where(k == 0, 2, -1))

    @pl.loop(0, (H + 2) // 2)
    def _(i):
        at = pl.ds(pl.multiple_of(i * 2 * PW, 2 * PW), 2 * PW)
        cs[at] = cf[pl.ds(i * 2, 2)].reshape(2 * PW, C).astype(BF16)

    def hidden_grad(pair):
        w_pro = wpbuf[2 * pair:2 * pair + 2].reshape(2 * S, C)

        @pl.loop(0, (H + 2) // 2)
        def _(i):
            at = pl.ds(pl.multiple_of(i * 2 * PW, 2 * PW), 2 * PW)
            back = lax.dot_general(cs[at], w_pro, NT_DIMS, preferred_element_type=F32)
            for t in range(3):
                gh[pair * 3 + t, pl.ds(i * 2, 2)] = back[:, 128 * t:128 * t + 128].reshape(2, PW, 128)

    gathered(zn, mz, at_z, lambda p: vbuf, zv, vz_s, vz_r)
    xv[mx] = jnp.sum(zv[...], axis=0)
    spread(xn, mx, at_x, lambda p: xv.at[mx], xv, vx_s, vx_r)
    hidden_grad(0)
    gathered(xn, mx, at_x, lambda p: xv.at[mx], xv, vx_s, vx_r)
    cv[ch] = jnp.sum(xv[...], axis=0)
    spread(ch_n, ch, at_ch, lambda p: cv.at[ch], cv, vc_s, vc_r)
    for pair in range(1, pairs):
        hidden_grad(pair)
    gathered(ch_n, ch, at_ch, lambda p: cv.at[ch], cv, vc_s, vc_r)
    relayed.wait()

    area = float(rows_n * H * yn * 2 * W)
    pooled, gate_grad, weights = [], [], []
    for core in (0, 1):
        total = cv[core]
        for q in range(1, yn):
            total = total + cv[2 * q + core]
        pooled.append(jnp.concatenate([total[t:t + 1] for t in range(nt)], axis=1) * (1.0 / area))
        gate_grad.append(jnp.concatenate([total[8 + t:9 + t] for t in range(nt)], axis=1))
        weights.append(sebuf[core].reshape(ce, 128))
    half = lax.broadcasted_iota(jnp.int32, (1, 128), 1) < 64

    def down(vectors):
        total = jnp.zeros((1, 128), F32)
        for core in (0, 1):
            total = total + jnp.sum(jnp.dot(split3(vectors[core]), weights[core], preferred_element_type=F32), axis=0, keepdims=True)
        return total

    def up(vector, core):
        return jnp.sum(lax.dot_general(split3(vector), weights[core], NT_DIMS, preferred_element_type=F32), axis=0, keepdims=True)

    squeeze_pre = jnp.where(half, down(pooled), 0.0)
    squeeze_sig = sigm(squeeze_pre)
    squeeze_act = squeeze_pre * squeeze_sig
    shifted = pltpu.roll(jnp.broadcast_to(squeeze_act, (8, 128)), 64, 1)[0:1]
    gates = [sigm(up(shifted, core)) for core in (0, 1)]
    excite = [gate_grad[core] * gates[core] * (1.0 - gates[core]) for core in (0, 1)]
    back = pltpu.roll(jnp.broadcast_to(down(excite), (8, 128)), 64, 1)[0:1]
    squeeze_slope = squeeze_sig * (1.0 + squeeze_pre * (1.0 - squeeze_sig))
    grad_squeeze = jnp.where(half, back * squeeze_slope, 0.0)

    def own(values):
        return jnp.where(mc == 0, values[0], values[1])

    gate = own(gates)
    grad_pool = own([up(grad_squeeze, core) for core in (0, 1)]) * (1.0 / area)
    for t in range(nt):
        gs[0, t:t + 1] = gate[:, 128 * t:128 * t + 128]
        gs[1, t:t + 1] = grad_pool[:, 128 * t:128 * t + 128]
    send_z(0)

    def shard_of(rows):
        part = rows[:, 0:S]
        for q in range(1, yn):
            part = jnp.where(my == q, rows[:, S * q:S * q + S], part)
        return part

    def project(source, k, w_all, into):
        def part(where):
            rows = source[:, where].reshape(H * W, ce)
            return jnp.dot(rows, w_all, preferred_element_type=F32).reshape(H, W, C)

        posend[k] = part(other).astype(BF16)
        copy(posend.at[k], porecv.at[k], po_s.at[k], po_r.at[k], sib).start()
        into[...] = part(mine)

    def projected(k, base, total, into):
        copy(posend.at[k], porecv.at[k], po_s.at[k], po_r.at[k], sib).wait()
        into[0] = (base[...].astype(F32) + (total[...] + porecv[k].astype(F32))).astype(BF16)

    place = lax.broadcasted_iota(jnp.int32, (PW, 128), 0)
    off_left = jnp.where(left_ok, PW, PW - 1)
    off_right = jnp.where(right_ok, 0, 1)
    inside = jnp.where((place < 64) | ((place == 64) & (off_right == 0)) | ((place == PW - 1) & (off_left == PW)), 1.0, 0.0)

    x_flat = xnat[...].reshape(H * 64, C)
    for b in range(pairs):
        pair = lax.rem(pair_mine + 1 + b, pairs)

        @pl.loop(0, 3)
        def _(t3):
            t = pair * 3 + t3
            lanes = pl.ds(pl.multiple_of(t * 128, 128), 128)
            taps = [ktile[t, k:k + 1] for k in range(9)]
            gate_t = gs[0, pl.ds(t, 1)]
            pool_t = gs[1, pl.ds(t, 1)]

            @pl.loop(0, H + 2)
            def _(i):
                keep = jnp.where(((i > 0) | top_ok) & ((i < H + 1) | low_ok), 1.0, 0.0)
                gh[t, i] = (gh[t, i] * gate_t + pool_t) * s2[t, i] * (inside * keep)

            @pl.loop(0, H)
            def _(i):
                rows = [gh[t, i + r] for r in range(3)]
                parts = [taps[c] * rows[2] + taps[3 + c] * rows[1] + taps[6 + c] * rows[0] for c in range(3)]
                grad = parts[1] + pltpu.roll(parts[0], PW - 1, 0) + pltpu.roll(parts[2], 1, 0)
                ge[i, :, lanes] = (grad[0:64] * s1[t, i + 2, 0:64]).astype(BF16)

        lanes3 = pl.ds(pl.multiple_of(pair * 384, 384), 384)
        rows = lax.dot_general(ge[:, :, lanes3].reshape(H * 64, 384), x_flat, TN_DIMS, preferred_element_type=F32)
        ysend[1, pl.ds(pair * 2, 2)] = rows.reshape(2, S, C).astype(BF16)
        if b < pairs - 1:
            to_y(far, 1, lambda p: ysend.at[1, p], yrecv.at[1], gy_s.at[1], gy_r.at[1])
            send_x(0)
        else:
            to_y([near], 0, lambda p: ysend.at[1, p], yrecv.at[1], gy_s.at[1], gy_r.at[1])
            yrecv[1, my] = ysend[1, my]

    project(ge, 1, webuf[...].reshape(ce, C), cf.at[0:H, 0:W])
    if pairs == 1:
        send_x(0)
    send_back(0)

    @pl.loop(0, nt)
    def _(t):
        def center(i, sums):
            here = jnp.concatenate([gh[t, i + 1, 0:64], jnp.zeros((8, 128), F32)], axis=0)
            moved = [pltpu.roll(here, PW - 1, 0), here, pltpu.roll(here, 1, 0)]
            fresh = []
            for r in range(3):
                act = a1[t, i + 1 + r]
                for c in range(3):
                    fresh.append(sums[3 * r + c] + jnp.sum((moved[c] * act).reshape(9, 8, 128), axis=0))
            return tuple(fresh)

        sums = lax.fori_loop(0, H, center, (jnp.zeros((8, 128), F32),) * 9)
        dkacc[t] = jnp.concatenate(
            [jnp.sum(part, axis=0, keepdims=True) for part in sums] + [jnp.zeros((7, 128), F32)], axis=0)

    dksend[...] = jnp.concatenate([dkacc[t] for t in range(nt)], axis=1).astype(BF16)
    spread(yn, my, at_y, lambda p: dksend, dkyr, ky_s, ky_r)
    dkyr[my] = dksend[...]
    send_z(1)

    @pl.loop(0, H)
    def _(i):
        act2[i] = (act2[i].astype(F32) * gate).astype(BF16)

    project(act2, 0, wpbuf[...].reshape(ce, C), xf.at[0:H, 0:W])

    def summed(parts):
        total = parts[0].astype(F32)
        for q in range(1, parts.shape[0]):
            total = total + parts[q].astype(F32)
        return total

    gathered(yn, my, at_y, lambda p: dksend, dkyr, ky_s, ky_r)
    dkzs[...] = jnp.concatenate([shard_of(summed(dkyr)), jnp.zeros((16, 256 - S), F32)], axis=1).astype(BF16)
    spread(zn, mz, at_z, lambda p: dkzs, dkzr, kz_s, kz_r)
    dkzr[mz] = dkzs[...]
    send_x(1)
    projected(1, c_ref, cf.at[0:H, 0:W], din_ref)
    gathered(zn, mz, at_z, lambda p: dkzs, dkzr, kz_s, kz_r)
    dkxs[...] = summed(dkzr).astype(BF16)
    spread(xn, mx, at_x, lambda p: dkxs, dkxr, kx_s, kx_r)
    dkxr[mx] = dkxs[...]
    send_back(1)

    own_gate = shard_of(gate)
    lefts, rights = pairs3(shard_of(own(pooled)), grad_squeeze * scale)
    dse1_ref[...] = lax.dot_general(lefts, rights, TN_DIMS, preferred_element_type=F32)[:, 0:64]
    lefts, rights = pairs3(squeeze_act, shard_of(own(excite)) * scale)
    dse2_ref[...] = lax.dot_general(lefts, rights, TN_DIMS, preferred_element_type=F32)[0:64]
    gate_wide = lax.dot_general(split3(own_gate * scale), ones, TN_DIMS, preferred_element_type=F32)
    projected(0, x_ref, xf.at[0:H, 0:W], out_ref)
    whole(0, gacc.at[0:S])
    dwp_ref[...] = gacc[0:S] * gate_wide
    gathered(xn, mx, at_x, lambda p: dkxs, dkxr, kx_s, kx_r)
    dk_ref[...] = summed(dkxr)[0:9, 0:S] * scale
    whole(1, gacc.at[S:2 * S])
    turned = lax.dot_general(gacc[S:2 * S].astype(BF16), eye, TN_DIMS, preferred_element_type=F32)
    dwe_ref[...] = turned * scale


def per_device(inputs, w_expand, kernel, w_se1, w_se2, w_project, cotangent):
    rows_n, ch_n = lax.axis_size("rows"), lax.axis_size("ch")
    zn = CHIPS_Z if rows_n % CHIPS_Z == 0 else 2
    xn, yn = rows_n // zn, ch_n // 2
    ce = S * yn
    nt = ce // 128
    zr = S // (zn // 2)
    grad_scale = 1.0 / math.sqrt(rows_n * H * ch_n * W)
    vmem, dma = pltpu.VMEM, pltpu.SemaphoreType.DMA
    scratch = [
        vmem((H, W, C), BF16), vmem((H, W, C), BF16),
        vmem((2, 3 * W, C), BF16), vmem((2, 2, 3 * W, C), BF16),
        vmem((3 * H, C), BF16), vmem((2, 3, 3 * H, C), BF16),
        vmem((S, C), BF16), vmem((yn, S, C), BF16), vmem((yn, S, C), BF16),
        vmem((S, 128), BF16), vmem((2, yn, S, 128), BF16),
        vmem((16, 256), BF16), vmem((yn, 16, 256), BF16),
        vmem((H + 4, PW, C), F32), vmem((H + 2, PW, C), F32),
        vmem(((H + 4) * PW, C), BF16), vmem(((H + 2) * PW, C), BF16),
        vmem((H, 64, C), BF16), vmem((H, 64, C), BF16),
        vmem((nt, H + 4, PW, 128), F32), vmem((nt, H + 4, PW, 128), F32),
        vmem((nt, H + 2, PW, 128), F32), vmem((nt, H + 2, PW, 128), F32),
        vmem((H, 64, ce), BF16), vmem((H, 64, ce), BF16),
        vmem((nt, 16, 128), F32), vmem((ce, C), F32), vmem((nt, 16, 128), F32),
        vmem((16, 128), F32), vmem((zn, 16, 128), F32), vmem((xn, 16, 128), F32), vmem((ch_n, 16, 128), F32),
        vmem((2, 8, 128), F32),
        vmem((2, yn, S, C), BF16), vmem((2, yn, S, C), BF16),
        vmem((2, zn, zr, 128), BF16), vmem((2, zn, zr, 128), BF16),
        vmem((2, xn, zr, 128), BF16), vmem((2, 2, zr, 128), BF16), vmem((2, zn, zr, 128), BF16),
        vmem((16, ce), BF16), vmem((yn, 16, ce), BF16),
        vmem((zn, 16, 256), BF16), vmem((16, 256), BF16), vmem((xn, 16, 256), BF16), vmem((16, 256), BF16),
        vmem((2, H, W, C), BF16), vmem((2, H, W, C), BF16),
        dma((2,)), dma((2,)), dma((2, 2)), dma((2, 2)), dma((3, 2)), dma((2, 3)),
        dma((yn,)), dma((yn,)), dma((yn,)), dma((yn,)),
        dma((yn,)), dma((yn,)), dma((1,)), dma((2,)), dma((yn,)), dma((yn,)),
        dma((zn,)), dma((zn,)), dma((xn,)), dma((xn,)), dma((ch_n,)), dma((ch_n,)),
        dma((2, yn)), dma((2, yn)), dma((2, zn)), dma((2, zn)), dma((2, xn)), dma((2, xn)), dma((2, zn)), dma((2, zn)),
        dma((yn,)), dma((yn,)), dma((zn,)), dma((zn,)), dma((xn,)), dma((xn,)),
        dma((2,)), dma((2,)),
    ]
    in_vmem = pl.BlockSpec(memory_space=pltpu.VMEM)
    return pl.pallas_call(
        functools.partial(fused, rows_n, ch_n, grad_scale),
        out_shape=(
            jax.ShapeDtypeStruct((1, H, W, C), BF16), jax.ShapeDtypeStruct((1, H, W, C), BF16),
            jax.ShapeDtypeStruct((C, S), F32), jax.ShapeDtypeStruct((9, S), F32),
            jax.ShapeDtypeStruct((S, 64), F32), jax.ShapeDtypeStruct((64, S), F32),
            jax.ShapeDtypeStruct((S, C), F32)),
        in_specs=[in_vmem] * 7,
        out_specs=(in_vmem,) * 7,
        scratch_shapes=scratch,
        compiler_params=pltpu.CompilerParams(
            collective_id=0, has_side_effects=True, vmem_limit_bytes=56 * 1024 * 1024),
    )(inputs, w_expand, kernel, w_se1, w_se2, w_project, cotangent)


def solution(mesh):
    return jax.shard_map(
        per_device,
        mesh=mesh,
        in_specs=(
            P(None, "rows", "ch", None),
            P(None, "ch"),
            P(None, "ch"),
            P("ch", None),
            P(None, "ch"),
            P("ch", None),
            P(None, "rows", "ch", None),
        ),
        out_specs=(
            P(None, "rows", "ch", None),
            P(None, "rows", "ch", None),
            P(None, "ch"),
            P(None, "ch"),
            P("ch", None),
            P(None, "ch"),
            P("ch", None),
        ),
        check_vma=False,
    )
```

```python
import functools
import math

import jax
import jax.numpy as jnp
from jax import lax
from jax.experimental import pallas as pl
from jax.experimental.pallas import tpu as pltpu
from jax.sharding import PartitionSpec as P

MESH = pl.DeviceIdType.MESH
F32 = jnp.float32
BF16 = jnp.bfloat16

CHIPS_Z = 8
H = 16
W = 32
C = 256
S = 192
PW = 72
EXPAND_ROWS = 10
GRAD_ROWS = 18
UNROLL = 4
NT_DIMS = (((1,), (1,)), ((), ()))
TN_DIMS = (((0,), (0,)), ((), ()))


def split3(row):
    hi = row.astype(BF16).astype(F32)
    mid = (row - hi).astype(BF16).astype(F32)
    low = row - hi - mid
    rest = jnp.zeros((5, row.shape[1]), F32)
    return jnp.concatenate([hi, mid, low, rest], axis=0).astype(BF16)


def sigm(v):
    return 0.5 * jnp.tanh(0.5 * v) + 0.5


def pairs3(left, right):
    def three(row):
        hi = row.astype(BF16).astype(F32)
        mid = (row - hi).astype(BF16).astype(F32)
        return hi, mid, row - hi - mid

    a, b = three(left), three(right)
    lefts = jnp.concatenate([a[k] for k in (0, 0, 1, 1, 0, 2, 1, 2)], axis=0).astype(BF16)
    rights = jnp.concatenate([b[k] for k in (0, 1, 0, 1, 2, 0, 2, 1)], axis=0).astype(BF16)
    return lefts, rights


def fused(rows_n, ch_n, scale, x_in, we_ref, tap_ref, se1_ref, se2_ref, wp_ref, c_in,
          out_ref, din_ref, dwe_ref, dk_ref, dse1_ref, dse2_ref, dwp_ref,
          xsib, csib, rowsend, rowbuf, colsend, colbuf, webuf, wpbuf, sesend, sebuf, tapsend, tapbuf,
          xf, cf, xs, cs, xnat, cnat, a1, s1, gh, s2, act2, ge, ktile, gacc, dkacc,
          vbuf, zv, xv, cv, gs, ysend, yrecv, zsend, zrecv, xrecv, fsend, frecv,
          dksend, dkyr, dkzr, dkxs, dkxr, dkzs, posend, porecv,
          sib_s, sib_r, row_s, row_r, col_s, col_r, we_s, we_r, wp_s, wp_r, se_s, se_r, rel_s, rel_r, tap_s, tap_r,
          vz_s, vz_r, vx_s, vx_r, vc_s, vc_r, gy_s, gy_r, gz_s, gz_r, gx_s, gx_r, gf_s, gf_r,
          ky_s, ky_r, kz_s, kz_r, kx_s, kx_r, po_s, po_r):
    x_ref, c_ref = x_in.at[0], c_in.at[0]
    zn = CHIPS_Z if rows_n % CHIPS_Z == 0 else 2
    xn = rows_n // zn
    yn = ch_n // 2
    ce = S * yn
    nt = ce // 128
    pairs = yn // 2
    zr = S // (zn // 2)
    row = lax.axis_index("rows")
    ch = lax.axis_index("ch")
    mx, mz = row // zn, lax.rem(row, zn)
    my, mc = ch // 2, lax.rem(ch, 2)
    oc = 1 - mc

    def dev_row(step):
        return lax.rem(row + step + rows_n, rows_n)

    def dev_y(step):
        return lax.rem(my + step + yn, yn)

    def copy(src, dst, ssem, rsem, where):
        return pltpu.make_async_remote_copy(
            src_ref=src, dst_ref=dst, send_sem=ssem, recv_sem=rsem, device_id=where, device_id_type=MESH)

    def at_y(peer):
        return (row, peer * 2 + mc)

    def at_z(peer):
        return (mx * zn + peer, ch)

    def at_x(peer):
        return (peer * zn + mz, ch)

    def at_ch(peer):
        return (row, peer)

    def spread(n, me, at, src, land, ssem, rsem):
        for step in range(1, n):
            peer = lax.rem(me + step, n)
            copy(src(peer), land.at[me], ssem.at[step - 1], rsem.at[me], at(peer)).start()

    def gathered(n, me, at, src, land, ssem, rsem):
        for step in range(1, n):
            peer = lax.rem(me + step, n)
            copy(src(peer), land.at[peer], ssem.at[step - 1], rsem.at[peer], at(peer)).wait()

    pair_mine = my // 2
    near = my + 1 - 2 * lax.rem(my, 2)
    far = [lax.rem(pair_mine + b, pairs) * 2 + k for b in range(1, pairs) for k in (0, 1)]

    def to_y(peers, first, src, land, ssem, rsem):
        for k, peer in enumerate(peers):
            copy(src(peer), land.at[my], ssem.at[first + k], rsem.at[my], at_y(peer)).start()

    def from_y(peers, first, src, land, ssem, rsem):
        for k, peer in enumerate(peers):
            copy(src(peer), land.at[peer], ssem.at[first + k], rsem.at[peer], at_y(peer)).wait()

    barrier = pltpu.get_barrier_semaphore()
    partners = [at_ch(lax.rem(ch + s, ch_n)) for s in range(1, ch_n)]
    partners += [at_z(lax.rem(mz + s, zn)) for s in range(1, zn)]
    partners += [at_x(lax.rem(mx + s, xn)) for s in range(1, xn)]
    partners += [(dev_row(dr), my * 2 + core) for dr in (-1, 1) for core in (0, 1)]
    partners += [(dev_row(dr), dev_y(dy) * 2 + core) for dr in (-1, 0, 1) for dy in (-1, 1) for core in (0, 1)]
    for where in partners:
        pl.semaphore_signal(barrier, inc=1, device_id=where, device_id_type=MESH)

    for d, (lo, edge) in enumerate(((0, 0), (H - 2, H - 1))):
        rowsend[d, 0:2 * W] = x_ref[lo:lo + 2].reshape(2 * W, C)
        rowsend[d, 2 * W:3 * W] = c_ref[edge]
    first = mc * (W - 2)
    ri = lax.broadcasted_iota(jnp.int32, (2 * H, H * W), 0)
    ci = lax.broadcasted_iota(jnp.int32, (2 * H, H * W), 1)
    pick = (ci == (ri & (H - 1)) * W + first + (ri >> 4)).astype(F32).astype(BF16)
    colsend[0:2 * H] = jnp.dot(pick, x_ref[...].reshape(H * W, C), preferred_element_type=F32).astype(BF16)
    ri = lax.broadcasted_iota(jnp.int32, (H, H * W), 0)
    ci = lax.broadcasted_iota(jnp.int32, (H, H * W), 1)
    pick = (ci == ri * W + mc * (W - 1)).astype(F32).astype(BF16)
    colsend[2 * H:3 * H] = jnp.dot(pick, c_ref[...].reshape(H * W, C), preferred_element_type=F32).astype(BF16)

    eye = (lax.broadcasted_iota(jnp.int32, (S, S), 0) == lax.broadcasted_iota(jnp.int32, (S, S), 1)).astype(F32).astype(BF16)
    se_t = jnp.concatenate([se1_ref[...], se2_ref[...]], axis=0)
    sesend[...] = lax.dot_general(eye, se_t, NT_DIMS, preferred_element_type=F32).astype(BF16)
    tap_rows = jnp.concatenate([tap_ref[...].astype(F32), jnp.zeros((7, S), F32)], axis=0)
    tapsend[...] = jnp.concatenate([tap_rows, jnp.zeros((16, 256 - S), F32)], axis=1).astype(BF16)

    pl.semaphore_wait(barrier, len(partners))

    sib = (row, my * 2 + oc)
    sib_copies = [copy(x_ref, xsib, sib_s.at[0], sib_r.at[0], sib), copy(c_ref, csib, sib_s.at[1], sib_r.at[1], sib)]
    row_copies = []
    for d, dr in ((0, -1), (1, 1)):
        for core in (0, 1):
            row_copies.append((copy(rowsend.at[d], rowbuf.at[1 - d, mc], row_s.at[d, core], row_r.at[1 - d, mc],
                                    (dev_row(dr), my * 2 + core)),
                               copy(rowsend.at[d], rowbuf.at[1 - d, core], row_s.at[d, core], row_r.at[1 - d, core],
                                    (dev_row(dr), my * 2 + core))))
    col_copies = []
    side = 1 - mc
    for i, dr in enumerate((-1, 0, 1)):
        for core in (0, 1):
            where = (dev_row(dr), dev_y(2 * mc - 1) * 2 + core)
            col_copies.append((copy(colsend, colbuf.at[side, 2 - i], col_s.at[i, core], col_r.at[side, 2 - i], where),
                               copy(colsend, colbuf.at[core, i], col_s.at[i, core], col_r.at[core, i], where)))
    sib_copies[0].start()
    for sent, _ in row_copies + col_copies:
        sent.start()
    to_y([near], 0, lambda p: we_ref, webuf, we_s, we_r)
    spread(yn, my, at_y, lambda p: tapsend, tapbuf, tap_s, tap_r)
    sib_copies[1].start()
    to_y(far, 1, lambda p: we_ref, webuf, we_s, we_r)
    to_y([near] + far, 0, lambda p: wp_ref, wpbuf, wp_s, wp_r)
    spread(yn, my, at_y, lambda p: sesend, sebuf.at[mc], se_s, se_r)
    relay = copy(sebuf.at[mc], sebuf.at[mc], rel_s.at[0], rel_r.at[mc], sib)
    relayed = copy(sebuf.at[mc], sebuf.at[oc], rel_s.at[0], rel_r.at[oc], sib)

    webuf[my] = we_ref[...]
    wpbuf[my] = wp_ref[...]
    tapbuf[my] = tapsend[...]
    sebuf[mc, my] = sesend[...]
    mine = pl.ds(pl.multiple_of(mc * W, W), W)
    other = pl.ds(pl.multiple_of(oc * W, W), W)
    xf[2:2 + H, mine] = x_ref[...].astype(F32)
    cf[1:1 + H, mine] = c_ref[...].astype(F32)
    xnat[:, mine] = x_ref[...]
    cnat[:, mine] = c_ref[...]
    sib_copies[0].wait()
    xf[2:2 + H, other] = xsib[...].astype(F32)
    xnat[:, other] = xsib[...]
    for _, landed in row_copies + col_copies:
        landed.wait()

    top_ok = row > 0
    low_ok = row < rows_n - 1
    left_ok = my > 0
    right_ok = my < yn - 1
    for d, ok in ((0, top_ok), (1, low_ok)):
        for core in (0, 1):
            part = rowbuf[d, core].astype(F32) * jnp.where(ok, 1.0, 0.0)
            xf[(2 + H) * d:(2 + H) * d + 2, W * core:W * core + W] = part[0:2 * W].reshape(2, W, C)
            cf[(1 + H) * d, W * core:W * core + W] = part[2 * W:3 * W]
    cols = colbuf[...].reshape(2 * 3 * 48, C)

    def rim(height, above, left_slot, right_slot):
        shape = (height * 8, 288)
        out_row = lax.broadcasted_iota(jnp.int32, shape, 0)
        src = lax.broadcasted_iota(jnp.int32, shape, 1)
        place = out_row & 7
        at_row = (out_row >> 3) - above
        third = jnp.where(at_row < 0, 0, jnp.where(at_row < H, 1, 2))
        ok = jnp.where(at_row < 0, top_ok.astype(jnp.int32), jnp.where(at_row < H, 1, low_ok.astype(jnp.int32)))
        want = third * 48 + (at_row & (H - 1))
        right_of = jnp.where(place < 4, 1, 0)
        slot = jnp.where(place < 4, right_slot(place), left_slot(place))
        ok = ok * jnp.where(slot < 0, 0, 1) * jnp.where(place < 4, right_ok.astype(jnp.int32), left_ok.astype(jnp.int32))
        want = want + right_of * 144 + slot * 16
        hit = jnp.where(src == want, ok, 0).astype(F32).astype(BF16)
        return jnp.dot(hit, cols, preferred_element_type=F32).reshape(height, 8, C)

    xf[:, 64:72] = rim(H + 4, 2, lambda k: jnp.where(k >= 6, k - 6, -1), lambda k: jnp.where(k < 2, k, -1))

    @pl.loop(0, (H + 4) // 2)
    def _(i):
        at = pl.ds(pl.multiple_of(i * 2 * PW, 2 * PW), 2 * PW)
        xs[at] = xf[pl.ds(i * 2, 2)].reshape(2 * PW, C).astype(BF16)

    gathered(yn, my, at_y, lambda p: tapsend, tapbuf, tap_s, tap_r)
    wide = jnp.concatenate([tapbuf[q].astype(F32)[:, 0:S] for q in range(yn)], axis=1)
    for t in range(nt):
        ktile[t] = wide[:, 128 * t:128 * t + 128]
    from_y([near], 0, lambda p: we_ref, webuf, we_s, we_r)

    for b in range(pairs):
        pair = lax.rem(pair_mine + b, pairs)
        if b == 1:
            from_y(far, 1, lambda p: we_ref, webuf, we_s, we_r)
        w_exp = webuf[pl.ds(pair * 2, 2)].reshape(2 * S, C)

        @pl.loop(0, (H + 4) // EXPAND_ROWS)
        def _(i):
            step = EXPAND_ROWS * PW
            at = pl.ds(pl.multiple_of(i * step, step), step)
            pre = lax.dot_general(xs[at], w_exp, NT_DIMS, preferred_element_type=F32)
            sig = sigm(pre)
            act = pre * sig
            slope = sig * (1.0 + (pre - act))
            for t in range(3):
                there = pl.ds(i * EXPAND_ROWS, EXPAND_ROWS)
                a1[pair * 3 + t, there] = act[:, 128 * t:128 * t + 128].reshape(EXPAND_ROWS, PW, 128)
                s1[pair * 3 + t, there] = slope[:, 128 * t:128 * t + 128].reshape(EXPAND_ROWS, PW, 128)

        @pl.loop(0, 3)
        def _(t3):
            t = pair * 3 + t3
            lanes = pl.ds(pl.multiple_of(t * 128, 128), 128)
            taps = [ktile[t, k:k + 1] for k in range(9)]

            def one_row(i):
                rows = [a1[t, i + r] for r in range(3)]
                parts = [taps[c] * rows[0] + taps[3 + c] * rows[1] + taps[6 + c] * rows[2] for c in range(3)]
                pre = parts[1] + pltpu.roll(parts[0], 1, 0) + pltpu.roll(parts[2], PW - 1, 0)
                sig = sigm(pre)
                act = pre * sig
                s2[t, i] = sig * (1.0 + (pre - act))
                return act[0:64]

            def center(i, pool):
                act = one_row(i)
                act2[i - 1, :, lanes] = act.astype(BF16)
                return pool + jnp.sum(act.reshape(8, 8, 128), axis=0)

            one_row(0)
            one_row(H + 1)
            pool = lax.fori_loop(1, H + 1, center, jnp.zeros((8, 128), F32), unroll=UNROLL)
            vbuf[pl.ds(t, 1)] = jnp.sum(pool, axis=0, keepdims=True)

    sib_copies[1].wait()
    cf[1:1 + H, other] = csib[...].astype(F32)
    cnat[:, other] = csib[...]
    cot_flat = cnat[...].reshape(H * 64, C)
    from_y([near] + far, 0, lambda p: wp_ref, wpbuf, wp_s, wp_r)
    ones = jnp.ones((8, C), F32).astype(BF16)
    for t in range(ce // 384):
        rows = lax.dot_general(
            act2[:, :, 384 * t:384 * t + 384].reshape(H * 64, 384), cot_flat, TN_DIMS, preferred_element_type=F32)
        gacc[384 * t:384 * t + 384] = rows
        prod = rows * wpbuf[2 * t:2 * t + 2].reshape(384, C).astype(F32)
        hi = prod.astype(BF16)
        rest = prod - hi.astype(F32)
        mid = rest.astype(BF16)
        low = (rest - mid.astype(F32)).astype(BF16)
        gate_sum = sum(lax.dot_general(ones, part, NT_DIMS, preferred_element_type=F32) for part in (hi, mid, low))
        for k in range(3):
            vbuf[8 + 3 * t + k:9 + 3 * t + k] = gate_sum[0:1, 128 * k:128 * k + 128]

    for t in range(nt, 8):
        vbuf[t:t + 1] = jnp.zeros((1, 128), F32)
        vbuf[8 + t:9 + t] = jnp.zeros((1, 128), F32)

    spread(zn, mz, at_z, lambda p: vbuf, zv, vz_s, vz_r)
    zv[mz] = vbuf[...]

    def send_rows(g, value):
        ysend[g] = value.reshape(yn, S, C).astype(BF16)
        to_y([near] + far, 0, lambda p: ysend.at[g, p], yrecv.at[g], gy_s.at[g], gy_r.at[g])
        yrecv[g, my] = ysend[g, my]

    def send_z(g):
        from_y([near] + far, 0, lambda p: ysend.at[g, p], yrecv.at[g], gy_s.at[g], gy_r.at[g])
        total = yrecv[g, 0].astype(F32)
        for q in range(1, yn):
            total = total + yrecv[g, q].astype(F32)
        for q in range(zn):
            zsend[g, q] = total[zr * (q // 2):zr * (q // 2) + zr, 128 * (q % 2):128 * (q % 2) + 128].astype(BF16)
        spread(zn, mz, at_z, lambda p: zsend.at[g, p], zrecv.at[g], gz_s.at[g], gz_r.at[g])
        zrecv[g, mz] = zsend[g, mz]

    def send_x(g):
        gathered(zn, mz, at_z, lambda p: zsend.at[g, p], zrecv.at[g], gz_s.at[g], gz_r.at[g])
        total = zrecv[g, 0].astype(F32)
        for q in range(1, zn):
            total = total + zrecv[g, q].astype(F32)
        fsend[g, 0] = total.astype(BF16)
        spread(xn, mx, at_x, lambda p: fsend.at[g, 0], xrecv.at[g], gx_s.at[g], gx_r.at[g])
        xrecv[g, mx] = fsend[g, 0]

    def send_back(g):
        gathered(xn, mx, at_x, lambda p: fsend.at[g, 0], xrecv.at[g], gx_s.at[g], gx_r.at[g])
        total = xrecv[g, 0].astype(F32)
        for q in range(1, xn):
            total = total + xrecv[g, q].astype(F32)
        fsend[g, 1] = total.astype(BF16)
        spread(zn, mz, at_z, lambda p: fsend.at[g, 1], frecv.at[g], gf_s.at[g], gf_r.at[g])
        frecv[g, mz] = fsend[g, 1]

    def whole(g, into):
        gathered(zn, mz, at_z, lambda p: fsend.at[g, 1], frecv.at[g], gf_s.at[g], gf_r.at[g])
        for q in range(zn):
            into[zr * (q // 2):zr * (q // 2) + zr, 128 * (q % 2):128 * (q % 2) + 128] = frecv[g, q].astype(F32)

    send_rows(0, gacc[...])
    gathered(yn, my, at_y, lambda p: sesend, sebuf.at[mc], se_s, se_r)
    relay.start()

    cf[:, 64:72] = rim(H + 2, 1, lambda k: jnp.where(k == 7, 2, -1), lambda k: jnp.where(k == 0, 2, -1))

    @pl.loop(0, (H + 2) // 2)
    def _(i):
        at = pl.ds(pl.multiple_of(i * 2 * PW, 2 * PW), 2 * PW)
        cs[at] = cf[pl.ds(i * 2, 2)].reshape(2 * PW, C).astype(BF16)

    def hidden_grad(pair):
        w_pro = wpbuf[2 * pair:2 * pair + 2].reshape(2 * S, C)

        @pl.loop(0, (H + 2) // GRAD_ROWS)
        def _(i):
            step = GRAD_ROWS * PW
            at = pl.ds(pl.multiple_of(i * step, step), step)
            back = lax.dot_general(cs[at], w_pro, NT_DIMS, preferred_element_type=F32)
            for t in range(3):
                gh[pair * 3 + t, pl.ds(i * GRAD_ROWS, GRAD_ROWS)] = back[:, 128 * t:128 * t + 128].reshape(GRAD_ROWS, PW, 128)

    gathered(zn, mz, at_z, lambda p: vbuf, zv, vz_s, vz_r)
    xv[mx] = jnp.sum(zv[...], axis=0)
    spread(xn, mx, at_x, lambda p: xv.at[mx], xv, vx_s, vx_r)
    hidden_grad(0)
    gathered(xn, mx, at_x, lambda p: xv.at[mx], xv, vx_s, vx_r)
    cv[ch] = jnp.sum(xv[...], axis=0)
    spread(ch_n, ch, at_ch, lambda p: cv.at[ch], cv, vc_s, vc_r)
    for pair in range(1, pairs):
        hidden_grad(pair)
    gathered(ch_n, ch, at_ch, lambda p: cv.at[ch], cv, vc_s, vc_r)
    relayed.wait()

    area = float(rows_n * H * yn * 2 * W)
    pooled, gate_grad, weights = [], [], []
    for core in (0, 1):
        total = cv[core]
        for q in range(1, yn):
            total = total + cv[2 * q + core]
        pooled.append(jnp.concatenate([total[t:t + 1] for t in range(nt)], axis=1) * (1.0 / area))
        gate_grad.append(jnp.concatenate([total[8 + t:9 + t] for t in range(nt)], axis=1))
        weights.append(sebuf[core].reshape(ce, 128))
    half = lax.broadcasted_iota(jnp.int32, (1, 128), 1) < 64

    def down(vectors):
        total = jnp.zeros((1, 128), F32)
        for core in (0, 1):
            total = total + jnp.sum(jnp.dot(split3(vectors[core]), weights[core], preferred_element_type=F32), axis=0, keepdims=True)
        return total

    def up(vector, core):
        return jnp.sum(lax.dot_general(split3(vector), weights[core], NT_DIMS, preferred_element_type=F32), axis=0, keepdims=True)

    squeeze_pre = jnp.where(half, down(pooled), 0.0)
    squeeze_sig = sigm(squeeze_pre)
    squeeze_act = squeeze_pre * squeeze_sig
    shifted = pltpu.roll(jnp.broadcast_to(squeeze_act, (8, 128)), 64, 1)[0:1]
    gates = [sigm(up(shifted, core)) for core in (0, 1)]
    excite = [gate_grad[core] * gates[core] * (1.0 - gates[core]) for core in (0, 1)]
    back = pltpu.roll(jnp.broadcast_to(down(excite), (8, 128)), 64, 1)[0:1]
    squeeze_slope = squeeze_sig * (1.0 + squeeze_pre * (1.0 - squeeze_sig))
    grad_squeeze = jnp.where(half, back * squeeze_slope, 0.0)

    def own(values):
        return jnp.where(mc == 0, values[0], values[1])

    gate = own(gates)
    grad_pool = own([up(grad_squeeze, core) for core in (0, 1)]) * (1.0 / area)
    for t in range(nt):
        gs[0, t:t + 1] = gate[:, 128 * t:128 * t + 128]
        gs[1, t:t + 1] = grad_pool[:, 128 * t:128 * t + 128]
    send_z(0)

    def shard_of(rows):
        part = rows[:, 0:S]
        for q in range(1, yn):
            part = jnp.where(my == q, rows[:, S * q:S * q + S], part)
        return part

    def project(source, k, w_all, into):
        def part(where):
            rows = source[:, where].reshape(H * W, ce)
            return jnp.dot(rows, w_all, preferred_element_type=F32).reshape(H, W, C)

        posend[k] = part(other).astype(BF16)
        copy(posend.at[k], porecv.at[k], po_s.at[k], po_r.at[k], sib).start()
        into[...] = part(mine)

    def projected(k, base, total, into):
        copy(posend.at[k], porecv.at[k], po_s.at[k], po_r.at[k], sib).wait()
        into[0] = (base[...].astype(F32) + (total[...] + porecv[k].astype(F32))).astype(BF16)

    place = lax.broadcasted_iota(jnp.int32, (PW, 128), 0)
    off_left = jnp.where(left_ok, PW, PW - 1)
    off_right = jnp.where(right_ok, 0, 1)
    inside = jnp.where((place < 64) | ((place == 64) & (off_right == 0)) | ((place == PW - 1) & (off_left == PW)), 1.0, 0.0)

    x_flat = xnat[...].reshape(H * 64, C)
    for b in range(pairs):
        pair = lax.rem(pair_mine + 1 + b, pairs)

        @pl.loop(0, 3)
        def _(t3):
            t = pair * 3 + t3
            lanes = pl.ds(pl.multiple_of(t * 128, 128), 128)
            taps = [ktile[t, k:k + 1] for k in range(9)]
            gate_t = gs[0, pl.ds(t, 1)]
            pool_t = gs[1, pl.ds(t, 1)]

            @pl.loop(0, H + 2, unroll=2)
            def _(i):
                keep = jnp.where(((i > 0) | top_ok) & ((i < H + 1) | low_ok), 1.0, 0.0)
                gh[t, i] = (gh[t, i] * gate_t + pool_t) * s2[t, i] * (inside * keep)

            @pl.loop(0, H, unroll=UNROLL)
            def _(i):
                rows = [gh[t, i + r] for r in range(3)]
                parts = [taps[c] * rows[2] + taps[3 + c] * rows[1] + taps[6 + c] * rows[0] for c in range(3)]
                grad = parts[1] + pltpu.roll(parts[0], PW - 1, 0) + pltpu.roll(parts[2], 1, 0)
                ge[i, :, lanes] = (grad[0:64] * s1[t, i + 2, 0:64]).astype(BF16)

        lanes3 = pl.ds(pl.multiple_of(pair * 384, 384), 384)
        rows = lax.dot_general(ge[:, :, lanes3].reshape(H * 64, 384), x_flat, TN_DIMS, preferred_element_type=F32)
        ysend[1, pl.ds(pair * 2, 2)] = rows.reshape(2, S, C).astype(BF16)
        if b < pairs - 1:
            to_y(far, 1, lambda p: ysend.at[1, p], yrecv.at[1], gy_s.at[1], gy_r.at[1])
            send_x(0)
        else:
            to_y([near], 0, lambda p: ysend.at[1, p], yrecv.at[1], gy_s.at[1], gy_r.at[1])
            yrecv[1, my] = ysend[1, my]

    project(ge, 1, webuf[...].reshape(ce, C), cf.at[0:H, 0:W])
    if pairs == 1:
        send_x(0)
    send_back(0)

    @pl.loop(0, nt)
    def _(t):
        def center(i, sums):
            here = jnp.concatenate([gh[t, i + 1, 0:64], jnp.zeros((8, 128), F32)], axis=0)
            moved = [pltpu.roll(here, PW - 1, 0), here, pltpu.roll(here, 1, 0)]
            fresh = []
            for r in range(3):
                act = a1[t, i + 1 + r]
                for c in range(3):
                    fresh.append(sums[3 * r + c] + jnp.sum((moved[c] * act).reshape(9, 8, 128), axis=0))
            return tuple(fresh)

        sums = lax.fori_loop(0, H, center, (jnp.zeros((8, 128), F32),) * 9, unroll=UNROLL)
        dkacc[t] = jnp.concatenate(
            [jnp.sum(part, axis=0, keepdims=True) for part in sums] + [jnp.zeros((7, 128), F32)], axis=0)

    dksend[...] = jnp.concatenate([dkacc[t] for t in range(nt)], axis=1).astype(BF16)
    spread(yn, my, at_y, lambda p: dksend, dkyr, ky_s, ky_r)
    dkyr[my] = dksend[...]
    send_z(1)

    @pl.loop(0, H)
    def _(i):
        act2[i] = (act2[i].astype(F32) * gate).astype(BF16)

    project(act2, 0, wpbuf[...].reshape(ce, C), xf.at[0:H, 0:W])

    def summed(parts):
        total = parts[0].astype(F32)
        for q in range(1, parts.shape[0]):
            total = total + parts[q].astype(F32)
        return total

    gathered(yn, my, at_y, lambda p: dksend, dkyr, ky_s, ky_r)
    dkzs[...] = jnp.concatenate([shard_of(summed(dkyr)), jnp.zeros((16, 256 - S), F32)], axis=1).astype(BF16)
    spread(zn, mz, at_z, lambda p: dkzs, dkzr, kz_s, kz_r)
    dkzr[mz] = dkzs[...]
    send_x(1)
    projected(1, c_ref, cf.at[0:H, 0:W], din_ref)
    gathered(zn, mz, at_z, lambda p: dkzs, dkzr, kz_s, kz_r)
    dkxs[...] = summed(dkzr).astype(BF16)
    spread(xn, mx, at_x, lambda p: dkxs, dkxr, kx_s, kx_r)
    dkxr[mx] = dkxs[...]
    send_back(1)

    own_gate = shard_of(gate)
    lefts, rights = pairs3(grad_squeeze * scale, shard_of(own(pooled)))
    dse1_ref[...] = lax.dot_general(lefts, rights, TN_DIMS, preferred_element_type=F32)[0:64]
    lefts, rights = pairs3(squeeze_act, shard_of(own(excite)) * scale)
    dse2_ref[...] = lax.dot_general(lefts, rights, TN_DIMS, preferred_element_type=F32)[0:64]
    gate_wide = lax.dot_general(split3(own_gate * scale), ones, TN_DIMS, preferred_element_type=F32)
    projected(0, x_ref, xf.at[0:H, 0:W], out_ref)
    whole(0, gacc.at[0:S])
    dwp_ref[...] = gacc[0:S] * gate_wide
    gathered(xn, mx, at_x, lambda p: dkxs, dkxr, kx_s, kx_r)
    dk_ref[...] = summed(dkxr)[0:9, 0:S] * scale
    whole(1, gacc.at[S:2 * S])
    dwe_ref[...] = gacc[S:2 * S] * scale


def settle(*refs):
    count = (len(refs) - 1) // 2
    moves = [pltpu.make_async_copy(refs[k], refs[count + k], refs[-1].at[k]) for k in range(count)]
    for move in moves:
        move.start()
    for move in moves:
        move.wait()


def per_device(inputs, w_expand, kernel, w_se1, w_se2, w_project, cotangent):
    rows_n, ch_n = lax.axis_size("rows"), lax.axis_size("ch")
    zn = CHIPS_Z if rows_n % CHIPS_Z == 0 else 2
    xn, yn = rows_n // zn, ch_n // 2
    ce = S * yn
    nt = ce // 128
    zr = S // (zn // 2)
    grad_scale = 1.0 / math.sqrt(rows_n * H * ch_n * W)
    vmem, dma = pltpu.VMEM, pltpu.SemaphoreType.DMA
    scratch = [
        vmem((H, W, C), BF16), vmem((H, W, C), BF16),
        vmem((2, 3 * W, C), BF16), vmem((2, 2, 3 * W, C), BF16),
        vmem((3 * H, C), BF16), vmem((2, 3, 3 * H, C), BF16),
        vmem((yn, S, C), BF16), vmem((yn, S, C), BF16),
        vmem((S, 128), BF16), vmem((2, yn, S, 128), BF16),
        vmem((16, 256), BF16), vmem((yn, 16, 256), BF16),
        vmem((H + 4, PW, C), F32), vmem((H + 2, PW, C), F32),
        vmem(((H + 4) * PW, C), BF16), vmem(((H + 2) * PW, C), BF16),
        vmem((H, 64, C), BF16), vmem((H, 64, C), BF16),
        vmem((nt, H + 4, PW, 128), F32), vmem((nt, H + 4, PW, 128), F32),
        vmem((nt, H + 2, PW, 128), F32), vmem((nt, H + 2, PW, 128), F32),
        vmem((H, 64, ce), BF16), vmem((H, 64, ce), BF16),
        vmem((nt, 16, 128), F32), vmem((ce, C), F32), vmem((nt, 16, 128), F32),
        vmem((16, 128), F32), vmem((zn, 16, 128), F32), vmem((xn, 16, 128), F32), vmem((ch_n, 16, 128), F32),
        vmem((2, 8, 128), F32),
        vmem((2, yn, S, C), BF16), vmem((2, yn, S, C), BF16),
        vmem((2, zn, zr, 128), BF16), vmem((2, zn, zr, 128), BF16),
        vmem((2, xn, zr, 128), BF16), vmem((2, 2, zr, 128), BF16), vmem((2, zn, zr, 128), BF16),
        vmem((16, ce), BF16), vmem((yn, 16, ce), BF16),
        vmem((zn, 16, 256), BF16), vmem((16, 256), BF16), vmem((xn, 16, 256), BF16), vmem((16, 256), BF16),
        vmem((2, H, W, C), BF16), vmem((2, H, W, C), BF16),
        dma((2,)), dma((2,)), dma((2, 2)), dma((2, 2)), dma((3, 2)), dma((2, 3)),
        dma((yn,)), dma((yn,)), dma((yn,)), dma((yn,)),
        dma((yn,)), dma((yn,)), dma((1,)), dma((2,)), dma((yn,)), dma((yn,)),
        dma((zn,)), dma((zn,)), dma((xn,)), dma((xn,)), dma((ch_n,)), dma((ch_n,)),
        dma((2, yn)), dma((2, yn)), dma((2, zn)), dma((2, zn)), dma((2, xn)), dma((2, xn)), dma((2, zn)), dma((2, zn)),
        dma((yn,)), dma((yn,)), dma((zn,)), dma((zn,)), dma((xn,)), dma((xn,)),
        dma((2,)), dma((2,)),
    ]
    in_vmem = pl.BlockSpec(memory_space=pltpu.VMEM)
    shapes = (
        jax.ShapeDtypeStruct((1, H, W, C), BF16), jax.ShapeDtypeStruct((1, H, W, C), BF16),
        jax.ShapeDtypeStruct((S, C), F32), jax.ShapeDtypeStruct((9, S), F32),
        jax.ShapeDtypeStruct((64, S), F32), jax.ShapeDtypeStruct((64, S), F32),
        jax.ShapeDtypeStruct((S, C), F32))
    results = pl.pallas_call(
        functools.partial(fused, rows_n, ch_n, grad_scale),
        out_shape=shapes,
        in_specs=[in_vmem] * 7,
        out_specs=(in_vmem,) * 7,
        scratch_shapes=scratch,
        compiler_params=pltpu.CompilerParams(
            collective_id=0, has_side_effects=True, vmem_limit_bytes=56 * 1024 * 1024),
    )(inputs, w_expand.T, kernel, w_se1.T, w_se2, w_project, cotangent)
    anywhere = pl.BlockSpec(memory_space=pl.ANY)
    output, d_input, d_expand_t, d_taps, d_se1_t, d_se2, d_project = pl.pallas_call(
        settle,
        out_shape=shapes,
        in_specs=[anywhere] * 7,
        out_specs=(anywhere,) * 7,
        scratch_shapes=[dma((7,))],
    )(*results)
    return output, d_input, d_expand_t.T, d_taps, d_se1_t.T, d_se2, d_project


def solution(mesh):
    return jax.shard_map(
        per_device,
        mesh=mesh,
        in_specs=(
            P(None, "rows", "ch", None),
            P(None, "ch"),
            P(None, "ch"),
            P("ch", None),
            P(None, "ch"),
            P("ch", None),
            P(None, "rows", "ch", None),
        ),
        out_specs=(
            P(None, "rows", "ch", None),
            P(None, "rows", "ch", None),
            P(None, "ch"),
            P(None, "ch"),
            P("ch", None),
            P(None, "ch"),
            P("ch", None),
        ),
        check_vma=False,
    )
```

```python
import functools
import math

import jax
import jax.numpy as jnp
from jax import lax
from jax.experimental import pallas as pl
from jax.experimental.pallas import tpu as pltpu
from jax.sharding import PartitionSpec as P

MESH = pl.DeviceIdType.MESH
F32 = jnp.float32
BF16 = jnp.bfloat16

CHIPS_Z = 8
H = 16
W = 32
C = 256
S = 192
PW = 72
EXPAND_ROWS = 10
GRAD_ROWS = 18
UNROLL = 4
NT_DIMS = (((1,), (1,)), ((), ()))
TN_DIMS = (((0,), (0,)), ((), ()))


def split3(row):
    hi = row.astype(BF16).astype(F32)
    mid = (row - hi).astype(BF16).astype(F32)
    low = row - hi - mid
    rest = jnp.zeros((5, row.shape[1]), F32)
    return jnp.concatenate([hi, mid, low, rest], axis=0).astype(BF16)


def sigm(v):
    return 0.5 * jnp.tanh(0.5 * v) + 0.5


def pairs3(left, right):
    def three(row):
        hi = row.astype(BF16).astype(F32)
        mid = (row - hi).astype(BF16).astype(F32)
        return hi, mid, row - hi - mid

    a, b = three(left), three(right)
    lefts = jnp.concatenate([a[k] for k in (0, 0, 1, 1, 0, 2, 1, 2)], axis=0).astype(BF16)
    rights = jnp.concatenate([b[k] for k in (0, 1, 0, 1, 2, 0, 2, 1)], axis=0).astype(BF16)
    return lefts, rights


def fused(rows_n, ch_n, scale, x_in, we_ref, tap_ref, se1_ref, se2_ref, wp_ref, c_in,
          out_ref, din_ref, dwe_ref, dk_ref, dse1_ref, dse2_ref, dwp_ref,
          xsib, csib, rowsend, rowbuf, colsend, colbuf, webuf, wpbuf, sesend, sebuf, tapsend, tapbuf,
          xf, cf, xs, cs, xnat, cnat, a1, s1, gh, s2, ca, cb, act2, ge, ktile, gacc, dkacc,
          vbuf, zv, xv, cv, gs, ysend, yrecv, zsend, zrecv, xrecv, fsend, frecv,
          dksend, dkyr, dkzr, dkxs, dkxr, dkzs, posend, porecv,
          sib_s, sib_r, row_s, row_r, col_s, col_r, we_s, we_r, wp_s, wp_r, se_s, se_r, rel_s, rel_r, tap_s, tap_r,
          vz_s, vz_r, vx_s, vx_r, vc_s, vc_r, gy_s, gy_r, gz_s, gz_r, gx_s, gx_r, gf_s, gf_r,
          ky_s, ky_r, kz_s, kz_r, kx_s, kx_r, po_s, po_r):
    x_ref, c_ref = x_in.at[0], c_in.at[0]
    zn = CHIPS_Z if rows_n % CHIPS_Z == 0 else 2
    xn = rows_n // zn
    yn = ch_n // 2
    ce = S * yn
    nt = ce // 128
    pairs = yn // 2
    zr = S // (zn // 2)
    row = lax.axis_index("rows")
    ch = lax.axis_index("ch")
    mx, mz = row // zn, lax.rem(row, zn)
    my, mc = ch // 2, lax.rem(ch, 2)
    oc = 1 - mc

    def dev_row(step):
        return lax.rem(row + step + rows_n, rows_n)

    def dev_y(step):
        return lax.rem(my + step + yn, yn)

    def copy(src, dst, ssem, rsem, where):
        return pltpu.make_async_remote_copy(
            src_ref=src, dst_ref=dst, send_sem=ssem, recv_sem=rsem, device_id=where, device_id_type=MESH)

    def at_y(peer):
        return (row, peer * 2 + mc)

    def at_z(peer):
        return (mx * zn + peer, ch)

    def at_x(peer):
        return (peer * zn + mz, ch)

    def at_ch(peer):
        return (row, peer)

    def spread(n, me, at, src, land, ssem, rsem):
        for step in range(1, n):
            peer = lax.rem(me + step, n)
            copy(src(peer), land.at[me], ssem.at[step - 1], rsem.at[me], at(peer)).start()

    def gathered(n, me, at, src, land, ssem, rsem):
        for step in range(1, n):
            peer = lax.rem(me + step, n)
            copy(src(peer), land.at[peer], ssem.at[step - 1], rsem.at[peer], at(peer)).wait()

    pair_mine = my // 2
    near = my + 1 - 2 * lax.rem(my, 2)
    far = [lax.rem(pair_mine + b, pairs) * 2 + k for b in range(1, pairs) for k in (0, 1)]

    def to_y(peers, first, src, land, ssem, rsem):
        for k, peer in enumerate(peers):
            copy(src(peer), land.at[my], ssem.at[first + k], rsem.at[my], at_y(peer)).start()

    def from_y(peers, first, src, land, ssem, rsem):
        for k, peer in enumerate(peers):
            copy(src(peer), land.at[peer], ssem.at[first + k], rsem.at[peer], at_y(peer)).wait()

    barrier = pltpu.get_barrier_semaphore()
    partners = [at_ch(lax.rem(ch + s, ch_n)) for s in range(1, ch_n)]
    partners += [at_z(lax.rem(mz + s, zn)) for s in range(1, zn)]
    partners += [at_x(lax.rem(mx + s, xn)) for s in range(1, xn)]
    partners += [(dev_row(dr), my * 2 + core) for dr in (-1, 1) for core in (0, 1)]
    partners += [(dev_row(dr), dev_y(dy) * 2 + core) for dr in (-1, 0, 1) for dy in (-1, 1) for core in (0, 1)]
    for where in partners:
        pl.semaphore_signal(barrier, inc=1, device_id=where, device_id_type=MESH)

    for d, (lo, edge) in enumerate(((0, 0), (H - 2, H - 1))):
        rowsend[d, 0:2 * W] = x_ref[lo:lo + 2].reshape(2 * W, C)
        rowsend[d, 2 * W:3 * W] = c_ref[edge]
    first = mc * (W - 2)
    ri = lax.broadcasted_iota(jnp.int32, (2 * H, H * W), 0)
    ci = lax.broadcasted_iota(jnp.int32, (2 * H, H * W), 1)
    pick = (ci == (ri & (H - 1)) * W + first + (ri >> 4)).astype(F32).astype(BF16)
    colsend[0:2 * H] = jnp.dot(pick, x_ref[...].reshape(H * W, C), preferred_element_type=F32).astype(BF16)
    ri = lax.broadcasted_iota(jnp.int32, (H, H * W), 0)
    ci = lax.broadcasted_iota(jnp.int32, (H, H * W), 1)
    pick = (ci == ri * W + mc * (W - 1)).astype(F32).astype(BF16)
    colsend[2 * H:3 * H] = jnp.dot(pick, c_ref[...].reshape(H * W, C), preferred_element_type=F32).astype(BF16)

    eye = (lax.broadcasted_iota(jnp.int32, (S, S), 0) == lax.broadcasted_iota(jnp.int32, (S, S), 1)).astype(F32).astype(BF16)
    se_t = jnp.concatenate([se1_ref[...], se2_ref[...]], axis=0)
    sesend[...] = lax.dot_general(eye, se_t, NT_DIMS, preferred_element_type=F32).astype(BF16)
    tap_rows = jnp.concatenate([tap_ref[...].astype(F32), jnp.zeros((7, S), F32)], axis=0)
    tapsend[...] = jnp.concatenate([tap_rows, jnp.zeros((16, 256 - S), F32)], axis=1).astype(BF16)

    pl.semaphore_wait(barrier, len(partners))

    sib = (row, my * 2 + oc)
    sib_copies = [copy(x_ref, xsib, sib_s.at[0], sib_r.at[0], sib), copy(c_ref, csib, sib_s.at[1], sib_r.at[1], sib)]
    row_copies = []
    for d, dr in ((0, -1), (1, 1)):
        for core in (0, 1):
            row_copies.append((copy(rowsend.at[d], rowbuf.at[1 - d, mc], row_s.at[d, core], row_r.at[1 - d, mc],
                                    (dev_row(dr), my * 2 + core)),
                               copy(rowsend.at[d], rowbuf.at[1 - d, core], row_s.at[d, core], row_r.at[1 - d, core],
                                    (dev_row(dr), my * 2 + core))))
    col_copies = []
    side = 1 - mc
    for i, dr in enumerate((-1, 0, 1)):
        for core in (0, 1):
            where = (dev_row(dr), dev_y(2 * mc - 1) * 2 + core)
            col_copies.append((copy(colsend, colbuf.at[side, 2 - i], col_s.at[i, core], col_r.at[side, 2 - i], where),
                               copy(colsend, colbuf.at[core, i], col_s.at[i, core], col_r.at[core, i], where)))
    sib_copies[0].start()
    for sent, _ in row_copies + col_copies:
        sent.start()
    to_y([near], 0, lambda p: we_ref, webuf, we_s, we_r)
    spread(yn, my, at_y, lambda p: tapsend, tapbuf, tap_s, tap_r)
    sib_copies[1].start()
    to_y(far, 1, lambda p: we_ref, webuf, we_s, we_r)
    to_y([near] + far, 0, lambda p: wp_ref, wpbuf, wp_s, wp_r)
    spread(yn, my, at_y, lambda p: sesend, sebuf.at[mc], se_s, se_r)
    relay = copy(sebuf.at[mc], sebuf.at[mc], rel_s.at[0], rel_r.at[mc], sib)
    relayed = copy(sebuf.at[mc], sebuf.at[oc], rel_s.at[0], rel_r.at[oc], sib)

    webuf[my] = we_ref[...]
    wpbuf[my] = wp_ref[...]
    tapbuf[my] = tapsend[...]
    sebuf[mc, my] = sesend[...]
    mine = pl.ds(pl.multiple_of(mc * W, W), W)
    other = pl.ds(pl.multiple_of(oc * W, W), W)
    xf[2:2 + H, mine] = x_ref[...].astype(F32)
    cf[1:1 + H, mine] = c_ref[...].astype(F32)
    xnat[:, mine] = x_ref[...]
    cnat[:, mine] = c_ref[...]
    sib_copies[0].wait()
    xf[2:2 + H, other] = xsib[...].astype(F32)
    xnat[:, other] = xsib[...]
    for _, landed in row_copies + col_copies:
        landed.wait()

    top_ok = row > 0
    low_ok = row < rows_n - 1
    left_ok = my > 0
    right_ok = my < yn - 1
    for d, ok in ((0, top_ok), (1, low_ok)):
        for core in (0, 1):
            part = rowbuf[d, core].astype(F32) * jnp.where(ok, 1.0, 0.0)
            xf[(2 + H) * d:(2 + H) * d + 2, W * core:W * core + W] = part[0:2 * W].reshape(2, W, C)
            cf[(1 + H) * d, W * core:W * core + W] = part[2 * W:3 * W]
    cols = colbuf[...].reshape(2 * 3 * 48, C)

    def rim(height, above, left_slot, right_slot):
        shape = (height * 8, 288)
        out_row = lax.broadcasted_iota(jnp.int32, shape, 0)
        src = lax.broadcasted_iota(jnp.int32, shape, 1)
        place = out_row & 7
        at_row = (out_row >> 3) - above
        third = jnp.where(at_row < 0, 0, jnp.where(at_row < H, 1, 2))
        ok = jnp.where(at_row < 0, top_ok.astype(jnp.int32), jnp.where(at_row < H, 1, low_ok.astype(jnp.int32)))
        want = third * 48 + (at_row & (H - 1))
        right_of = jnp.where(place < 4, 1, 0)
        slot = jnp.where(place < 4, right_slot(place), left_slot(place))
        ok = ok * jnp.where(slot < 0, 0, 1) * jnp.where(place < 4, right_ok.astype(jnp.int32), left_ok.astype(jnp.int32))
        want = want + right_of * 144 + slot * 16
        hit = jnp.where(src == want, ok, 0).astype(F32).astype(BF16)
        return jnp.dot(hit, cols, preferred_element_type=F32).reshape(height, 8, C)

    xf[:, 64:72] = rim(H + 4, 2, lambda k: jnp.where(k >= 6, k - 6, -1), lambda k: jnp.where(k < 2, k, -1))

    @pl.loop(0, (H + 4) // 2)
    def _(i):
        at = pl.ds(pl.multiple_of(i * 2 * PW, 2 * PW), 2 * PW)
        xs[at] = xf[pl.ds(i * 2, 2)].reshape(2 * PW, C).astype(BF16)

    gathered(yn, my, at_y, lambda p: tapsend, tapbuf, tap_s, tap_r)
    wide = jnp.concatenate([tapbuf[q].astype(F32)[:, 0:S] for q in range(yn)], axis=1)
    for t in range(nt):
        ktile[t] = wide[:, 128 * t:128 * t + 128]
    from_y([near], 0, lambda p: we_ref, webuf, we_s, we_r)

    for b in range(pairs):
        pair = lax.rem(pair_mine + b, pairs)
        if b == 1:
            from_y(far, 1, lambda p: we_ref, webuf, we_s, we_r)
        w_exp = webuf[pl.ds(pair * 2, 2)].reshape(2 * S, C)

        @pl.loop(0, (H + 4) // EXPAND_ROWS)
        def _(i):
            step = EXPAND_ROWS * PW
            at = pl.ds(pl.multiple_of(i * step, step), step)
            pre = lax.dot_general(xs[at], w_exp, NT_DIMS, preferred_element_type=F32)
            sig = sigm(pre)
            act = pre * sig
            slope = sig * (1.0 + (pre - act))
            for t in range(3):
                there = pl.ds(i * EXPAND_ROWS, EXPAND_ROWS)
                a1[pair * 3 + t, there] = act[:, 128 * t:128 * t + 128].reshape(EXPAND_ROWS, PW, 128)
                s1[pair * 3 + t, there] = slope[:, 128 * t:128 * t + 128].reshape(EXPAND_ROWS, PW, 128)

        @pl.loop(0, 3)
        def _(t3):
            t = pair * 3 + t3
            lanes = pl.ds(pl.multiple_of(t * 128, 128), 128)
            taps = [ktile[t, k:k + 1] for k in range(9)]

            def one_row(i):
                rows = [a1[t, i + r] for r in range(3)]
                parts = [taps[c] * rows[0] + taps[3 + c] * rows[1] + taps[6 + c] * rows[2] for c in range(3)]
                pre = parts[1] + pltpu.roll(parts[0], 1, 0) + pltpu.roll(parts[2], PW - 1, 0)
                sig = sigm(pre)
                act = pre * sig
                s2[t, i] = sig * (1.0 + (pre - act))
                return act[0:64]

            def center(i, pool):
                act = one_row(i)
                act2[i - 1, :, lanes] = act.astype(BF16)
                return pool + jnp.sum(act.reshape(8, 8, 128), axis=0)

            one_row(0)
            one_row(H + 1)
            pool = lax.fori_loop(1, H + 1, center, jnp.zeros((8, 128), F32), unroll=UNROLL)
            vbuf[pl.ds(t, 1)] = jnp.sum(pool, axis=0, keepdims=True)

    sib_copies[1].wait()
    cf[1:1 + H, other] = csib[...].astype(F32)
    cnat[:, other] = csib[...]
    cot_flat = cnat[...].reshape(H * 64, C)
    from_y([near] + far, 0, lambda p: wp_ref, wpbuf, wp_s, wp_r)
    ones = jnp.ones((8, C), F32).astype(BF16)
    for t in range(ce // 384):
        rows = lax.dot_general(
            act2[:, :, 384 * t:384 * t + 384].reshape(H * 64, 384), cot_flat, TN_DIMS, preferred_element_type=F32)
        gacc[384 * t:384 * t + 384] = rows
        prod = rows * wpbuf[2 * t:2 * t + 2].reshape(384, C).astype(F32)
        hi = prod.astype(BF16)
        rest = prod - hi.astype(F32)
        mid = rest.astype(BF16)
        low = (rest - mid.astype(F32)).astype(BF16)
        gate_sum = sum(lax.dot_general(ones, part, NT_DIMS, preferred_element_type=F32) for part in (hi, mid, low))
        for k in range(3):
            vbuf[8 + 3 * t + k:9 + 3 * t + k] = gate_sum[0:1, 128 * k:128 * k + 128]

    for t in range(nt, 8):
        vbuf[t:t + 1] = jnp.zeros((1, 128), F32)
        vbuf[8 + t:9 + t] = jnp.zeros((1, 128), F32)

    spread(zn, mz, at_z, lambda p: vbuf, zv, vz_s, vz_r)
    zv[mz] = vbuf[...]

    def send_rows(g, value):
        ysend[g] = value.reshape(yn, S, C).astype(BF16)
        to_y([near] + far, 0, lambda p: ysend.at[g, p], yrecv.at[g], gy_s.at[g], gy_r.at[g])
        yrecv[g, my] = ysend[g, my]

    def send_z(g):
        from_y([near] + far, 0, lambda p: ysend.at[g, p], yrecv.at[g], gy_s.at[g], gy_r.at[g])
        total = yrecv[g, 0].astype(F32)
        for q in range(1, yn):
            total = total + yrecv[g, q].astype(F32)
        for q in range(zn):
            zsend[g, q] = total[zr * (q // 2):zr * (q // 2) + zr, 128 * (q % 2):128 * (q % 2) + 128].astype(BF16)
        spread(zn, mz, at_z, lambda p: zsend.at[g, p], zrecv.at[g], gz_s.at[g], gz_r.at[g])
        zrecv[g, mz] = zsend[g, mz]

    def send_x(g):
        gathered(zn, mz, at_z, lambda p: zsend.at[g, p], zrecv.at[g], gz_s.at[g], gz_r.at[g])
        total = zrecv[g, 0].astype(F32)
        for q in range(1, zn):
            total = total + zrecv[g, q].astype(F32)
        fsend[g, 0] = total.astype(BF16)
        spread(xn, mx, at_x, lambda p: fsend.at[g, 0], xrecv.at[g], gx_s.at[g], gx_r.at[g])
        xrecv[g, mx] = fsend[g, 0]

    def send_back(g):
        gathered(xn, mx, at_x, lambda p: fsend.at[g, 0], xrecv.at[g], gx_s.at[g], gx_r.at[g])
        total = xrecv[g, 0].astype(F32)
        for q in range(1, xn):
            total = total + xrecv[g, q].astype(F32)
        fsend[g, 1] = total.astype(BF16)
        spread(zn, mz, at_z, lambda p: fsend.at[g, 1], frecv.at[g], gf_s.at[g], gf_r.at[g])
        frecv[g, mz] = fsend[g, 1]

    def whole(g, into):
        gathered(zn, mz, at_z, lambda p: fsend.at[g, 1], frecv.at[g], gf_s.at[g], gf_r.at[g])
        for q in range(zn):
            into[zr * (q // 2):zr * (q // 2) + zr, 128 * (q % 2):128 * (q % 2) + 128] = frecv[g, q].astype(F32)

    send_rows(0, gacc[...])
    gathered(yn, my, at_y, lambda p: sesend, sebuf.at[mc], se_s, se_r)
    relay.start()

    cf[:, 64:72] = rim(H + 2, 1, lambda k: jnp.where(k == 7, 2, -1), lambda k: jnp.where(k == 0, 2, -1))

    @pl.loop(0, (H + 2) // 2)
    def _(i):
        at = pl.ds(pl.multiple_of(i * 2 * PW, 2 * PW), 2 * PW)
        cs[at] = cf[pl.ds(i * 2, 2)].reshape(2 * PW, C).astype(BF16)

    def hidden_grad(pair):
        w_pro = wpbuf[2 * pair:2 * pair + 2].reshape(2 * S, C)

        @pl.loop(0, (H + 2) // GRAD_ROWS)
        def _(i):
            step = GRAD_ROWS * PW
            at = pl.ds(pl.multiple_of(i * step, step), step)
            back = lax.dot_general(cs[at], w_pro, NT_DIMS, preferred_element_type=F32)
            for t in range(3):
                gh[pair * 3 + t, pl.ds(i * GRAD_ROWS, GRAD_ROWS)] = back[:, 128 * t:128 * t + 128].reshape(GRAD_ROWS, PW, 128)

    place = lax.broadcasted_iota(jnp.int32, (PW, 128), 0)
    off_left = jnp.where(left_ok, PW, PW - 1)
    off_right = jnp.where(right_ok, 0, 1)
    inside = jnp.where((place < 64) | ((place == 64) & (off_right == 0)) | ((place == PW - 1) & (off_left == PW)), 1.0, 0.0)

    def depth_back(pair):
        @pl.loop(0, 3)
        def _(t3):
            t = pair * 3 + t3
            taps = [ktile[t, k:k + 1] for k in range(9)]

            @pl.loop(0, H + 2, unroll=2)
            def _(i):
                keep = jnp.where(((i > 0) | top_ok) & ((i < H + 1) | low_ok), 1.0, 0.0)
                slope = s2[t, i] * (inside * keep)
                s2[t, i] = slope
                gh[t, i] = gh[t, i] * slope

            @pl.loop(0, H, unroll=UNROLL)
            def _(i):
                first_slope = s1[t, i + 2, 0:64]
                for source, into in ((gh, ca), (s2, cb)):
                    rows = [source[t, i + r] for r in range(3)]
                    parts = [taps[c] * rows[2] + taps[3 + c] * rows[1] + taps[6 + c] * rows[0] for c in range(3)]
                    grad = parts[1] + pltpu.roll(parts[0], PW - 1, 0) + pltpu.roll(parts[2], 1, 0)
                    into[t, i] = grad[0:64] * first_slope

    for pair in range(pairs):
        hidden_grad(pair)
    gathered(zn, mz, at_z, lambda p: vbuf, zv, vz_s, vz_r)
    xv[mx] = jnp.sum(zv[...], axis=0)
    spread(xn, mx, at_x, lambda p: xv.at[mx], xv, vx_s, vx_r)
    depth_back(0)
    gathered(xn, mx, at_x, lambda p: xv.at[mx], xv, vx_s, vx_r)
    cv[ch] = jnp.sum(xv[...], axis=0)
    spread(ch_n, ch, at_ch, lambda p: cv.at[ch], cv, vc_s, vc_r)
    for pair in range(1, pairs):
        depth_back(pair)
    gathered(ch_n, ch, at_ch, lambda p: cv.at[ch], cv, vc_s, vc_r)
    relayed.wait()

    area = float(rows_n * H * yn * 2 * W)
    pooled, gate_grad, weights = [], [], []
    for core in (0, 1):
        total = cv[core]
        for q in range(1, yn):
            total = total + cv[2 * q + core]
        pooled.append(jnp.concatenate([total[t:t + 1] for t in range(nt)], axis=1) * (1.0 / area))
        gate_grad.append(jnp.concatenate([total[8 + t:9 + t] for t in range(nt)], axis=1))
        weights.append(sebuf[core].reshape(ce, 128))
    half = lax.broadcasted_iota(jnp.int32, (1, 128), 1) < 64

    def down(vectors):
        total = jnp.zeros((1, 128), F32)
        for core in (0, 1):
            total = total + jnp.sum(jnp.dot(split3(vectors[core]), weights[core], preferred_element_type=F32), axis=0, keepdims=True)
        return total

    def up(vector, core):
        return jnp.sum(lax.dot_general(split3(vector), weights[core], NT_DIMS, preferred_element_type=F32), axis=0, keepdims=True)

    squeeze_pre = jnp.where(half, down(pooled), 0.0)
    squeeze_sig = sigm(squeeze_pre)
    squeeze_act = squeeze_pre * squeeze_sig
    shifted = pltpu.roll(jnp.broadcast_to(squeeze_act, (8, 128)), 64, 1)[0:1]
    gates = [sigm(up(shifted, core)) for core in (0, 1)]
    excite = [gate_grad[core] * gates[core] * (1.0 - gates[core]) for core in (0, 1)]
    back = pltpu.roll(jnp.broadcast_to(down(excite), (8, 128)), 64, 1)[0:1]
    squeeze_slope = squeeze_sig * (1.0 + squeeze_pre * (1.0 - squeeze_sig))
    grad_squeeze = jnp.where(half, back * squeeze_slope, 0.0)

    def own(values):
        return jnp.where(mc == 0, values[0], values[1])

    gate = own(gates)
    grad_pool = own([up(grad_squeeze, core) for core in (0, 1)]) * (1.0 / area)
    for t in range(nt):
        gs[0, t:t + 1] = gate[:, 128 * t:128 * t + 128]
        gs[1, t:t + 1] = grad_pool[:, 128 * t:128 * t + 128]
    send_z(0)

    def shard_of(rows):
        part = rows[:, 0:S]
        for q in range(1, yn):
            part = jnp.where(my == q, rows[:, S * q:S * q + S], part)
        return part

    def project(source, k, w_all, into):
        def part(where):
            rows = source[:, where].reshape(H * W, ce)
            return jnp.dot(rows, w_all, preferred_element_type=F32).reshape(H, W, C)

        posend[k] = part(other).astype(BF16)
        copy(posend.at[k], porecv.at[k], po_s.at[k], po_r.at[k], sib).start()
        into[...] = part(mine)

    def projected(k, base, total, into):
        copy(posend.at[k], porecv.at[k], po_s.at[k], po_r.at[k], sib).wait()
        into[0] = (base[...].astype(F32) + (total[...] + porecv[k].astype(F32))).astype(BF16)

    x_flat = xnat[...].reshape(H * 64, C)
    for b in range(pairs):
        pair = lax.rem(pair_mine + 1 + b, pairs)

        @pl.loop(0, 3)
        def _(t3):
            t = pair * 3 + t3
            lanes = pl.ds(pl.multiple_of(t * 128, 128), 128)
            gate_t = gs[0, pl.ds(t, 1)]
            pool_t = gs[1, pl.ds(t, 1)]

            @pl.loop(0, H, unroll=UNROLL)
            def _(i):
                ge[i, :, lanes] = (ca[t, i] * gate_t + cb[t, i] * pool_t).astype(BF16)

        lanes3 = pl.ds(pl.multiple_of(pair * 384, 384), 384)
        rows = lax.dot_general(ge[:, :, lanes3].reshape(H * 64, 384), x_flat, TN_DIMS, preferred_element_type=F32)
        ysend[1, pl.ds(pair * 2, 2)] = rows.reshape(2, S, C).astype(BF16)
        if b < pairs - 1:
            to_y(far, 1, lambda p: ysend.at[1, p], yrecv.at[1], gy_s.at[1], gy_r.at[1])
            send_x(0)
        else:
            to_y([near], 0, lambda p: ysend.at[1, p], yrecv.at[1], gy_s.at[1], gy_r.at[1])
            yrecv[1, my] = ysend[1, my]

    project(ge, 1, webuf[...].reshape(ce, C), cf.at[0:H, 0:W])
    if pairs == 1:
        send_x(0)
    send_back(0)

    @pl.loop(0, nt)
    def _(t):
        gate_t = gs[0, pl.ds(t, 1)]
        pool_t = gs[1, pl.ds(t, 1)]

        def center(i, sums):
            grad = gh[t, i + 1, 0:64] * gate_t + s2[t, i + 1, 0:64] * pool_t
            here = jnp.concatenate([grad, jnp.zeros((8, 128), F32)], axis=0)
            moved = [pltpu.roll(here, PW - 1, 0), here, pltpu.roll(here, 1, 0)]
            fresh = []
            for r in range(3):
                act = a1[t, i + 1 + r]
                for c in range(3):
                    fresh.append(sums[3 * r + c] + jnp.sum((moved[c] * act).reshape(9, 8, 128), axis=0))
            return tuple(fresh)

        sums = lax.fori_loop(0, H, center, (jnp.zeros((8, 128), F32),) * 9, unroll=UNROLL)
        dkacc[t] = jnp.concatenate(
            [jnp.sum(part, axis=0, keepdims=True) for part in sums] + [jnp.zeros((7, 128), F32)], axis=0)

    dksend[...] = jnp.concatenate([dkacc[t] for t in range(nt)], axis=1).astype(BF16)
    spread(yn, my, at_y, lambda p: dksend, dkyr, ky_s, ky_r)
    dkyr[my] = dksend[...]
    send_z(1)

    @pl.loop(0, H)
    def _(i):
        act2[i] = (act2[i].astype(F32) * gate).astype(BF16)

    project(act2, 0, wpbuf[...].reshape(ce, C), xf.at[0:H, 0:W])

    def summed(parts):
        total = parts[0].astype(F32)
        for q in range(1, parts.shape[0]):
            total = total + parts[q].astype(F32)
        return total

    gathered(yn, my, at_y, lambda p: dksend, dkyr, ky_s, ky_r)
    dkzs[...] = jnp.concatenate([shard_of(summed(dkyr)), jnp.zeros((16, 256 - S), F32)], axis=1).astype(BF16)
    spread(zn, mz, at_z, lambda p: dkzs, dkzr, kz_s, kz_r)
    dkzr[mz] = dkzs[...]
    send_x(1)
    projected(1, c_ref, cf.at[0:H, 0:W], din_ref)
    gathered(zn, mz, at_z, lambda p: dkzs, dkzr, kz_s, kz_r)
    dkxs[...] = summed(dkzr).astype(BF16)
    spread(xn, mx, at_x, lambda p: dkxs, dkxr, kx_s, kx_r)
    dkxr[mx] = dkxs[...]
    send_back(1)

    own_gate = shard_of(gate)
    lefts, rights = pairs3(grad_squeeze * scale, shard_of(own(pooled)))
    dse1_ref[...] = lax.dot_general(lefts, rights, TN_DIMS, preferred_element_type=F32)[0:64]
    lefts, rights = pairs3(squeeze_act, shard_of(own(excite)) * scale)
    dse2_ref[...] = lax.dot_general(lefts, rights, TN_DIMS, preferred_element_type=F32)[0:64]
    gate_wide = lax.dot_general(split3(own_gate * scale), ones, TN_DIMS, preferred_element_type=F32)
    projected(0, x_ref, xf.at[0:H, 0:W], out_ref)
    whole(0, gacc.at[0:S])
    dwp_ref[...] = gacc[0:S] * gate_wide
    gathered(xn, mx, at_x, lambda p: dkxs, dkxr, kx_s, kx_r)
    dk_ref[...] = summed(dkxr)[0:9, 0:S] * scale
    whole(1, gacc.at[S:2 * S])
    dwe_ref[...] = gacc[S:2 * S] * scale


def settle(*refs):
    count = (len(refs) - 1) // 2
    moves = [pltpu.make_async_copy(refs[k], refs[count + k], refs[-1].at[k]) for k in range(count)]
    for move in moves:
        move.start()
    for move in moves:
        move.wait()


def per_device(inputs, w_expand, kernel, w_se1, w_se2, w_project, cotangent):
    rows_n, ch_n = lax.axis_size("rows"), lax.axis_size("ch")
    zn = CHIPS_Z if rows_n % CHIPS_Z == 0 else 2
    xn, yn = rows_n // zn, ch_n // 2
    ce = S * yn
    nt = ce // 128
    zr = S // (zn // 2)
    grad_scale = 1.0 / math.sqrt(rows_n * H * ch_n * W)
    vmem, dma = pltpu.VMEM, pltpu.SemaphoreType.DMA
    scratch = [
        vmem((H, W, C), BF16), vmem((H, W, C), BF16),
        vmem((2, 3 * W, C), BF16), vmem((2, 2, 3 * W, C), BF16),
        vmem((3 * H, C), BF16), vmem((2, 3, 3 * H, C), BF16),
        vmem((yn, S, C), BF16), vmem((yn, S, C), BF16),
        vmem((S, 128), BF16), vmem((2, yn, S, 128), BF16),
        vmem((16, 256), BF16), vmem((yn, 16, 256), BF16),
        vmem((H + 4, PW, C), F32), vmem((H + 2, PW, C), F32),
        vmem(((H + 4) * PW, C), BF16), vmem(((H + 2) * PW, C), BF16),
        vmem((H, 64, C), BF16), vmem((H, 64, C), BF16),
        vmem((nt, H + 4, PW, 128), F32), vmem((nt, H + 4, PW, 128), F32),
        vmem((nt, H + 2, PW, 128), F32), vmem((nt, H + 2, PW, 128), F32),
        vmem((nt, H, 64, 128), F32), vmem((nt, H, 64, 128), F32),
        vmem((H, 64, ce), BF16), vmem((H, 64, ce), BF16),
        vmem((nt, 16, 128), F32), vmem((ce, C), F32), vmem((nt, 16, 128), F32),
        vmem((16, 128), F32), vmem((zn, 16, 128), F32), vmem((xn, 16, 128), F32), vmem((ch_n, 16, 128), F32),
        vmem((2, 8, 128), F32),
        vmem((2, yn, S, C), BF16), vmem((2, yn, S, C), BF16),
        vmem((2, zn, zr, 128), BF16), vmem((2, zn, zr, 128), BF16),
        vmem((2, xn, zr, 128), BF16), vmem((2, 2, zr, 128), BF16), vmem((2, zn, zr, 128), BF16),
        vmem((16, ce), BF16), vmem((yn, 16, ce), BF16),
        vmem((zn, 16, 256), BF16), vmem((16, 256), BF16), vmem((xn, 16, 256), BF16), vmem((16, 256), BF16),
        vmem((2, H, W, C), BF16), vmem((2, H, W, C), BF16),
        dma((2,)), dma((2,)), dma((2, 2)), dma((2, 2)), dma((3, 2)), dma((2, 3)),
        dma((yn,)), dma((yn,)), dma((yn,)), dma((yn,)),
        dma((yn,)), dma((yn,)), dma((1,)), dma((2,)), dma((yn,)), dma((yn,)),
        dma((zn,)), dma((zn,)), dma((xn,)), dma((xn,)), dma((ch_n,)), dma((ch_n,)),
        dma((2, yn)), dma((2, yn)), dma((2, zn)), dma((2, zn)), dma((2, xn)), dma((2, xn)), dma((2, zn)), dma((2, zn)),
        dma((yn,)), dma((yn,)), dma((zn,)), dma((zn,)), dma((xn,)), dma((xn,)),
        dma((2,)), dma((2,)),
    ]
    in_vmem = pl.BlockSpec(memory_space=pltpu.VMEM)
    shapes = (
        jax.ShapeDtypeStruct((1, H, W, C), BF16), jax.ShapeDtypeStruct((1, H, W, C), BF16),
        jax.ShapeDtypeStruct((S, C), F32), jax.ShapeDtypeStruct((9, S), F32),
        jax.ShapeDtypeStruct((64, S), F32), jax.ShapeDtypeStruct((64, S), F32),
        jax.ShapeDtypeStruct((S, C), F32))
    results = pl.pallas_call(
        functools.partial(fused, rows_n, ch_n, grad_scale),
        out_shape=shapes,
        in_specs=[in_vmem] * 7,
        out_specs=(in_vmem,) * 7,
        scratch_shapes=scratch,
        compiler_params=pltpu.CompilerParams(
            collective_id=0, has_side_effects=True, vmem_limit_bytes=56 * 1024 * 1024),
    )(inputs, w_expand.T, kernel, w_se1.T, w_se2, w_project, cotangent)
    anywhere = pl.BlockSpec(memory_space=pl.ANY)
    output, d_input, d_expand_t, d_taps, d_se1_t, d_se2, d_project = pl.pallas_call(
        settle,
        out_shape=shapes,
        in_specs=[anywhere] * 7,
        out_specs=(in_vmem,) * 7,
        scratch_shapes=[dma((7,))],
    )(*results)
    return output, d_input, d_expand_t.T, d_taps, d_se1_t.T, d_se2, d_project


def solution(mesh):
    return jax.shard_map(
        per_device,
        mesh=mesh,
        in_specs=(
            P(None, "rows", "ch", None),
            P(None, "ch"),
            P(None, "ch"),
            P("ch", None),
            P(None, "ch"),
            P("ch", None),
            P(None, "rows", "ch", None),
        ),
        out_specs=(
            P(None, "rows", "ch", None),
            P(None, "rows", "ch", None),
            P(None, "ch"),
            P(None, "ch"),
            P("ch", None),
            P(None, "ch"),
            P("ch", None),
        ),
        check_vma=False,
    )
```

```python
import functools
import math

import jax
import jax.numpy as jnp
from jax import lax
from jax.experimental import pallas as pl
from jax.experimental.pallas import tpu as pltpu
from jax.sharding import PartitionSpec as P

MESH = pl.DeviceIdType.MESH
F32 = jnp.float32
BF16 = jnp.bfloat16

CHIPS_Z = 8
H = 16
W = 32
C = 256
S = 192
PW = 72
EXPAND_ROWS = 10
GRAD_ROWS = 18
UNROLL = 4
NT_DIMS = (((1,), (1,)), ((), ()))
TN_DIMS = (((0,), (0,)), ((), ()))


def split3(row):
    hi = row.astype(BF16).astype(F32)
    mid = (row - hi).astype(BF16).astype(F32)
    low = row - hi - mid
    rest = jnp.zeros((5, row.shape[1]), F32)
    return jnp.concatenate([hi, mid, low, rest], axis=0).astype(BF16)


def sigm(v):
    return 0.5 * jnp.tanh(0.5 * v) + 0.5


def pairs3(left, right):
    def three(row):
        hi = row.astype(BF16).astype(F32)
        mid = (row - hi).astype(BF16).astype(F32)
        return hi, mid, row - hi - mid

    a, b = three(left), three(right)
    lefts = jnp.concatenate([a[k] for k in (0, 0, 1, 1, 0, 2, 1, 2)], axis=0).astype(BF16)
    rights = jnp.concatenate([b[k] for k in (0, 1, 0, 1, 2, 0, 2, 1)], axis=0).astype(BF16)
    return lefts, rights


def fused(rows_n, ch_n, scale, x_in, we_in, tap_in, se1_in, se2_in, wp_in, c_in,
          out_ref, din_ref, dwe_ref, dk_ref, dse1_ref, dse2_ref, dwp_ref,
          x_ref, we_ref, tap_ref, se1_ref, se2_ref, wp_ref, c_ref, xsib, csib, rowsend, rowbuf, colsend, colbuf, webuf, wpbuf, sesend, sebuf, tapsend, tapbuf,
          xf, cf, xs, cs, xnat, cnat, a1, s1, gh, s2, ca, cb, act2, ge, ktile, gacc, dkacc,
          vbuf, zv, xv, cv, gs, ysend, yrecv, zsend, zrecv, xrecv, fsend, frecv,
          dksend, dkyr, dkzr, dkxs, dkxr, dkzs, posend, porecv,
          load_s, sib_s, sib_r, row_s, row_r, col_s, col_r, we_s, we_r, wp_s, wp_r, se_s, se_r, rel_s, rel_r, tap_s, tap_r,
          vz_s, vz_r, vx_s, vx_r, vc_s, vc_r, gy_s, gy_r, gz_s, gz_r, gx_s, gx_r, gf_s, gf_r,
          ky_s, ky_r, kz_s, kz_r, kx_s, kx_r, po_s, po_r):
    zn = CHIPS_Z if rows_n % CHIPS_Z == 0 else 2
    xn = rows_n // zn
    yn = ch_n // 2
    ce = S * yn
    nt = ce // 128
    pairs = yn // 2
    zr = S // (zn // 2)
    row = lax.axis_index("rows")
    ch = lax.axis_index("ch")
    mx, mz = row // zn, lax.rem(row, zn)
    my, mc = ch // 2, lax.rem(ch, 2)
    oc = 1 - mc

    def dev_row(step):
        return lax.rem(row + step + rows_n, rows_n)

    def dev_y(step):
        return lax.rem(my + step + yn, yn)

    def copy(src, dst, ssem, rsem, where):
        return pltpu.make_async_remote_copy(
            src_ref=src, dst_ref=dst, send_sem=ssem, recv_sem=rsem, device_id=where, device_id_type=MESH)

    def at_y(peer):
        return (row, peer * 2 + mc)

    def at_z(peer):
        return (mx * zn + peer, ch)

    def at_x(peer):
        return (peer * zn + mz, ch)

    def at_ch(peer):
        return (row, peer)

    def spread(n, me, at, src, land, ssem, rsem):
        for step in range(1, n):
            peer = lax.rem(me + step, n)
            copy(src(peer), land.at[me], ssem.at[step - 1], rsem.at[me], at(peer)).start()

    def gathered(n, me, at, src, land, ssem, rsem):
        for step in range(1, n):
            peer = lax.rem(me + step, n)
            copy(src(peer), land.at[peer], ssem.at[step - 1], rsem.at[peer], at(peer)).wait()

    pair_mine = my // 2
    near = my + 1 - 2 * lax.rem(my, 2)
    far = [lax.rem(pair_mine + b, pairs) * 2 + k for b in range(1, pairs) for k in (0, 1)]

    def to_y(peers, first, src, land, ssem, rsem):
        for k, peer in enumerate(peers):
            copy(src(peer), land.at[my], ssem.at[first + k], rsem.at[my], at_y(peer)).start()

    def from_y(peers, first, src, land, ssem, rsem):
        for k, peer in enumerate(peers):
            copy(src(peer), land.at[peer], ssem.at[first + k], rsem.at[peer], at_y(peer)).wait()

    barrier = pltpu.get_barrier_semaphore()
    partners = [at_ch(lax.rem(ch + s, ch_n)) for s in range(1, ch_n)]
    partners += [at_z(lax.rem(mz + s, zn)) for s in range(1, zn)]
    partners += [at_x(lax.rem(mx + s, xn)) for s in range(1, xn)]
    partners += [(dev_row(dr), my * 2 + core) for dr in (-1, 1) for core in (0, 1)]
    partners += [(dev_row(dr), dev_y(dy) * 2 + core) for dr in (-1, 0, 1) for dy in (-1, 1) for core in (0, 1)]
    for where in partners:
        pl.semaphore_signal(barrier, inc=1, device_id=where, device_id_type=MESH)

    arrays = ((x_in.at[0], x_ref), (c_in.at[0], c_ref), (we_in, we_ref), (tap_in, tap_ref), (se1_in, se1_ref),
              (se2_in, se2_ref), (wp_in, wp_ref))
    loads = [pltpu.make_async_copy(source, into, load_s.at[k]) for k, (source, into) in enumerate(arrays)]
    for load in loads:
        load.start()
    for load in loads:
        load.wait()

    for d, (lo, edge) in enumerate(((0, 0), (H - 2, H - 1))):
        rowsend[d, 0:2 * W] = x_ref[lo:lo + 2].reshape(2 * W, C)
        rowsend[d, 2 * W:3 * W] = c_ref[edge]
    first = mc * (W - 2)
    ri = lax.broadcasted_iota(jnp.int32, (2 * H, H * W), 0)
    ci = lax.broadcasted_iota(jnp.int32, (2 * H, H * W), 1)
    pick = (ci == (ri & (H - 1)) * W + first + (ri >> 4)).astype(F32).astype(BF16)
    colsend[0:2 * H] = jnp.dot(pick, x_ref[...].reshape(H * W, C), preferred_element_type=F32).astype(BF16)
    ri = lax.broadcasted_iota(jnp.int32, (H, H * W), 0)
    ci = lax.broadcasted_iota(jnp.int32, (H, H * W), 1)
    pick = (ci == ri * W + mc * (W - 1)).astype(F32).astype(BF16)
    colsend[2 * H:3 * H] = jnp.dot(pick, c_ref[...].reshape(H * W, C), preferred_element_type=F32).astype(BF16)

    eye = (lax.broadcasted_iota(jnp.int32, (S, S), 0) == lax.broadcasted_iota(jnp.int32, (S, S), 1)).astype(F32).astype(BF16)
    se_t = jnp.concatenate([se1_ref[...], se2_ref[...]], axis=0)
    sesend[...] = lax.dot_general(eye, se_t, NT_DIMS, preferred_element_type=F32).astype(BF16)
    tap_rows = jnp.concatenate([tap_ref[...].astype(F32), jnp.zeros((7, S), F32)], axis=0)
    tapsend[...] = jnp.concatenate([tap_rows, jnp.zeros((16, 256 - S), F32)], axis=1).astype(BF16)

    pl.semaphore_wait(barrier, len(partners))

    sib = (row, my * 2 + oc)
    sib_copies = [copy(x_ref, xsib, sib_s.at[0], sib_r.at[0], sib), copy(c_ref, csib, sib_s.at[1], sib_r.at[1], sib)]
    row_copies = []
    for d, dr in ((0, -1), (1, 1)):
        for core in (0, 1):
            row_copies.append((copy(rowsend.at[d], rowbuf.at[1 - d, mc], row_s.at[d, core], row_r.at[1 - d, mc],
                                    (dev_row(dr), my * 2 + core)),
                               copy(rowsend.at[d], rowbuf.at[1 - d, core], row_s.at[d, core], row_r.at[1 - d, core],
                                    (dev_row(dr), my * 2 + core))))
    col_copies = []
    side = 1 - mc
    for i, dr in enumerate((-1, 0, 1)):
        for core in (0, 1):
            where = (dev_row(dr), dev_y(2 * mc - 1) * 2 + core)
            col_copies.append((copy(colsend, colbuf.at[side, 2 - i], col_s.at[i, core], col_r.at[side, 2 - i], where),
                               copy(colsend, colbuf.at[core, i], col_s.at[i, core], col_r.at[core, i], where)))
    sib_copies[0].start()
    for sent, _ in row_copies + col_copies:
        sent.start()
    to_y([near], 0, lambda p: we_ref, webuf, we_s, we_r)
    spread(yn, my, at_y, lambda p: tapsend, tapbuf, tap_s, tap_r)
    sib_copies[1].start()
    to_y(far, 1, lambda p: we_ref, webuf, we_s, we_r)
    to_y([near] + far, 0, lambda p: wp_ref, wpbuf, wp_s, wp_r)
    spread(yn, my, at_y, lambda p: sesend, sebuf.at[mc], se_s, se_r)
    relay = copy(sebuf.at[mc], sebuf.at[mc], rel_s.at[0], rel_r.at[mc], sib)
    relayed = copy(sebuf.at[mc], sebuf.at[oc], rel_s.at[0], rel_r.at[oc], sib)

    webuf[my] = we_ref[...]
    wpbuf[my] = wp_ref[...]
    tapbuf[my] = tapsend[...]
    sebuf[mc, my] = sesend[...]
    mine = pl.ds(pl.multiple_of(mc * W, W), W)
    other = pl.ds(pl.multiple_of(oc * W, W), W)
    xf[2:2 + H, mine] = x_ref[...].astype(F32)
    cf[1:1 + H, mine] = c_ref[...].astype(F32)
    xnat[:, mine] = x_ref[...]
    cnat[:, mine] = c_ref[...]
    sib_copies[0].wait()
    xf[2:2 + H, other] = xsib[...].astype(F32)
    xnat[:, other] = xsib[...]
    for _, landed in row_copies + col_copies:
        landed.wait()

    top_ok = row > 0
    low_ok = row < rows_n - 1
    left_ok = my > 0
    right_ok = my < yn - 1
    for d, ok in ((0, top_ok), (1, low_ok)):
        for core in (0, 1):
            part = rowbuf[d, core].astype(F32) * jnp.where(ok, 1.0, 0.0)
            xf[(2 + H) * d:(2 + H) * d + 2, W * core:W * core + W] = part[0:2 * W].reshape(2, W, C)
            cf[(1 + H) * d, W * core:W * core + W] = part[2 * W:3 * W]
    cols = colbuf[...].reshape(2 * 3 * 48, C)

    def rim(height, above, left_slot, right_slot):
        shape = (height * 8, 288)
        out_row = lax.broadcasted_iota(jnp.int32, shape, 0)
        src = lax.broadcasted_iota(jnp.int32, shape, 1)
        place = out_row & 7
        at_row = (out_row >> 3) - above
        third = jnp.where(at_row < 0, 0, jnp.where(at_row < H, 1, 2))
        ok = jnp.where(at_row < 0, top_ok.astype(jnp.int32), jnp.where(at_row < H, 1, low_ok.astype(jnp.int32)))
        want = third * 48 + (at_row & (H - 1))
        right_of = jnp.where(place < 4, 1, 0)
        slot = jnp.where(place < 4, right_slot(place), left_slot(place))
        ok = ok * jnp.where(slot < 0, 0, 1) * jnp.where(place < 4, right_ok.astype(jnp.int32), left_ok.astype(jnp.int32))
        want = want + right_of * 144 + slot * 16
        hit = jnp.where(src == want, ok, 0).astype(F32).astype(BF16)
        return jnp.dot(hit, cols, preferred_element_type=F32).reshape(height, 8, C)

    xf[:, 64:72] = rim(H + 4, 2, lambda k: jnp.where(k >= 6, k - 6, -1), lambda k: jnp.where(k < 2, k, -1))

    @pl.loop(0, (H + 4) // 2)
    def _(i):
        at = pl.ds(pl.multiple_of(i * 2 * PW, 2 * PW), 2 * PW)
        xs[at] = xf[pl.ds(i * 2, 2)].reshape(2 * PW, C).astype(BF16)

    gathered(yn, my, at_y, lambda p: tapsend, tapbuf, tap_s, tap_r)
    wide = jnp.concatenate([tapbuf[q].astype(F32)[:, 0:S] for q in range(yn)], axis=1)
    for t in range(nt):
        ktile[t] = wide[:, 128 * t:128 * t + 128]
    from_y([near], 0, lambda p: we_ref, webuf, we_s, we_r)

    for b in range(pairs):
        pair = lax.rem(pair_mine + b, pairs)
        if b == 1:
            from_y(far, 1, lambda p: we_ref, webuf, we_s, we_r)
        w_exp = webuf[pl.ds(pair * 2, 2)].reshape(2 * S, C)

        @pl.loop(0, (H + 4) // EXPAND_ROWS)
        def _(i):
            step = EXPAND_ROWS * PW
            at = pl.ds(pl.multiple_of(i * step, step), step)
            pre = lax.dot_general(xs[at], w_exp, NT_DIMS, preferred_element_type=F32)
            sig = sigm(pre)
            act = pre * sig
            slope = sig * (1.0 + (pre - act))
            for t in range(3):
                there = pl.ds(i * EXPAND_ROWS, EXPAND_ROWS)
                a1[pair * 3 + t, there] = act[:, 128 * t:128 * t + 128].reshape(EXPAND_ROWS, PW, 128)
                s1[pair * 3 + t, there] = slope[:, 128 * t:128 * t + 128].reshape(EXPAND_ROWS, PW, 128)

        @pl.loop(0, 3)
        def _(t3):
            t = pair * 3 + t3
            lanes = pl.ds(pl.multiple_of(t * 128, 128), 128)
            taps = [ktile[t, k:k + 1] for k in range(9)]

            def one_row(i):
                rows = [a1[t, i + r] for r in range(3)]
                parts = [taps[c] * rows[0] + taps[3 + c] * rows[1] + taps[6 + c] * rows[2] for c in range(3)]
                pre = parts[1] + pltpu.roll(parts[0], 1, 0) + pltpu.roll(parts[2], PW - 1, 0)
                sig = sigm(pre)
                act = pre * sig
                s2[t, i] = sig * (1.0 + (pre - act))
                return act[0:64]

            def center(i, pool):
                act = one_row(i)
                act2[i - 1, :, lanes] = act.astype(BF16)
                return pool + jnp.sum(act.reshape(8, 8, 128), axis=0)

            one_row(0)
            one_row(H + 1)
            pool = lax.fori_loop(1, H + 1, center, jnp.zeros((8, 128), F32), unroll=UNROLL)
            vbuf[pl.ds(t, 1)] = jnp.sum(pool, axis=0, keepdims=True)

    sib_copies[1].wait()
    cf[1:1 + H, other] = csib[...].astype(F32)
    cnat[:, other] = csib[...]
    cot_flat = cnat[...].reshape(H * 64, C)
    from_y([near] + far, 0, lambda p: wp_ref, wpbuf, wp_s, wp_r)
    ones = jnp.ones((8, C), F32).astype(BF16)
    for t in range(ce // 384):
        rows = lax.dot_general(
            act2[:, :, 384 * t:384 * t + 384].reshape(H * 64, 384), cot_flat, TN_DIMS, preferred_element_type=F32)
        gacc[384 * t:384 * t + 384] = rows
        prod = rows * wpbuf[2 * t:2 * t + 2].reshape(384, C).astype(F32)
        hi = prod.astype(BF16)
        rest = prod - hi.astype(F32)
        mid = rest.astype(BF16)
        low = (rest - mid.astype(F32)).astype(BF16)
        gate_sum = sum(lax.dot_general(ones, part, NT_DIMS, preferred_element_type=F32) for part in (hi, mid, low))
        for k in range(3):
            vbuf[8 + 3 * t + k:9 + 3 * t + k] = gate_sum[0:1, 128 * k:128 * k + 128]

    for t in range(nt, 8):
        vbuf[t:t + 1] = jnp.zeros((1, 128), F32)
        vbuf[8 + t:9 + t] = jnp.zeros((1, 128), F32)

    spread(zn, mz, at_z, lambda p: vbuf, zv, vz_s, vz_r)
    zv[mz] = vbuf[...]

    def send_rows(g, value):
        ysend[g] = value.reshape(yn, S, C).astype(BF16)
        to_y([near] + far, 0, lambda p: ysend.at[g, p], yrecv.at[g], gy_s.at[g], gy_r.at[g])
        yrecv[g, my] = ysend[g, my]

    def send_z(g):
        from_y([near] + far, 0, lambda p: ysend.at[g, p], yrecv.at[g], gy_s.at[g], gy_r.at[g])
        total = yrecv[g, 0].astype(F32)
        for q in range(1, yn):
            total = total + yrecv[g, q].astype(F32)
        for q in range(zn):
            zsend[g, q] = total[zr * (q // 2):zr * (q // 2) + zr, 128 * (q % 2):128 * (q % 2) + 128].astype(BF16)
        spread(zn, mz, at_z, lambda p: zsend.at[g, p], zrecv.at[g], gz_s.at[g], gz_r.at[g])
        zrecv[g, mz] = zsend[g, mz]

    def send_x(g):
        gathered(zn, mz, at_z, lambda p: zsend.at[g, p], zrecv.at[g], gz_s.at[g], gz_r.at[g])
        total = zrecv[g, 0].astype(F32)
        for q in range(1, zn):
            total = total + zrecv[g, q].astype(F32)
        fsend[g, 0] = total.astype(BF16)
        spread(xn, mx, at_x, lambda p: fsend.at[g, 0], xrecv.at[g], gx_s.at[g], gx_r.at[g])
        xrecv[g, mx] = fsend[g, 0]

    def send_back(g):
        gathered(xn, mx, at_x, lambda p: fsend.at[g, 0], xrecv.at[g], gx_s.at[g], gx_r.at[g])
        total = xrecv[g, 0].astype(F32)
        for q in range(1, xn):
            total = total + xrecv[g, q].astype(F32)
        fsend[g, 1] = total.astype(BF16)
        spread(zn, mz, at_z, lambda p: fsend.at[g, 1], frecv.at[g], gf_s.at[g], gf_r.at[g])
        frecv[g, mz] = fsend[g, 1]

    def whole(g, into):
        gathered(zn, mz, at_z, lambda p: fsend.at[g, 1], frecv.at[g], gf_s.at[g], gf_r.at[g])
        for q in range(zn):
            into[zr * (q // 2):zr * (q // 2) + zr, 128 * (q % 2):128 * (q % 2) + 128] = frecv[g, q].astype(F32)

    send_rows(0, gacc[...])
    gathered(yn, my, at_y, lambda p: sesend, sebuf.at[mc], se_s, se_r)
    relay.start()

    cf[:, 64:72] = rim(H + 2, 1, lambda k: jnp.where(k == 7, 2, -1), lambda k: jnp.where(k == 0, 2, -1))

    @pl.loop(0, (H + 2) // 2)
    def _(i):
        at = pl.ds(pl.multiple_of(i * 2 * PW, 2 * PW), 2 * PW)
        cs[at] = cf[pl.ds(i * 2, 2)].reshape(2 * PW, C).astype(BF16)

    def hidden_grad(pair):
        w_pro = wpbuf[2 * pair:2 * pair + 2].reshape(2 * S, C)

        @pl.loop(0, (H + 2) // GRAD_ROWS)
        def _(i):
            step = GRAD_ROWS * PW
            at = pl.ds(pl.multiple_of(i * step, step), step)
            back = lax.dot_general(cs[at], w_pro, NT_DIMS, preferred_element_type=F32)
            for t in range(3):
                gh[pair * 3 + t, pl.ds(i * GRAD_ROWS, GRAD_ROWS)] = back[:, 128 * t:128 * t + 128].reshape(GRAD_ROWS, PW, 128)

    place = lax.broadcasted_iota(jnp.int32, (PW, 128), 0)
    off_left = jnp.where(left_ok, PW, PW - 1)
    off_right = jnp.where(right_ok, 0, 1)
    inside = jnp.where((place < 64) | ((place == 64) & (off_right == 0)) | ((place == PW - 1) & (off_left == PW)), 1.0, 0.0)

    def depth_back(pair):
        @pl.loop(0, 3)
        def _(t3):
            t = pair * 3 + t3
            taps = [ktile[t, k:k + 1] for k in range(9)]

            @pl.loop(0, H + 2, unroll=2)
            def _(i):
                keep = jnp.where(((i > 0) | top_ok) & ((i < H + 1) | low_ok), 1.0, 0.0)
                slope = s2[t, i] * (inside * keep)
                s2[t, i] = slope
                gh[t, i] = gh[t, i] * slope

            @pl.loop(0, H, unroll=UNROLL)
            def _(i):
                first_slope = s1[t, i + 2, 0:64]
                for source, into in ((gh, ca), (s2, cb)):
                    rows = [source[t, i + r] for r in range(3)]
                    parts = [taps[c] * rows[2] + taps[3 + c] * rows[1] + taps[6 + c] * rows[0] for c in range(3)]
                    grad = parts[1] + pltpu.roll(parts[0], PW - 1, 0) + pltpu.roll(parts[2], 1, 0)
                    into[t, i] = grad[0:64] * first_slope

    for pair in range(pairs):
        hidden_grad(pair)
    gathered(zn, mz, at_z, lambda p: vbuf, zv, vz_s, vz_r)
    xv[mx] = jnp.sum(zv[...], axis=0)
    spread(xn, mx, at_x, lambda p: xv.at[mx], xv, vx_s, vx_r)
    depth_back(0)
    gathered(xn, mx, at_x, lambda p: xv.at[mx], xv, vx_s, vx_r)
    cv[ch] = jnp.sum(xv[...], axis=0)
    spread(ch_n, ch, at_ch, lambda p: cv.at[ch], cv, vc_s, vc_r)
    send_z(0)
    for pair in range(1, pairs):
        depth_back(pair)
    gathered(ch_n, ch, at_ch, lambda p: cv.at[ch], cv, vc_s, vc_r)
    relayed.wait()

    area = float(rows_n * H * yn * 2 * W)
    pooled, gate_grad, weights = [], [], []
    for core in (0, 1):
        total = cv[core]
        for q in range(1, yn):
            total = total + cv[2 * q + core]
        pooled.append(jnp.concatenate([total[t:t + 1] for t in range(nt)], axis=1) * (1.0 / area))
        gate_grad.append(jnp.concatenate([total[8 + t:9 + t] for t in range(nt)], axis=1))
        weights.append(sebuf[core].reshape(ce, 128))
    half = lax.broadcasted_iota(jnp.int32, (1, 128), 1) < 64

    def down(vectors):
        total = jnp.zeros((1, 128), F32)
        for core in (0, 1):
            total = total + jnp.sum(jnp.dot(split3(vectors[core]), weights[core], preferred_element_type=F32), axis=0, keepdims=True)
        return total

    def up(vector, core):
        return jnp.sum(lax.dot_general(split3(vector), weights[core], NT_DIMS, preferred_element_type=F32), axis=0, keepdims=True)

    squeeze_pre = jnp.where(half, down(pooled), 0.0)
    squeeze_sig = sigm(squeeze_pre)
    squeeze_act = squeeze_pre * squeeze_sig
    shifted = pltpu.roll(jnp.broadcast_to(squeeze_act, (8, 128)), 64, 1)[0:1]
    gates = [sigm(up(shifted, core)) for core in (0, 1)]
    excite = [gate_grad[core] * gates[core] * (1.0 - gates[core]) for core in (0, 1)]
    back = pltpu.roll(jnp.broadcast_to(down(excite), (8, 128)), 64, 1)[0:1]
    squeeze_slope = squeeze_sig * (1.0 + squeeze_pre * (1.0 - squeeze_sig))
    grad_squeeze = jnp.where(half, back * squeeze_slope, 0.0)

    def own(values):
        return jnp.where(mc == 0, values[0], values[1])

    gate = own(gates)
    grad_pool = own([up(grad_squeeze, core) for core in (0, 1)]) * (1.0 / area)
    for t in range(nt):
        gs[0, t:t + 1] = gate[:, 128 * t:128 * t + 128]
        gs[1, t:t + 1] = grad_pool[:, 128 * t:128 * t + 128]
    send_x(0)

    def shard_of(rows):
        part = rows[:, 0:S]
        for q in range(1, yn):
            part = jnp.where(my == q, rows[:, S * q:S * q + S], part)
        return part

    def project(source, k, w_all, into):
        def part(where):
            rows = source[:, where].reshape(H * W, ce)
            return jnp.dot(rows, w_all, preferred_element_type=F32).reshape(H, W, C)

        posend[k] = part(other).astype(BF16)
        copy(posend.at[k], porecv.at[k], po_s.at[k], po_r.at[k], sib).start()
        into[...] = part(mine)

    def projected(k, base, total, into):
        copy(posend.at[k], porecv.at[k], po_s.at[k], po_r.at[k], sib).wait()
        into[0] = (base[...].astype(F32) + (total[...] + porecv[k].astype(F32))).astype(BF16)

    x_flat = xnat[...].reshape(H * 64, C)
    for b in range(pairs):
        pair = lax.rem(pair_mine + 1 + b, pairs)

        @pl.loop(0, 3)
        def _(t3):
            t = pair * 3 + t3
            lanes = pl.ds(pl.multiple_of(t * 128, 128), 128)
            gate_t = gs[0, pl.ds(t, 1)]
            pool_t = gs[1, pl.ds(t, 1)]

            @pl.loop(0, H, unroll=UNROLL)
            def _(i):
                ge[i, :, lanes] = (ca[t, i] * gate_t + cb[t, i] * pool_t).astype(BF16)

        lanes3 = pl.ds(pl.multiple_of(pair * 384, 384), 384)
        rows = lax.dot_general(ge[:, :, lanes3].reshape(H * 64, 384), x_flat, TN_DIMS, preferred_element_type=F32)
        ysend[1, pl.ds(pair * 2, 2)] = rows.reshape(2, S, C).astype(BF16)
        if b < pairs - 1:
            to_y(far, 1, lambda p: ysend.at[1, p], yrecv.at[1], gy_s.at[1], gy_r.at[1])
        else:
            to_y([near], 0, lambda p: ysend.at[1, p], yrecv.at[1], gy_s.at[1], gy_r.at[1])
            yrecv[1, my] = ysend[1, my]

    project(ge, 1, webuf[...].reshape(ce, C), cf.at[0:H, 0:W])
    send_back(0)

    @pl.loop(0, nt)
    def _(t):
        gate_t = gs[0, pl.ds(t, 1)]
        pool_t = gs[1, pl.ds(t, 1)]

        def center(i, sums):
            grad = gh[t, i + 1, 0:64] * gate_t + s2[t, i + 1, 0:64] * pool_t
            here = jnp.concatenate([grad, jnp.zeros((8, 128), F32)], axis=0)
            moved = [pltpu.roll(here, PW - 1, 0), here, pltpu.roll(here, 1, 0)]
            fresh = []
            for r in range(3):
                act = a1[t, i + 1 + r]
                for c in range(3):
                    fresh.append(sums[3 * r + c] + jnp.sum((moved[c] * act).reshape(9, 8, 128), axis=0))
            return tuple(fresh)

        sums = lax.fori_loop(0, H, center, (jnp.zeros((8, 128), F32),) * 9, unroll=UNROLL)
        dkacc[t] = jnp.concatenate(
            [jnp.sum(part, axis=0, keepdims=True) for part in sums] + [jnp.zeros((7, 128), F32)], axis=0)

    dksend[...] = jnp.concatenate([dkacc[t] for t in range(nt)], axis=1).astype(BF16)
    spread(yn, my, at_y, lambda p: dksend, dkyr, ky_s, ky_r)
    dkyr[my] = dksend[...]
    send_z(1)

    @pl.loop(0, H)
    def _(i):
        act2[i] = (act2[i].astype(F32) * gate).astype(BF16)

    project(act2, 0, wpbuf[...].reshape(ce, C), xf.at[0:H, 0:W])

    def summed(parts):
        total = parts[0].astype(F32)
        for q in range(1, parts.shape[0]):
            total = total + parts[q].astype(F32)
        return total

    gathered(yn, my, at_y, lambda p: dksend, dkyr, ky_s, ky_r)
    dkzs[...] = jnp.concatenate([shard_of(summed(dkyr)), jnp.zeros((16, 256 - S), F32)], axis=1).astype(BF16)
    spread(zn, mz, at_z, lambda p: dkzs, dkzr, kz_s, kz_r)
    dkzr[mz] = dkzs[...]
    send_x(1)
    projected(1, c_ref, cf.at[0:H, 0:W], din_ref)
    gathered(zn, mz, at_z, lambda p: dkzs, dkzr, kz_s, kz_r)
    dkxs[...] = summed(dkzr).astype(BF16)
    spread(xn, mx, at_x, lambda p: dkxs, dkxr, kx_s, kx_r)
    dkxr[mx] = dkxs[...]
    send_back(1)

    own_gate = shard_of(gate)
    lefts, rights = pairs3(grad_squeeze * scale, shard_of(own(pooled)))
    dse1_ref[...] = lax.dot_general(lefts, rights, TN_DIMS, preferred_element_type=F32)[0:64]
    lefts, rights = pairs3(squeeze_act, shard_of(own(excite)) * scale)
    dse2_ref[...] = lax.dot_general(lefts, rights, TN_DIMS, preferred_element_type=F32)[0:64]
    gate_wide = lax.dot_general(split3(own_gate * scale), ones, TN_DIMS, preferred_element_type=F32)
    projected(0, x_ref, xf.at[0:H, 0:W], out_ref)
    whole(0, gacc.at[0:S])
    dwp_ref[...] = gacc[0:S] * gate_wide
    gathered(xn, mx, at_x, lambda p: dkxs, dkxr, kx_s, kx_r)
    dk_ref[...] = summed(dkxr)[0:9, 0:S] * scale
    whole(1, gacc.at[S:2 * S])
    dwe_ref[...] = gacc[S:2 * S] * scale


def settle(*refs):
    count = (len(refs) - 1) // 2
    moves = [pltpu.make_async_copy(refs[k], refs[count + k], refs[-1].at[k]) for k in range(count)]
    for move in moves:
        move.start()
    for move in moves:
        move.wait()


def per_device(inputs, w_expand, kernel, w_se1, w_se2, w_project, cotangent):
    rows_n, ch_n = lax.axis_size("rows"), lax.axis_size("ch")
    zn = CHIPS_Z if rows_n % CHIPS_Z == 0 else 2
    xn, yn = rows_n // zn, ch_n // 2
    ce = S * yn
    nt = ce // 128
    zr = S // (zn // 2)
    grad_scale = 1.0 / math.sqrt(rows_n * H * ch_n * W)
    vmem, dma = pltpu.VMEM, pltpu.SemaphoreType.DMA
    scratch = [
        vmem((H, W, C), BF16), vmem((S, C), BF16), vmem((9, S), BF16), vmem((64, S), BF16), vmem((64, S), BF16),
        vmem((S, C), BF16), vmem((H, W, C), BF16),
        vmem((H, W, C), BF16), vmem((H, W, C), BF16),
        vmem((2, 3 * W, C), BF16), vmem((2, 2, 3 * W, C), BF16),
        vmem((3 * H, C), BF16), vmem((2, 3, 3 * H, C), BF16),
        vmem((yn, S, C), BF16), vmem((yn, S, C), BF16),
        vmem((S, 128), BF16), vmem((2, yn, S, 128), BF16),
        vmem((16, 256), BF16), vmem((yn, 16, 256), BF16),
        vmem((H + 4, PW, C), F32), vmem((H + 2, PW, C), F32),
        vmem(((H + 4) * PW, C), BF16), vmem(((H + 2) * PW, C), BF16),
        vmem((H, 64, C), BF16), vmem((H, 64, C), BF16),
        vmem((nt, H + 4, PW, 128), F32), vmem((nt, H + 4, PW, 128), F32),
        vmem((nt, H + 2, PW, 128), F32), vmem((nt, H + 2, PW, 128), F32),
        vmem((nt, H, 64, 128), F32), vmem((nt, H, 64, 128), F32),
        vmem((H, 64, ce), BF16), vmem((H, 64, ce), BF16),
        vmem((nt, 16, 128), F32), vmem((ce, C), F32), vmem((nt, 16, 128), F32),
        vmem((16, 128), F32), vmem((zn, 16, 128), F32), vmem((xn, 16, 128), F32), vmem((ch_n, 16, 128), F32),
        vmem((2, 8, 128), F32),
        vmem((2, yn, S, C), BF16), vmem((2, yn, S, C), BF16),
        vmem((2, zn, zr, 128), BF16), vmem((2, zn, zr, 128), BF16),
        vmem((2, xn, zr, 128), BF16), vmem((2, 2, zr, 128), BF16), vmem((2, zn, zr, 128), BF16),
        vmem((16, ce), BF16), vmem((yn, 16, ce), BF16),
        vmem((zn, 16, 256), BF16), vmem((16, 256), BF16), vmem((xn, 16, 256), BF16), vmem((16, 256), BF16),
        vmem((2, H, W, C), BF16), vmem((2, H, W, C), BF16),
        dma((7,)), dma((2,)), dma((2,)), dma((2, 2)), dma((2, 2)), dma((3, 2)), dma((2, 3)),
        dma((yn,)), dma((yn,)), dma((yn,)), dma((yn,)),
        dma((yn,)), dma((yn,)), dma((1,)), dma((2,)), dma((yn,)), dma((yn,)),
        dma((zn,)), dma((zn,)), dma((xn,)), dma((xn,)), dma((ch_n,)), dma((ch_n,)),
        dma((2, yn)), dma((2, yn)), dma((2, zn)), dma((2, zn)), dma((2, xn)), dma((2, xn)), dma((2, zn)), dma((2, zn)),
        dma((yn,)), dma((yn,)), dma((zn,)), dma((zn,)), dma((xn,)), dma((xn,)),
        dma((2,)), dma((2,)),
    ]
    anywhere = pl.BlockSpec(memory_space=pl.ANY)
    in_vmem = pl.BlockSpec(memory_space=pltpu.VMEM)
    shapes = (
        jax.ShapeDtypeStruct((1, H, W, C), BF16), jax.ShapeDtypeStruct((1, H, W, C), BF16),
        jax.ShapeDtypeStruct((S, C), F32), jax.ShapeDtypeStruct((9, S), F32),
        jax.ShapeDtypeStruct((64, S), F32), jax.ShapeDtypeStruct((64, S), F32),
        jax.ShapeDtypeStruct((S, C), F32))
    results = pl.pallas_call(
        functools.partial(fused, rows_n, ch_n, grad_scale),
        out_shape=shapes,
        in_specs=[anywhere] * 7,
        out_specs=(in_vmem,) * 7,
        scratch_shapes=scratch,
        compiler_params=pltpu.CompilerParams(
            collective_id=0, has_side_effects=True, vmem_limit_bytes=56 * 1024 * 1024),
    )(inputs, w_expand.T, kernel, w_se1.T, w_se2, w_project, cotangent)
    output, d_input, d_expand_t, d_taps, d_se1_t, d_se2, d_project = pl.pallas_call(
        settle,
        out_shape=shapes,
        in_specs=[anywhere] * 7,
        out_specs=(in_vmem,) * 7,
        scratch_shapes=[dma((7,))],
    )(*results)
    return output, d_input, d_expand_t.T, d_taps, d_se1_t.T, d_se2, d_project


def solution(mesh):
    return jax.shard_map(
        per_device,
        mesh=mesh,
        in_specs=(
            P(None, "rows", "ch", None),
            P(None, "ch"),
            P(None, "ch"),
            P("ch", None),
            P(None, "ch"),
            P("ch", None),
            P(None, "rows", "ch", None),
        ),
        out_specs=(
            P(None, "rows", "ch", None),
            P(None, "rows", "ch", None),
            P(None, "ch"),
            P(None, "ch"),
            P("ch", None),
            P(None, "ch"),
            P("ch", None),
        ),
        check_vma=False,
    )
```

```python
import functools
import math

import jax
import jax.numpy as jnp
from jax import lax
from jax.experimental import pallas as pl
from jax.experimental.pallas import tpu as pltpu
from jax.sharding import PartitionSpec as P

MESH = pl.DeviceIdType.MESH
F32 = jnp.float32
BF16 = jnp.bfloat16

CHIPS_Z = 8
H = 16
W = 32
C = 256
S = 192
PW = 72
EXPAND_ROWS = 10
GRAD_ROWS = 18
UNROLL = 8
NT_DIMS = (((1,), (1,)), ((), ()))
TN_DIMS = (((0,), (0,)), ((), ()))


def split3(row):
    hi = row.astype(BF16).astype(F32)
    mid = (row - hi).astype(BF16).astype(F32)
    low = row - hi - mid
    rest = jnp.zeros((5, row.shape[1]), F32)
    return jnp.concatenate([hi, mid, low, rest], axis=0).astype(BF16)


def sigm(v):
    return 0.5 * jnp.tanh(0.5 * v) + 0.5


def pairs3(left, right):
    def three(row):
        hi = row.astype(BF16).astype(F32)
        mid = (row - hi).astype(BF16).astype(F32)
        return hi, mid, row - hi - mid

    a, b = three(left), three(right)
    lefts = jnp.concatenate([a[k] for k in (0, 0, 1, 1, 0, 2, 1, 2)], axis=0).astype(BF16)
    rights = jnp.concatenate([b[k] for k in (0, 1, 0, 1, 2, 0, 2, 1)], axis=0).astype(BF16)
    return lefts, rights


def fused(rows_n, ch_n, scale, x_in, we_in, tap_in, se1_in, se2_in, wp_in, c_in,
          out_ref, din_ref, dwe_ref, dk_ref, dse1_ref, dse2_ref, dwp_ref,
          x_ref, we_ref, tap_ref, se1_ref, se2_ref, wp_ref, c_ref, xsib, csib, rowsend, rowbuf, colsend, colbuf, webuf, wpbuf, sesend, sebuf, tapsend, tapbuf,
          xf, cf, xs, cs, xnat, cnat, a1, s1, gh, s2, ca, cb, act2, ge, ktile, gacc, dkacc,
          vbuf, zv, xv, cv, gs, ysend, yrecv, zsend, zrecv, xrecv, fsend, frecv,
          dksend, dkyr, dkzr, dkxs, dkxr, dkzs, posend, porecv,
          load_s, sib_s, sib_r, row_s, row_r, col_s, col_r, we_s, we_r, wp_s, wp_r, se_s, se_r, rel_s, rel_r, tap_s, tap_r,
          vz_s, vz_r, vx_s, vx_r, vc_s, vc_r, gy_s, gy_r, gz_s, gz_r, gx_s, gx_r, gf_s, gf_r,
          ky_s, ky_r, kz_s, kz_r, kx_s, kx_r, po_s, po_r):
    zn = CHIPS_Z if rows_n % CHIPS_Z == 0 else 2
    xn = rows_n // zn
    yn = ch_n // 2
    ce = S * yn
    nt = ce // 128
    pairs = yn // 2
    zr = S // (zn // 2)
    row = lax.axis_index("rows")
    ch = lax.axis_index("ch")
    mx, mz = row // zn, lax.rem(row, zn)
    my, mc = ch // 2, lax.rem(ch, 2)
    oc = 1 - mc

    def dev_row(step):
        return lax.rem(row + step + rows_n, rows_n)

    def dev_y(step):
        return lax.rem(my + step + yn, yn)

    def copy(src, dst, ssem, rsem, where):
        return pltpu.make_async_remote_copy(
            src_ref=src, dst_ref=dst, send_sem=ssem, recv_sem=rsem, device_id=where, device_id_type=MESH)

    def at_y(peer):
        return (row, peer * 2 + mc)

    def at_z(peer):
        return (mx * zn + peer, ch)

    def at_x(peer):
        return (peer * zn + mz, ch)

    def at_ch(peer):
        return (row, peer)

    def spread(n, me, at, src, land, ssem, rsem):
        for step in range(1, n):
            peer = lax.rem(me + step, n)
            copy(src(peer), land.at[me], ssem.at[step - 1], rsem.at[me], at(peer)).start()

    def gathered(n, me, at, src, land, ssem, rsem):
        for step in range(1, n):
            peer = lax.rem(me + step, n)
            copy(src(peer), land.at[peer], ssem.at[step - 1], rsem.at[peer], at(peer)).wait()

    pair_mine = my // 2
    near = my + 1 - 2 * lax.rem(my, 2)
    far = [lax.rem(pair_mine + b, pairs) * 2 + k for b in range(1, pairs) for k in (0, 1)]

    def to_y(peers, first, src, land, ssem, rsem):
        for k, peer in enumerate(peers):
            copy(src(peer), land.at[my], ssem.at[first + k], rsem.at[my], at_y(peer)).start()

    def from_y(peers, first, src, land, ssem, rsem):
        for k, peer in enumerate(peers):
            copy(src(peer), land.at[peer], ssem.at[first + k], rsem.at[peer], at_y(peer)).wait()

    barrier = pltpu.get_barrier_semaphore()
    partners = [at_ch(lax.rem(ch + s, ch_n)) for s in range(1, ch_n)]
    partners += [at_z(lax.rem(mz + s, zn)) for s in range(1, zn)]
    partners += [at_x(lax.rem(mx + s, xn)) for s in range(1, xn)]
    partners += [(dev_row(dr), my * 2 + core) for dr in (-1, 1) for core in (0, 1)]
    partners += [(dev_row(dr), dev_y(dy) * 2 + core) for dr in (-1, 0, 1) for dy in (-1, 1) for core in (0, 1)]
    for where in partners:
        pl.semaphore_signal(barrier, inc=1, device_id=where, device_id_type=MESH)

    arrays = ((x_in.at[0], x_ref), (c_in.at[0], c_ref), (we_in, we_ref), (tap_in, tap_ref), (se1_in, se1_ref),
              (se2_in, se2_ref), (wp_in, wp_ref))
    loads = [pltpu.make_async_copy(source, into, load_s.at[k]) for k, (source, into) in enumerate(arrays)]
    for load in loads:
        load.start()
    for load in loads:
        load.wait()

    for d, (lo, edge) in enumerate(((0, 0), (H - 2, H - 1))):
        rowsend[d, 0:2 * W] = x_ref[lo:lo + 2].reshape(2 * W, C)
        rowsend[d, 2 * W:3 * W] = c_ref[edge]
    first = mc * (W - 2)
    ri = lax.broadcasted_iota(jnp.int32, (2 * H, H * W), 0)
    ci = lax.broadcasted_iota(jnp.int32, (2 * H, H * W), 1)
    pick = (ci == (ri & (H - 1)) * W + first + (ri >> 4)).astype(F32).astype(BF16)
    colsend[0:2 * H] = jnp.dot(pick, x_ref[...].reshape(H * W, C), preferred_element_type=F32).astype(BF16)
    ri = lax.broadcasted_iota(jnp.int32, (H, H * W), 0)
    ci = lax.broadcasted_iota(jnp.int32, (H, H * W), 1)
    pick = (ci == ri * W + mc * (W - 1)).astype(F32).astype(BF16)
    colsend[2 * H:3 * H] = jnp.dot(pick, c_ref[...].reshape(H * W, C), preferred_element_type=F32).astype(BF16)

    eye = (lax.broadcasted_iota(jnp.int32, (S, S), 0) == lax.broadcasted_iota(jnp.int32, (S, S), 1)).astype(F32).astype(BF16)
    se_t = jnp.concatenate([se1_ref[...], se2_ref[...]], axis=0)
    sesend[...] = lax.dot_general(eye, se_t, NT_DIMS, preferred_element_type=F32).astype(BF16)
    tap_rows = jnp.concatenate([tap_ref[...].astype(F32), jnp.zeros((7, S), F32)], axis=0)
    tapsend[...] = jnp.concatenate([tap_rows, jnp.zeros((16, 256 - S), F32)], axis=1).astype(BF16)

    pl.semaphore_wait(barrier, len(partners))

    sib = (row, my * 2 + oc)
    sib_copies = [copy(x_ref, xsib, sib_s.at[0], sib_r.at[0], sib), copy(c_ref, csib, sib_s.at[1], sib_r.at[1], sib)]
    row_copies = []
    for d, dr in ((0, -1), (1, 1)):
        for core in (0, 1):
            row_copies.append((copy(rowsend.at[d], rowbuf.at[1 - d, mc], row_s.at[d, core], row_r.at[1 - d, mc],
                                    (dev_row(dr), my * 2 + core)),
                               copy(rowsend.at[d], rowbuf.at[1 - d, core], row_s.at[d, core], row_r.at[1 - d, core],
                                    (dev_row(dr), my * 2 + core))))
    col_copies = []
    side = 1 - mc
    for i, dr in enumerate((-1, 0, 1)):
        for core in (0, 1):
            where = (dev_row(dr), dev_y(2 * mc - 1) * 2 + core)
            col_copies.append((copy(colsend, colbuf.at[side, 2 - i], col_s.at[i, core], col_r.at[side, 2 - i], where),
                               copy(colsend, colbuf.at[core, i], col_s.at[i, core], col_r.at[core, i], where)))
    sib_copies[0].start()
    for sent, _ in row_copies + col_copies:
        sent.start()
    to_y([near], 0, lambda p: we_ref, webuf, we_s, we_r)
    spread(yn, my, at_y, lambda p: tapsend, tapbuf, tap_s, tap_r)
    sib_copies[1].start()
    to_y(far, 1, lambda p: we_ref, webuf, we_s, we_r)
    to_y([near] + far, 0, lambda p: wp_ref, wpbuf, wp_s, wp_r)
    spread(yn, my, at_y, lambda p: sesend, sebuf.at[mc], se_s, se_r)
    relay = copy(sebuf.at[mc], sebuf.at[mc], rel_s.at[0], rel_r.at[mc], sib)
    relayed = copy(sebuf.at[mc], sebuf.at[oc], rel_s.at[0], rel_r.at[oc], sib)

    webuf[my] = we_ref[...]
    wpbuf[my] = wp_ref[...]
    tapbuf[my] = tapsend[...]
    sebuf[mc, my] = sesend[...]
    mine = pl.ds(pl.multiple_of(mc * W, W), W)
    other = pl.ds(pl.multiple_of(oc * W, W), W)
    xf[2:2 + H, mine] = x_ref[...].astype(F32)
    cf[1:1 + H, mine] = c_ref[...].astype(F32)
    xnat[:, mine] = x_ref[...]
    cnat[:, mine] = c_ref[...]
    sib_copies[0].wait()
    xf[2:2 + H, other] = xsib[...].astype(F32)
    xnat[:, other] = xsib[...]
    for _, landed in row_copies + col_copies:
        landed.wait()

    top_ok = row > 0
    low_ok = row < rows_n - 1
    left_ok = my > 0
    right_ok = my < yn - 1
    for d, ok in ((0, top_ok), (1, low_ok)):
        for core in (0, 1):
            part = rowbuf[d, core].astype(F32) * jnp.where(ok, 1.0, 0.0)
            xf[(2 + H) * d:(2 + H) * d + 2, W * core:W * core + W] = part[0:2 * W].reshape(2, W, C)
            cf[(1 + H) * d, W * core:W * core + W] = part[2 * W:3 * W]
    cols = colbuf[...].reshape(2 * 3 * 48, C)

    def rim(height, above, left_slot, right_slot):
        shape = (height * 8, 288)
        out_row = lax.broadcasted_iota(jnp.int32, shape, 0)
        src = lax.broadcasted_iota(jnp.int32, shape, 1)
        place = out_row & 7
        at_row = (out_row >> 3) - above
        third = jnp.where(at_row < 0, 0, jnp.where(at_row < H, 1, 2))
        ok = jnp.where(at_row < 0, top_ok.astype(jnp.int32), jnp.where(at_row < H, 1, low_ok.astype(jnp.int32)))
        want = third * 48 + (at_row & (H - 1))
        right_of = jnp.where(place < 4, 1, 0)
        slot = jnp.where(place < 4, right_slot(place), left_slot(place))
        ok = ok * jnp.where(slot < 0, 0, 1) * jnp.where(place < 4, right_ok.astype(jnp.int32), left_ok.astype(jnp.int32))
        want = want + right_of * 144 + slot * 16
        hit = jnp.where(src == want, ok, 0).astype(F32).astype(BF16)
        return jnp.dot(hit, cols, preferred_element_type=F32).reshape(height, 8, C)

    xf[:, 64:72] = rim(H + 4, 2, lambda k: jnp.where(k >= 6, k - 6, -1), lambda k: jnp.where(k < 2, k, -1))

    @pl.loop(0, (H + 4) // 2)
    def _(i):
        at = pl.ds(pl.multiple_of(i * 2 * PW, 2 * PW), 2 * PW)
        xs[at] = xf[pl.ds(i * 2, 2)].reshape(2 * PW, C).astype(BF16)

    gathered(yn, my, at_y, lambda p: tapsend, tapbuf, tap_s, tap_r)
    wide = jnp.concatenate([tapbuf[q].astype(F32)[:, 0:S] for q in range(yn)], axis=1)
    for t in range(nt):
        ktile[t] = wide[:, 128 * t:128 * t + 128]
    from_y([near], 0, lambda p: we_ref, webuf, we_s, we_r)

    for b in range(pairs):
        pair = lax.rem(pair_mine + b, pairs)
        if b == 1:
            from_y(far, 1, lambda p: we_ref, webuf, we_s, we_r)
        w_exp = webuf[pl.ds(pair * 2, 2)].reshape(2 * S, C)

        @pl.loop(0, (H + 4) // EXPAND_ROWS)
        def _(i):
            step = EXPAND_ROWS * PW
            at = pl.ds(pl.multiple_of(i * step, step), step)
            pre = lax.dot_general(xs[at], w_exp, NT_DIMS, preferred_element_type=F32)
            sig = sigm(pre)
            act = pre * sig
            slope = sig * (1.0 + (pre - act))
            for t in range(3):
                there = pl.ds(i * EXPAND_ROWS, EXPAND_ROWS)
                a1[pair * 3 + t, there] = act[:, 128 * t:128 * t + 128].reshape(EXPAND_ROWS, PW, 128)
                s1[pair * 3 + t, there] = slope[:, 128 * t:128 * t + 128].reshape(EXPAND_ROWS, PW, 128)

        @pl.loop(0, 3)
        def _(t3):
            t = pair * 3 + t3
            lanes = pl.ds(pl.multiple_of(t * 128, 128), 128)
            taps = [ktile[t, k:k + 1] for k in range(9)]

            def one_row(i):
                rows = [a1[t, i + r] for r in range(3)]
                parts = [taps[c] * rows[0] + taps[3 + c] * rows[1] + taps[6 + c] * rows[2] for c in range(3)]
                pre = parts[1] + pltpu.roll(parts[0], 1, 0) + pltpu.roll(parts[2], PW - 1, 0)
                sig = sigm(pre)
                act = pre * sig
                s2[t, i] = sig * (1.0 + (pre - act))
                return act[0:64]

            def center(i, pool):
                act = one_row(i)
                act2[i - 1, :, lanes] = act.astype(BF16)
                return pool + jnp.sum(act.reshape(8, 8, 128), axis=0)

            one_row(0)
            one_row(H + 1)
            pool = lax.fori_loop(1, H + 1, center, jnp.zeros((8, 128), F32), unroll=UNROLL)
            vbuf[pl.ds(t, 1)] = jnp.sum(pool, axis=0, keepdims=True)

    sib_copies[1].wait()
    cf[1:1 + H, other] = csib[...].astype(F32)
    cnat[:, other] = csib[...]
    cot_flat = cnat[...].reshape(H * 64, C)
    from_y([near] + far, 0, lambda p: wp_ref, wpbuf, wp_s, wp_r)
    ones = jnp.ones((8, C), F32).astype(BF16)
    for t in range(ce // 384):
        rows = lax.dot_general(
            act2[:, :, 384 * t:384 * t + 384].reshape(H * 64, 384), cot_flat, TN_DIMS, preferred_element_type=F32)
        gacc[384 * t:384 * t + 384] = rows
        prod = rows * wpbuf[2 * t:2 * t + 2].reshape(384, C).astype(F32)
        hi = prod.astype(BF16)
        rest = prod - hi.astype(F32)
        mid = rest.astype(BF16)
        low = (rest - mid.astype(F32)).astype(BF16)
        gate_sum = sum(lax.dot_general(ones, part, NT_DIMS, preferred_element_type=F32) for part in (hi, mid, low))
        for k in range(3):
            vbuf[8 + 3 * t + k:9 + 3 * t + k] = gate_sum[0:1, 128 * k:128 * k + 128]

    for t in range(nt, 8):
        vbuf[t:t + 1] = jnp.zeros((1, 128), F32)
        vbuf[8 + t:9 + t] = jnp.zeros((1, 128), F32)

    spread(zn, mz, at_z, lambda p: vbuf, zv, vz_s, vz_r)
    zv[mz] = vbuf[...]

    def send_rows(g, value):
        ysend[g] = value.reshape(yn, S, C).astype(BF16)
        to_y([near] + far, 0, lambda p: ysend.at[g, p], yrecv.at[g], gy_s.at[g], gy_r.at[g])
        yrecv[g, my] = ysend[g, my]

    def send_z(g):
        from_y([near] + far, 0, lambda p: ysend.at[g, p], yrecv.at[g], gy_s.at[g], gy_r.at[g])
        total = yrecv[g, 0].astype(F32)
        for q in range(1, yn):
            total = total + yrecv[g, q].astype(F32)
        for q in range(zn):
            zsend[g, q] = total[zr * (q // 2):zr * (q // 2) + zr, 128 * (q % 2):128 * (q % 2) + 128].astype(BF16)
        spread(zn, mz, at_z, lambda p: zsend.at[g, p], zrecv.at[g], gz_s.at[g], gz_r.at[g])
        zrecv[g, mz] = zsend[g, mz]

    def send_x(g):
        gathered(zn, mz, at_z, lambda p: zsend.at[g, p], zrecv.at[g], gz_s.at[g], gz_r.at[g])
        total = zrecv[g, 0].astype(F32)
        for q in range(1, zn):
            total = total + zrecv[g, q].astype(F32)
        fsend[g, 0] = total.astype(BF16)
        spread(xn, mx, at_x, lambda p: fsend.at[g, 0], xrecv.at[g], gx_s.at[g], gx_r.at[g])
        xrecv[g, mx] = fsend[g, 0]

    def send_back(g):
        gathered(xn, mx, at_x, lambda p: fsend.at[g, 0], xrecv.at[g], gx_s.at[g], gx_r.at[g])
        total = xrecv[g, 0].astype(F32)
        for q in range(1, xn):
            total = total + xrecv[g, q].astype(F32)
        fsend[g, 1] = total.astype(BF16)
        spread(zn, mz, at_z, lambda p: fsend.at[g, 1], frecv.at[g], gf_s.at[g], gf_r.at[g])
        frecv[g, mz] = fsend[g, 1]

    def whole(g, into):
        gathered(zn, mz, at_z, lambda p: fsend.at[g, 1], frecv.at[g], gf_s.at[g], gf_r.at[g])
        for q in range(zn):
            into[zr * (q // 2):zr * (q // 2) + zr, 128 * (q % 2):128 * (q % 2) + 128] = frecv[g, q].astype(F32)

    send_rows(0, gacc[...])
    gathered(yn, my, at_y, lambda p: sesend, sebuf.at[mc], se_s, se_r)
    relay.start()

    cf[:, 64:72] = rim(H + 2, 1, lambda k: jnp.where(k == 7, 2, -1), lambda k: jnp.where(k == 0, 2, -1))

    @pl.loop(0, (H + 2) // 2)
    def _(i):
        at = pl.ds(pl.multiple_of(i * 2 * PW, 2 * PW), 2 * PW)
        cs[at] = cf[pl.ds(i * 2, 2)].reshape(2 * PW, C).astype(BF16)

    def hidden_grad(pair):
        w_pro = wpbuf[2 * pair:2 * pair + 2].reshape(2 * S, C)

        @pl.loop(0, (H + 2) // GRAD_ROWS)
        def _(i):
            step = GRAD_ROWS * PW
            at = pl.ds(pl.multiple_of(i * step, step), step)
            back = lax.dot_general(cs[at], w_pro, NT_DIMS, preferred_element_type=F32)
            for t in range(3):
                gh[pair * 3 + t, pl.ds(i * GRAD_ROWS, GRAD_ROWS)] = back[:, 128 * t:128 * t + 128].reshape(GRAD_ROWS, PW, 128)

    place = lax.broadcasted_iota(jnp.int32, (PW, 128), 0)
    off_left = jnp.where(left_ok, PW, PW - 1)
    off_right = jnp.where(right_ok, 0, 1)
    inside = jnp.where((place < 64) | ((place == 64) & (off_right == 0)) | ((place == PW - 1) & (off_left == PW)), 1.0, 0.0)

    def depth_back(pair):
        @pl.loop(0, 3)
        def _(t3):
            t = pair * 3 + t3
            taps = [ktile[t, k:k + 1] for k in range(9)]

            @pl.loop(0, H + 2, unroll=2)
            def _(i):
                keep = jnp.where(((i > 0) | top_ok) & ((i < H + 1) | low_ok), 1.0, 0.0)
                slope = s2[t, i] * (inside * keep)
                s2[t, i] = slope
                gh[t, i] = gh[t, i] * slope

            @pl.loop(0, H, unroll=UNROLL)
            def _(i):
                first_slope = s1[t, i + 2, 0:64]
                for source, into in ((gh, ca), (s2, cb)):
                    rows = [source[t, i + r] for r in range(3)]
                    parts = [taps[c] * rows[2] + taps[3 + c] * rows[1] + taps[6 + c] * rows[0] for c in range(3)]
                    grad = parts[1] + pltpu.roll(parts[0], PW - 1, 0) + pltpu.roll(parts[2], 1, 0)
                    into[t, i] = grad[0:64] * first_slope

    for pair in range(pairs):
        hidden_grad(pair)
    gathered(zn, mz, at_z, lambda p: vbuf, zv, vz_s, vz_r)
    xv[mx] = jnp.sum(zv[...], axis=0)
    spread(xn, mx, at_x, lambda p: xv.at[mx], xv, vx_s, vx_r)
    depth_back(0)
    gathered(xn, mx, at_x, lambda p: xv.at[mx], xv, vx_s, vx_r)
    cv[ch] = jnp.sum(xv[...], axis=0)
    spread(ch_n, ch, at_ch, lambda p: cv.at[ch], cv, vc_s, vc_r)
    send_z(0)
    for pair in range(1, pairs):
        depth_back(pair)
    gathered(ch_n, ch, at_ch, lambda p: cv.at[ch], cv, vc_s, vc_r)
    relayed.wait()

    area = float(rows_n * H * yn * 2 * W)
    pooled, gate_grad, weights = [], [], []
    for core in (0, 1):
        total = cv[core]
        for q in range(1, yn):
            total = total + cv[2 * q + core]
        pooled.append(jnp.concatenate([total[t:t + 1] for t in range(nt)], axis=1) * (1.0 / area))
        gate_grad.append(jnp.concatenate([total[8 + t:9 + t] for t in range(nt)], axis=1))
        weights.append(sebuf[core].reshape(ce, 128))
    half = lax.broadcasted_iota(jnp.int32, (1, 128), 1) < 64

    def down(vectors):
        total = jnp.zeros((1, 128), F32)
        for core in (0, 1):
            total = total + jnp.sum(jnp.dot(split3(vectors[core]), weights[core], preferred_element_type=F32), axis=0, keepdims=True)
        return total

    def up(vector, core):
        return jnp.sum(lax.dot_general(split3(vector), weights[core], NT_DIMS, preferred_element_type=F32), axis=0, keepdims=True)

    squeeze_pre = jnp.where(half, down(pooled), 0.0)
    squeeze_sig = sigm(squeeze_pre)
    squeeze_act = squeeze_pre * squeeze_sig
    shifted = pltpu.roll(jnp.broadcast_to(squeeze_act, (8, 128)), 64, 1)[0:1]
    gates = [sigm(up(shifted, core)) for core in (0, 1)]
    excite = [gate_grad[core] * gates[core] * (1.0 - gates[core]) for core in (0, 1)]
    back = pltpu.roll(jnp.broadcast_to(down(excite), (8, 128)), 64, 1)[0:1]
    squeeze_slope = squeeze_sig * (1.0 + squeeze_pre * (1.0 - squeeze_sig))
    grad_squeeze = jnp.where(half, back * squeeze_slope, 0.0)

    def own(values):
        return jnp.where(mc == 0, values[0], values[1])

    gate = own(gates)
    grad_pool = own([up(grad_squeeze, core) for core in (0, 1)]) * (1.0 / area)
    for t in range(nt):
        gs[0, t:t + 1] = gate[:, 128 * t:128 * t + 128]
        gs[1, t:t + 1] = grad_pool[:, 128 * t:128 * t + 128]
    send_x(0)

    def shard_of(rows):
        part = rows[:, 0:S]
        for q in range(1, yn):
            part = jnp.where(my == q, rows[:, S * q:S * q + S], part)
        return part

    def project(source, k, w_all, into):
        def part(where):
            rows = source[:, where].reshape(H * W, ce)
            return jnp.dot(rows, w_all, preferred_element_type=F32).reshape(H, W, C)

        posend[k] = part(other).astype(BF16)
        copy(posend.at[k], porecv.at[k], po_s.at[k], po_r.at[k], sib).start()
        into[...] = part(mine)

    def projected(k, base, total, into):
        copy(posend.at[k], porecv.at[k], po_s.at[k], po_r.at[k], sib).wait()
        into[0] = (base[...].astype(F32) + (total[...] + porecv[k].astype(F32))).astype(BF16)

    x_flat = xnat[...].reshape(H * 64, C)
    for b in range(pairs):
        pair = lax.rem(pair_mine + 1 + b, pairs)

        @pl.loop(0, 3)
        def _(t3):
            t = pair * 3 + t3
            lanes = pl.ds(pl.multiple_of(t * 128, 128), 128)
            gate_t = gs[0, pl.ds(t, 1)]
            pool_t = gs[1, pl.ds(t, 1)]

            @pl.loop(0, H, unroll=UNROLL)
            def _(i):
                ge[i, :, lanes] = (ca[t, i] * gate_t + cb[t, i] * pool_t).astype(BF16)

        lanes3 = pl.ds(pl.multiple_of(pair * 384, 384), 384)
        rows = lax.dot_general(ge[:, :, lanes3].reshape(H * 64, 384), x_flat, TN_DIMS, preferred_element_type=F32)
        ysend[1, pl.ds(pair * 2, 2)] = rows.reshape(2, S, C).astype(BF16)
        if b < pairs - 1:
            to_y(far, 1, lambda p: ysend.at[1, p], yrecv.at[1], gy_s.at[1], gy_r.at[1])
        else:
            to_y([near], 0, lambda p: ysend.at[1, p], yrecv.at[1], gy_s.at[1], gy_r.at[1])
            yrecv[1, my] = ysend[1, my]

    project(ge, 1, webuf[...].reshape(ce, C), cf.at[0:H, 0:W])
    @pl.loop(0, nt)
    def _(t):
        gate_t = gs[0, pl.ds(t, 1)]
        pool_t = gs[1, pl.ds(t, 1)]

        def center(i, sums):
            grad = gh[t, i + 1, 0:64] * gate_t + s2[t, i + 1, 0:64] * pool_t
            here = jnp.concatenate([grad, jnp.zeros((8, 128), F32)], axis=0)
            moved = [pltpu.roll(here, PW - 1, 0), here, pltpu.roll(here, 1, 0)]
            fresh = []
            for r in range(3):
                act = a1[t, i + 1 + r]
                for c in range(3):
                    fresh.append(sums[3 * r + c] + jnp.sum((moved[c] * act).reshape(9, 8, 128), axis=0))
            return tuple(fresh)

        sums = lax.fori_loop(0, H, center, (jnp.zeros((8, 128), F32),) * 9, unroll=UNROLL)
        dkacc[t] = jnp.concatenate(
            [jnp.sum(part, axis=0, keepdims=True) for part in sums] + [jnp.zeros((7, 128), F32)], axis=0)

    dksend[...] = jnp.concatenate([dkacc[t] for t in range(nt)], axis=1).astype(BF16)
    spread(yn, my, at_y, lambda p: dksend, dkyr, ky_s, ky_r)
    dkyr[my] = dksend[...]
    send_z(1)

    @pl.loop(0, H)
    def _(i):
        act2[i] = (act2[i].astype(F32) * gate).astype(BF16)

    project(act2, 0, wpbuf[...].reshape(ce, C), xf.at[0:H, 0:W])

    def summed(parts):
        total = parts[0].astype(F32)
        for q in range(1, parts.shape[0]):
            total = total + parts[q].astype(F32)
        return total

    gathered(yn, my, at_y, lambda p: dksend, dkyr, ky_s, ky_r)
    dkzs[...] = jnp.concatenate([shard_of(summed(dkyr)), jnp.zeros((16, 256 - S), F32)], axis=1).astype(BF16)
    spread(zn, mz, at_z, lambda p: dkzs, dkzr, kz_s, kz_r)
    dkzr[mz] = dkzs[...]
    send_x(1)
    send_back(0)
    projected(1, c_ref, cf.at[0:H, 0:W], din_ref)
    gathered(zn, mz, at_z, lambda p: dkzs, dkzr, kz_s, kz_r)
    dkxs[...] = summed(dkzr).astype(BF16)
    spread(xn, mx, at_x, lambda p: dkxs, dkxr, kx_s, kx_r)
    dkxr[mx] = dkxs[...]
    send_back(1)

    own_gate = shard_of(gate)
    lefts, rights = pairs3(grad_squeeze * scale, shard_of(own(pooled)))
    dse1_ref[...] = lax.dot_general(lefts, rights, TN_DIMS, preferred_element_type=F32)[0:64]
    lefts, rights = pairs3(squeeze_act, shard_of(own(excite)) * scale)
    dse2_ref[...] = lax.dot_general(lefts, rights, TN_DIMS, preferred_element_type=F32)[0:64]
    gate_wide = lax.dot_general(split3(own_gate * scale), ones, TN_DIMS, preferred_element_type=F32)
    projected(0, x_ref, xf.at[0:H, 0:W], out_ref)
    whole(0, gacc.at[0:S])
    dwp_ref[...] = gacc[0:S] * gate_wide
    gathered(xn, mx, at_x, lambda p: dkxs, dkxr, kx_s, kx_r)
    dk_ref[...] = summed(dkxr)[0:9, 0:S] * scale
    whole(1, gacc.at[S:2 * S])
    dwe_ref[...] = gacc[S:2 * S] * scale


def settle(*refs):
    count = (len(refs) - 1) // 2
    moves = [pltpu.make_async_copy(refs[k], refs[count + k], refs[-1].at[k]) for k in range(count)]
    for move in moves:
        move.start()
    for move in moves:
        move.wait()


def per_device(inputs, w_expand, kernel, w_se1, w_se2, w_project, cotangent):
    rows_n, ch_n = lax.axis_size("rows"), lax.axis_size("ch")
    zn = CHIPS_Z if rows_n % CHIPS_Z == 0 else 2
    xn, yn = rows_n // zn, ch_n // 2
    ce = S * yn
    nt = ce // 128
    zr = S // (zn // 2)
    grad_scale = 1.0 / math.sqrt(rows_n * H * ch_n * W)
    vmem, dma = pltpu.VMEM, pltpu.SemaphoreType.DMA
    scratch = [
        vmem((H, W, C), BF16), vmem((S, C), BF16), vmem((9, S), BF16), vmem((64, S), BF16), vmem((64, S), BF16),
        vmem((S, C), BF16), vmem((H, W, C), BF16),
        vmem((H, W, C), BF16), vmem((H, W, C), BF16),
        vmem((2, 3 * W, C), BF16), vmem((2, 2, 3 * W, C), BF16),
        vmem((3 * H, C), BF16), vmem((2, 3, 3 * H, C), BF16),
        vmem((yn, S, C), BF16), vmem((yn, S, C), BF16),
        vmem((S, 128), BF16), vmem((2, yn, S, 128), BF16),
        vmem((16, 256), BF16), vmem((yn, 16, 256), BF16),
        vmem((H + 4, PW, C), F32), vmem((H + 2, PW, C), F32),
        vmem(((H + 4) * PW, C), BF16), vmem(((H + 2) * PW, C), BF16),
        vmem((H, 64, C), BF16), vmem((H, 64, C), BF16),
        vmem((nt, H + 4, PW, 128), F32), vmem((nt, H + 4, PW, 128), F32),
        vmem((nt, H + 2, PW, 128), F32), vmem((nt, H + 2, PW, 128), F32),
        vmem((nt, H, 64, 128), F32), vmem((nt, H, 64, 128), F32),
        vmem((H, 64, ce), BF16), vmem((H, 64, ce), BF16),
        vmem((nt, 16, 128), F32), vmem((ce, C), F32), vmem((nt, 16, 128), F32),
        vmem((16, 128), F32), vmem((zn, 16, 128), F32), vmem((xn, 16, 128), F32), vmem((ch_n, 16, 128), F32),
        vmem((2, 8, 128), F32),
        vmem((2, yn, S, C), BF16), vmem((2, yn, S, C), BF16),
        vmem((2, zn, zr, 128), BF16), vmem((2, zn, zr, 128), BF16),
        vmem((2, xn, zr, 128), BF16), vmem((2, 2, zr, 128), BF16), vmem((2, zn, zr, 128), BF16),
        vmem((16, ce), BF16), vmem((yn, 16, ce), BF16),
        vmem((zn, 16, 256), BF16), vmem((16, 256), BF16), vmem((xn, 16, 256), BF16), vmem((16, 256), BF16),
        vmem((2, H, W, C), BF16), vmem((2, H, W, C), BF16),
        dma((7,)), dma((2,)), dma((2,)), dma((2, 2)), dma((2, 2)), dma((3, 2)), dma((2, 3)),
        dma((yn,)), dma((yn,)), dma((yn,)), dma((yn,)),
        dma((yn,)), dma((yn,)), dma((1,)), dma((2,)), dma((yn,)), dma((yn,)),
        dma((zn,)), dma((zn,)), dma((xn,)), dma((xn,)), dma((ch_n,)), dma((ch_n,)),
        dma((2, yn)), dma((2, yn)), dma((2, zn)), dma((2, zn)), dma((2, xn)), dma((2, xn)), dma((2, zn)), dma((2, zn)),
        dma((yn,)), dma((yn,)), dma((zn,)), dma((zn,)), dma((xn,)), dma((xn,)),
        dma((2,)), dma((2,)),
    ]
    anywhere = pl.BlockSpec(memory_space=pl.ANY)
    in_vmem = pl.BlockSpec(memory_space=pltpu.VMEM)
    shapes = (
        jax.ShapeDtypeStruct((1, H, W, C), BF16), jax.ShapeDtypeStruct((1, H, W, C), BF16),
        jax.ShapeDtypeStruct((S, C), F32), jax.ShapeDtypeStruct((9, S), F32),
        jax.ShapeDtypeStruct((64, S), F32), jax.ShapeDtypeStruct((64, S), F32),
        jax.ShapeDtypeStruct((S, C), F32))
    results = pl.pallas_call(
        functools.partial(fused, rows_n, ch_n, grad_scale),
        out_shape=shapes,
        in_specs=[anywhere] * 7,
        out_specs=(in_vmem,) * 7,
        scratch_shapes=scratch,
        compiler_params=pltpu.CompilerParams(
            collective_id=0, has_side_effects=True, vmem_limit_bytes=56 * 1024 * 1024),
    )(inputs, w_expand.T, kernel, w_se1.T, w_se2, w_project, cotangent)
    output, d_input, d_expand_t, d_taps, d_se1_t, d_se2, d_project = pl.pallas_call(
        settle,
        out_shape=shapes,
        in_specs=[anywhere] * 7,
        out_specs=(in_vmem,) * 7,
        scratch_shapes=[dma((7,))],
    )(*results)
    return output, d_input, d_expand_t.T, d_taps, d_se1_t.T, d_se2, d_project


def solution(mesh):
    return jax.shard_map(
        per_device,
        mesh=mesh,
        in_specs=(
            P(None, "rows", "ch", None),
            P(None, "ch"),
            P(None, "ch"),
            P("ch", None),
            P(None, "ch"),
            P("ch", None),
            P(None, "rows", "ch", None),
        ),
        out_specs=(
            P(None, "rows", "ch", None),
            P(None, "rows", "ch", None),
            P(None, "ch"),
            P(None, "ch"),
            P("ch", None),
            P(None, "ch"),
            P("ch", None),
        ),
        check_vma=False,
    )
```

```python
import functools
import math

import jax
import jax.numpy as jnp
from jax import lax
from jax.experimental import pallas as pl
from jax.experimental.pallas import tpu as pltpu
from jax.sharding import PartitionSpec as P

MESH = pl.DeviceIdType.MESH
F32 = jnp.float32
BF16 = jnp.bfloat16

CHIPS_Z = 8
H = 16
W = 32
C = 256
S = 192
PW = 72
EXPAND_ROWS = 20
GRAD_ROWS = 18
UNROLL = 8
NT_DIMS = (((1,), (1,)), ((), ()))
TN_DIMS = (((0,), (0,)), ((), ()))


def split3(row):
    hi = row.astype(BF16).astype(F32)
    mid = (row - hi).astype(BF16).astype(F32)
    low = row - hi - mid
    rest = jnp.zeros((5, row.shape[1]), F32)
    return jnp.concatenate([hi, mid, low, rest], axis=0).astype(BF16)


def sigm(v):
    return 0.5 * jnp.tanh(0.5 * v) + 0.5


def pairs3(left, right):
    def three(row):
        hi = row.astype(BF16).astype(F32)
        mid = (row - hi).astype(BF16).astype(F32)
        return hi, mid, row - hi - mid

    a, b = three(left), three(right)
    lefts = jnp.concatenate([a[k] for k in (0, 0, 1, 1, 0, 2, 1, 2)], axis=0).astype(BF16)
    rights = jnp.concatenate([b[k] for k in (0, 1, 0, 1, 2, 0, 2, 1)], axis=0).astype(BF16)
    return lefts, rights


def fused(rows_n, ch_n, scale, x_in, we_in, tap_in, se1_in, se2_in, wp_in, c_in,
          out_ref, din_ref, dwe_ref, dk_ref, dse1_ref, dse2_ref, dwp_ref,
          x_ref, we_ref, tap_ref, se1_ref, se2_ref, wp_ref, c_ref, xsib, csib, rowsend, rowbuf, colsend, colbuf, webuf, wpbuf, sesend, sebuf, tapsend, tapbuf,
          xf, cf, xs, cs, xnat, cnat, a1, s1, gh, s2, ca, cb, act2, ge, ktile, gacc, dkacc,
          vbuf, zv, xv, cv, gs, ysend, yrecv, zsend, zrecv, xrecv, fsend, frecv,
          dksend, dkyr, dkzr, dkxs, dkxr, dkzs, posend, porecv,
          load_s, sib_s, sib_r, row_s, row_r, col_s, col_r, we_s, we_r, wp_s, wp_r, se_s, se_r, rel_s, rel_r, tap_s, tap_r,
          vz_s, vz_r, vx_s, vx_r, vc_s, vc_r, gy_s, gy_r, gz_s, gz_r, gx_s, gx_r, gf_s, gf_r,
          ky_s, ky_r, kz_s, kz_r, kx_s, kx_r, po_s, po_r):
    zn = CHIPS_Z if rows_n % CHIPS_Z == 0 else 2
    xn = rows_n // zn
    yn = ch_n // 2
    ce = S * yn
    nt = ce // 128
    pairs = yn // 2
    zr = S // (zn // 2)
    row = lax.axis_index("rows")
    ch = lax.axis_index("ch")
    mx, mz = row // zn, lax.rem(row, zn)
    my, mc = ch // 2, lax.rem(ch, 2)
    oc = 1 - mc

    def dev_row(step):
        return lax.rem(row + step + rows_n, rows_n)

    def dev_y(step):
        return lax.rem(my + step + yn, yn)

    def copy(src, dst, ssem, rsem, where):
        return pltpu.make_async_remote_copy(
            src_ref=src, dst_ref=dst, send_sem=ssem, recv_sem=rsem, device_id=where, device_id_type=MESH)

    def at_y(peer):
        return (row, peer * 2 + mc)

    def at_z(peer):
        return (mx * zn + peer, ch)

    def at_x(peer):
        return (peer * zn + mz, ch)

    def at_ch(peer):
        return (row, peer)

    def spread(n, me, at, src, land, ssem, rsem):
        for step in range(1, n):
            peer = lax.rem(me + step, n)
            copy(src(peer), land.at[me], ssem.at[step - 1], rsem.at[me], at(peer)).start()

    def gathered(n, me, at, src, land, ssem, rsem):
        for step in range(1, n):
            peer = lax.rem(me + step, n)
            copy(src(peer), land.at[peer], ssem.at[step - 1], rsem.at[peer], at(peer)).wait()

    pair_mine = my // 2
    near = my + 1 - 2 * lax.rem(my, 2)
    far = [lax.rem(pair_mine + b, pairs) * 2 + k for b in range(1, pairs) for k in (0, 1)]

    def to_y(peers, first, src, land, ssem, rsem):
        for k, peer in enumerate(peers):
            copy(src(peer), land.at[my], ssem.at[first + k], rsem.at[my], at_y(peer)).start()

    def from_y(peers, first, src, land, ssem, rsem):
        for k, peer in enumerate(peers):
            copy(src(peer), land.at[peer], ssem.at[first + k], rsem.at[peer], at_y(peer)).wait()

    barrier = pltpu.get_barrier_semaphore()
    partners = [at_ch(lax.rem(ch + s, ch_n)) for s in range(1, ch_n)]
    partners += [at_z(lax.rem(mz + s, zn)) for s in range(1, zn)]
    partners += [at_x(lax.rem(mx + s, xn)) for s in range(1, xn)]
    partners += [(dev_row(dr), my * 2 + core) for dr in (-1, 1) for core in (0, 1)]
    partners += [(dev_row(dr), dev_y(dy) * 2 + core) for dr in (-1, 1) for dy in (-1, 1) for core in (0, 1)]
    for where in partners:
        pl.semaphore_signal(barrier, inc=1, device_id=where, device_id_type=MESH)

    arrays = ((x_in.at[0], x_ref), (c_in.at[0], c_ref), (we_in, we_ref), (tap_in, tap_ref), (se1_in, se1_ref),
              (se2_in, se2_ref), (wp_in, wp_ref))
    loads = [pltpu.make_async_copy(source, into, load_s.at[k]) for k, (source, into) in enumerate(arrays)]
    for load in loads:
        load.start()
    for load in loads:
        load.wait()

    for d, (lo, edge) in enumerate(((0, 0), (H - 2, H - 1))):
        rowsend[d, 0:2 * W] = x_ref[lo:lo + 2].reshape(2 * W, C)
        rowsend[d, 2 * W:3 * W] = c_ref[edge]
    first = mc * (W - 2)
    ri = lax.broadcasted_iota(jnp.int32, (2 * H, H * W), 0)
    ci = lax.broadcasted_iota(jnp.int32, (2 * H, H * W), 1)
    pick = (ci == (ri & (H - 1)) * W + first + (ri >> 4)).astype(F32).astype(BF16)
    colsend[0:2 * H] = jnp.dot(pick, x_ref[...].reshape(H * W, C), preferred_element_type=F32).astype(BF16)
    ri = lax.broadcasted_iota(jnp.int32, (H, H * W), 0)
    ci = lax.broadcasted_iota(jnp.int32, (H, H * W), 1)
    pick = (ci == ri * W + mc * (W - 1)).astype(F32).astype(BF16)
    colsend[2 * H:3 * H] = jnp.dot(pick, c_ref[...].reshape(H * W, C), preferred_element_type=F32).astype(BF16)

    eye = (lax.broadcasted_iota(jnp.int32, (S, S), 0) == lax.broadcasted_iota(jnp.int32, (S, S), 1)).astype(F32).astype(BF16)
    se_t = jnp.concatenate([se1_ref[...], se2_ref[...]], axis=0)
    sesend[...] = lax.dot_general(eye, se_t, NT_DIMS, preferred_element_type=F32).astype(BF16)
    tap_rows = jnp.concatenate([tap_ref[...].astype(F32), jnp.zeros((7, S), F32)], axis=0)
    tapsend[...] = jnp.concatenate([tap_rows, jnp.zeros((16, 256 - S), F32)], axis=1).astype(BF16)

    pl.semaphore_wait(barrier, len(partners))

    sib = (row, my * 2 + oc)
    sib_copies = [copy(x_ref, xsib, sib_s.at[0], sib_r.at[0], sib), copy(c_ref, csib, sib_s.at[1], sib_r.at[1], sib)]
    row_copies = []
    for d, dr in ((0, -1), (1, 1)):
        for core in (0, 1):
            row_copies.append((copy(rowsend.at[d], rowbuf.at[1 - d, mc], row_s.at[d, core], row_r.at[1 - d, mc],
                                    (dev_row(dr), my * 2 + core)),
                               copy(rowsend.at[d], rowbuf.at[1 - d, core], row_s.at[d, core], row_r.at[1 - d, core],
                                    (dev_row(dr), my * 2 + core))))
    col_copies = []
    side = 1 - mc
    for i, dr in enumerate((-1, 0, 1)):
        for core in (0, 1):
            where = (dev_row(dr), dev_y(2 * mc - 1) * 2 + core)
            col_copies.append((copy(colsend, colbuf.at[side, 2 - i], col_s.at[i, core], col_r.at[side, 2 - i], where),
                               copy(colsend, colbuf.at[core, i], col_s.at[i, core], col_r.at[core, i], where)))
    sib_copies[0].start()
    for sent, _ in row_copies + col_copies:
        sent.start()
    to_y([near], 0, lambda p: we_ref, webuf, we_s, we_r)
    spread(yn, my, at_y, lambda p: tapsend, tapbuf, tap_s, tap_r)
    sib_copies[1].start()
    to_y(far, 1, lambda p: we_ref, webuf, we_s, we_r)
    to_y([near] + far, 0, lambda p: wp_ref, wpbuf, wp_s, wp_r)
    spread(yn, my, at_y, lambda p: sesend, sebuf.at[mc], se_s, se_r)
    relay = copy(sebuf.at[mc], sebuf.at[mc], rel_s.at[0], rel_r.at[mc], sib)
    relayed = copy(sebuf.at[mc], sebuf.at[oc], rel_s.at[0], rel_r.at[oc], sib)

    webuf[my] = we_ref[...]
    wpbuf[my] = wp_ref[...]
    tapbuf[my] = tapsend[...]
    sebuf[mc, my] = sesend[...]
    mine = pl.ds(pl.multiple_of(mc * W, W), W)
    other = pl.ds(pl.multiple_of(oc * W, W), W)
    xf[2:2 + H, mine] = x_ref[...].astype(F32)
    cf[1:1 + H, mine] = c_ref[...].astype(F32)
    xnat[:, mine] = x_ref[...]
    cnat[:, mine] = c_ref[...]
    sib_copies[0].wait()
    xf[2:2 + H, other] = xsib[...].astype(F32)
    xnat[:, other] = xsib[...]
    for _, landed in row_copies + col_copies:
        landed.wait()

    top_ok = row > 0
    low_ok = row < rows_n - 1
    left_ok = my > 0
    right_ok = my < yn - 1
    for d, ok in ((0, top_ok), (1, low_ok)):
        for core in (0, 1):
            part = rowbuf[d, core].astype(F32) * jnp.where(ok, 1.0, 0.0)
            xf[(2 + H) * d:(2 + H) * d + 2, W * core:W * core + W] = part[0:2 * W].reshape(2, W, C)
            cf[(1 + H) * d, W * core:W * core + W] = part[2 * W:3 * W]
    cols = colbuf[...].reshape(2 * 3 * 48, C)

    def rim(height, above, left_slot, right_slot):
        shape = (height * 8, 288)
        out_row = lax.broadcasted_iota(jnp.int32, shape, 0)
        src = lax.broadcasted_iota(jnp.int32, shape, 1)
        place = out_row & 7
        at_row = (out_row >> 3) - above
        third = jnp.where(at_row < 0, 0, jnp.where(at_row < H, 1, 2))
        ok = jnp.where(at_row < 0, top_ok.astype(jnp.int32), jnp.where(at_row < H, 1, low_ok.astype(jnp.int32)))
        want = third * 48 + (at_row & (H - 1))
        right_of = jnp.where(place < 4, 1, 0)
        slot = jnp.where(place < 4, right_slot(place), left_slot(place))
        ok = ok * jnp.where(slot < 0, 0, 1) * jnp.where(place < 4, right_ok.astype(jnp.int32), left_ok.astype(jnp.int32))
        want = want + right_of * 144 + slot * 16
        hit = jnp.where(src == want, ok, 0).astype(F32).astype(BF16)
        return jnp.dot(hit, cols, preferred_element_type=F32).reshape(height, 8, C)

    xf[:, 64:72] = rim(H + 4, 2, lambda k: jnp.where(k >= 6, k - 6, -1), lambda k: jnp.where(k < 2, k, -1))

    @pl.loop(0, (H + 4) // 2)
    def _(i):
        at = pl.ds(pl.multiple_of(i * 2 * PW, 2 * PW), 2 * PW)
        xs[at] = xf[pl.ds(i * 2, 2)].reshape(2 * PW, C).astype(BF16)

    gathered(yn, my, at_y, lambda p: tapsend, tapbuf, tap_s, tap_r)
    wide = jnp.concatenate([tapbuf[q].astype(F32)[:, 0:S] for q in range(yn)], axis=1)
    for t in range(nt):
        ktile[t] = wide[:, 128 * t:128 * t + 128]
    from_y([near], 0, lambda p: we_ref, webuf, we_s, we_r)

    for b in range(pairs):
        pair = lax.rem(pair_mine + b, pairs)
        if b == 1:
            from_y(far, 1, lambda p: we_ref, webuf, we_s, we_r)
        w_exp = webuf[pl.ds(pair * 2, 2)].reshape(2 * S, C)

        @pl.loop(0, (H + 4) // EXPAND_ROWS)
        def _(i):
            step = EXPAND_ROWS * PW
            at = pl.ds(pl.multiple_of(i * step, step), step)
            pre = lax.dot_general(xs[at], w_exp, NT_DIMS, preferred_element_type=F32)
            sig = sigm(pre)
            act = pre * sig
            slope = sig * (1.0 + (pre - act))
            for t in range(3):
                there = pl.ds(i * EXPAND_ROWS, EXPAND_ROWS)
                a1[pair * 3 + t, there] = act[:, 128 * t:128 * t + 128].reshape(EXPAND_ROWS, PW, 128)
                s1[pair * 3 + t, there] = slope[:, 128 * t:128 * t + 128].reshape(EXPAND_ROWS, PW, 128)

        @pl.loop(0, 3)
        def _(t3):
            t = pair * 3 + t3
            lanes = pl.ds(pl.multiple_of(t * 128, 128), 128)
            taps = [ktile[t, k:k + 1] for k in range(9)]

            def one_row(i):
                rows = [a1[t, i + r] for r in range(3)]
                parts = [taps[c] * rows[0] + taps[3 + c] * rows[1] + taps[6 + c] * rows[2] for c in range(3)]
                pre = parts[1] + pltpu.roll(parts[0], 1, 0) + pltpu.roll(parts[2], PW - 1, 0)
                sig = sigm(pre)
                act = pre * sig
                s2[t, i] = sig * (1.0 + (pre - act))
                return act[0:64]

            def center(i, pool):
                act = one_row(i)
                act2[i - 1, :, lanes] = act.astype(BF16)
                return pool + jnp.sum(act.reshape(8, 8, 128), axis=0)

            one_row(0)
            one_row(H + 1)
            pool = lax.fori_loop(1, H + 1, center, jnp.zeros((8, 128), F32), unroll=UNROLL)
            vbuf[pl.ds(t, 1)] = jnp.sum(pool, axis=0, keepdims=True)

    sib_copies[1].wait()
    cf[1:1 + H, other] = csib[...].astype(F32)
    cnat[:, other] = csib[...]
    cot_flat = cnat[...].reshape(H * 64, C)
    from_y([near] + far, 0, lambda p: wp_ref, wpbuf, wp_s, wp_r)
    ones = jnp.ones((8, C), F32).astype(BF16)
    for t in range(ce // 384):
        rows = lax.dot_general(
            act2[:, :, 384 * t:384 * t + 384].reshape(H * 64, 384), cot_flat, TN_DIMS, preferred_element_type=F32)
        gacc[384 * t:384 * t + 384] = rows
        prod = rows * wpbuf[2 * t:2 * t + 2].reshape(384, C).astype(F32)
        hi = prod.astype(BF16)
        rest = prod - hi.astype(F32)
        mid = rest.astype(BF16)
        low = (rest - mid.astype(F32)).astype(BF16)
        gate_sum = sum(lax.dot_general(ones, part, NT_DIMS, preferred_element_type=F32) for part in (hi, mid, low))
        for k in range(3):
            vbuf[8 + 3 * t + k:9 + 3 * t + k] = gate_sum[0:1, 128 * k:128 * k + 128]

    for t in range(nt, 8):
        vbuf[t:t + 1] = jnp.zeros((1, 128), F32)
        vbuf[8 + t:9 + t] = jnp.zeros((1, 128), F32)

    spread(zn, mz, at_z, lambda p: vbuf, zv, vz_s, vz_r)
    zv[mz] = vbuf[...]

    def send_rows(g, value):
        ysend[g] = value.reshape(yn, S, C).astype(BF16)
        to_y([near] + far, 0, lambda p: ysend.at[g, p], yrecv.at[g], gy_s.at[g], gy_r.at[g])
        yrecv[g, my] = ysend[g, my]

    def send_z(g):
        from_y([near] + far, 0, lambda p: ysend.at[g, p], yrecv.at[g], gy_s.at[g], gy_r.at[g])
        total = yrecv[g, 0].astype(F32)
        for q in range(1, yn):
            total = total + yrecv[g, q].astype(F32)
        for q in range(zn):
            zsend[g, q] = total[zr * (q // 2):zr * (q // 2) + zr, 128 * (q % 2):128 * (q % 2) + 128].astype(BF16)
        spread(zn, mz, at_z, lambda p: zsend.at[g, p], zrecv.at[g], gz_s.at[g], gz_r.at[g])
        zrecv[g, mz] = zsend[g, mz]

    def send_x(g):
        gathered(zn, mz, at_z, lambda p: zsend.at[g, p], zrecv.at[g], gz_s.at[g], gz_r.at[g])
        total = zrecv[g, 0].astype(F32)
        for q in range(1, zn):
            total = total + zrecv[g, q].astype(F32)
        fsend[g, 0] = total.astype(BF16)
        spread(xn, mx, at_x, lambda p: fsend.at[g, 0], xrecv.at[g], gx_s.at[g], gx_r.at[g])
        xrecv[g, mx] = fsend[g, 0]

    def send_back(g):
        gathered(xn, mx, at_x, lambda p: fsend.at[g, 0], xrecv.at[g], gx_s.at[g], gx_r.at[g])
        total = xrecv[g, 0].astype(F32)
        for q in range(1, xn):
            total = total + xrecv[g, q].astype(F32)
        fsend[g, 1] = total.astype(BF16)
        spread(zn, mz, at_z, lambda p: fsend.at[g, 1], frecv.at[g], gf_s.at[g], gf_r.at[g])
        frecv[g, mz] = fsend[g, 1]

    def whole(g, into):
        gathered(zn, mz, at_z, lambda p: fsend.at[g, 1], frecv.at[g], gf_s.at[g], gf_r.at[g])
        for q in range(zn):
            into[zr * (q // 2):zr * (q // 2) + zr, 128 * (q % 2):128 * (q % 2) + 128] = frecv[g, q].astype(F32)

    send_rows(0, gacc[...])
    gathered(yn, my, at_y, lambda p: sesend, sebuf.at[mc], se_s, se_r)
    relay.start()

    cf[:, 64:72] = rim(H + 2, 1, lambda k: jnp.where(k == 7, 2, -1), lambda k: jnp.where(k == 0, 2, -1))

    @pl.loop(0, (H + 2) // 2)
    def _(i):
        at = pl.ds(pl.multiple_of(i * 2 * PW, 2 * PW), 2 * PW)
        cs[at] = cf[pl.ds(i * 2, 2)].reshape(2 * PW, C).astype(BF16)

    def hidden_grad(pair):
        w_pro = wpbuf[2 * pair:2 * pair + 2].reshape(2 * S, C)

        @pl.loop(0, (H + 2) // GRAD_ROWS)
        def _(i):
            step = GRAD_ROWS * PW
            at = pl.ds(pl.multiple_of(i * step, step), step)
            back = lax.dot_general(cs[at], w_pro, NT_DIMS, preferred_element_type=F32)
            for t in range(3):
                gh[pair * 3 + t, pl.ds(i * GRAD_ROWS, GRAD_ROWS)] = back[:, 128 * t:128 * t + 128].reshape(GRAD_ROWS, PW, 128)

    place = lax.broadcasted_iota(jnp.int32, (PW, 128), 0)
    off_left = jnp.where(left_ok, PW, PW - 1)
    off_right = jnp.where(right_ok, 0, 1)
    inside = jnp.where((place < 64) | ((place == 64) & (off_right == 0)) | ((place == PW - 1) & (off_left == PW)), 1.0, 0.0)

    def depth_back(pair):
        @pl.loop(0, 3)
        def _(t3):
            t = pair * 3 + t3
            taps = [ktile[t, k:k + 1] for k in range(9)]

            @pl.loop(0, H + 2, unroll=2)
            def _(i):
                keep = jnp.where(((i > 0) | top_ok) & ((i < H + 1) | low_ok), 1.0, 0.0)
                slope = s2[t, i] * (inside * keep)
                s2[t, i] = slope
                gh[t, i] = gh[t, i] * slope

            @pl.loop(0, H, unroll=UNROLL)
            def _(i):
                first_slope = s1[t, i + 2, 0:64]
                for source, into in ((gh, ca), (s2, cb)):
                    rows = [source[t, i + r] for r in range(3)]
                    parts = [taps[c] * rows[2] + taps[3 + c] * rows[1] + taps[6 + c] * rows[0] for c in range(3)]
                    grad = parts[1] + pltpu.roll(parts[0], PW - 1, 0) + pltpu.roll(parts[2], 1, 0)
                    into[t, i] = grad[0:64] * first_slope

    for pair in range(pairs):
        hidden_grad(pair)
    gathered(zn, mz, at_z, lambda p: vbuf, zv, vz_s, vz_r)
    xv[mx] = jnp.sum(zv[...], axis=0)
    spread(xn, mx, at_x, lambda p: xv.at[mx], xv, vx_s, vx_r)
    depth_back(0)
    gathered(xn, mx, at_x, lambda p: xv.at[mx], xv, vx_s, vx_r)
    cv[ch] = jnp.sum(xv[...], axis=0)
    spread(ch_n, ch, at_ch, lambda p: cv.at[ch], cv, vc_s, vc_r)
    send_z(0)
    for pair in range(1, pairs):
        depth_back(pair)
    gathered(ch_n, ch, at_ch, lambda p: cv.at[ch], cv, vc_s, vc_r)
    relayed.wait()

    area = float(rows_n * H * yn * 2 * W)
    pooled, gate_grad, weights = [], [], []
    for core in (0, 1):
        total = cv[core]
        for q in range(1, yn):
            total = total + cv[2 * q + core]
        pooled.append(jnp.concatenate([total[t:t + 1] for t in range(nt)], axis=1) * (1.0 / area))
        gate_grad.append(jnp.concatenate([total[8 + t:9 + t] for t in range(nt)], axis=1))
        weights.append(sebuf[core].reshape(ce, 128))
    half = lax.broadcasted_iota(jnp.int32, (1, 128), 1) < 64

    def down(vectors):
        total = jnp.zeros((1, 128), F32)
        for core in (0, 1):
            total = total + jnp.sum(jnp.dot(split3(vectors[core]), weights[core], preferred_element_type=F32), axis=0, keepdims=True)
        return total

    def up(vector, core):
        return jnp.sum(lax.dot_general(split3(vector), weights[core], NT_DIMS, preferred_element_type=F32), axis=0, keepdims=True)

    squeeze_pre = jnp.where(half, down(pooled), 0.0)
    squeeze_sig = sigm(squeeze_pre)
    squeeze_act = squeeze_pre * squeeze_sig
    shifted = pltpu.roll(jnp.broadcast_to(squeeze_act, (8, 128)), 64, 1)[0:1]
    gates = [sigm(up(shifted, core)) for core in (0, 1)]
    excite = [gate_grad[core] * gates[core] * (1.0 - gates[core]) for core in (0, 1)]
    back = pltpu.roll(jnp.broadcast_to(down(excite), (8, 128)), 64, 1)[0:1]
    squeeze_slope = squeeze_sig * (1.0 + squeeze_pre * (1.0 - squeeze_sig))
    grad_squeeze = jnp.where(half, back * squeeze_slope, 0.0)

    def own(values):
        return jnp.where(mc == 0, values[0], values[1])

    gate = own(gates)
    grad_pool = own([up(grad_squeeze, core) for core in (0, 1)]) * (1.0 / area)
    for t in range(nt):
        gs[0, t:t + 1] = gate[:, 128 * t:128 * t + 128]
        gs[1, t:t + 1] = grad_pool[:, 128 * t:128 * t + 128]
    send_x(0)

    def shard_of(rows):
        part = rows[:, 0:S]
        for q in range(1, yn):
            part = jnp.where(my == q, rows[:, S * q:S * q + S], part)
        return part

    def project(source, k, w_all, into):
        def part(where):
            rows = source[:, where].reshape(H * W, ce)
            return jnp.dot(rows, w_all, preferred_element_type=F32).reshape(H, W, C)

        posend[k] = part(other).astype(BF16)
        copy(posend.at[k], porecv.at[k], po_s.at[k], po_r.at[k], sib).start()
        into[...] = part(mine)

    def projected(k, base, total, into):
        copy(posend.at[k], porecv.at[k], po_s.at[k], po_r.at[k], sib).wait()
        into[0] = (base[...].astype(F32) + (total[...] + porecv[k].astype(F32))).astype(BF16)

    x_flat = xnat[...].reshape(H * 64, C)
    for b in range(pairs):
        pair = lax.rem(pair_mine + 1 + b, pairs)

        @pl.loop(0, 3)
        def _(t3):
            t = pair * 3 + t3
            lanes = pl.ds(pl.multiple_of(t * 128, 128), 128)
            gate_t = gs[0, pl.ds(t, 1)]
            pool_t = gs[1, pl.ds(t, 1)]

            @pl.loop(0, H, unroll=UNROLL)
            def _(i):
                ge[i, :, lanes] = (ca[t, i] * gate_t + cb[t, i] * pool_t).astype(BF16)

        lanes3 = pl.ds(pl.multiple_of(pair * 384, 384), 384)
        rows = lax.dot_general(ge[:, :, lanes3].reshape(H * 64, 384), x_flat, TN_DIMS, preferred_element_type=F32)
        ysend[1, pl.ds(pair * 2, 2)] = rows.reshape(2, S, C).astype(BF16)
        if b < pairs - 1:
            to_y(far, 1, lambda p: ysend.at[1, p], yrecv.at[1], gy_s.at[1], gy_r.at[1])
        else:
            to_y([near], 0, lambda p: ysend.at[1, p], yrecv.at[1], gy_s.at[1], gy_r.at[1])
            yrecv[1, my] = ysend[1, my]

    project(ge, 1, webuf[...].reshape(ce, C), cf.at[0:H, 0:W])
    @pl.loop(0, nt)
    def _(t):
        gate_t = gs[0, pl.ds(t, 1)]
        pool_t = gs[1, pl.ds(t, 1)]

        def center(i, sums):
            grad = gh[t, i + 1, 0:64] * gate_t + s2[t, i + 1, 0:64] * pool_t
            here = jnp.concatenate([grad, jnp.zeros((8, 128), F32)], axis=0)
            moved = [pltpu.roll(here, PW - 1, 0), here, pltpu.roll(here, 1, 0)]
            fresh = []
            for r in range(3):
                act = a1[t, i + 1 + r]
                for c in range(3):
                    fresh.append(sums[3 * r + c] + jnp.sum((moved[c] * act).reshape(9, 8, 128), axis=0))
            return tuple(fresh)

        sums = lax.fori_loop(0, H, center, (jnp.zeros((8, 128), F32),) * 9, unroll=UNROLL)
        dkacc[t] = jnp.concatenate(
            [jnp.sum(part, axis=0, keepdims=True) for part in sums] + [jnp.zeros((7, 128), F32)], axis=0)

    dksend[...] = jnp.concatenate([dkacc[t] for t in range(nt)], axis=1).astype(BF16)
    spread(yn, my, at_y, lambda p: dksend, dkyr, ky_s, ky_r)
    dkyr[my] = dksend[...]
    send_z(1)

    @pl.loop(0, H)
    def _(i):
        act2[i] = (act2[i].astype(F32) * gate).astype(BF16)

    project(act2, 0, wpbuf[...].reshape(ce, C), xf.at[0:H, 0:W])

    def summed(parts):
        total = parts[0].astype(F32)
        for q in range(1, parts.shape[0]):
            total = total + parts[q].astype(F32)
        return total

    gathered(yn, my, at_y, lambda p: dksend, dkyr, ky_s, ky_r)
    dkzs[...] = jnp.concatenate([shard_of(summed(dkyr)), jnp.zeros((16, 256 - S), F32)], axis=1).astype(BF16)
    spread(zn, mz, at_z, lambda p: dkzs, dkzr, kz_s, kz_r)
    dkzr[mz] = dkzs[...]
    send_x(1)
    send_back(0)
    projected(1, c_ref, cf.at[0:H, 0:W], din_ref)
    gathered(zn, mz, at_z, lambda p: dkzs, dkzr, kz_s, kz_r)
    dkxs[...] = summed(dkzr).astype(BF16)
    spread(xn, mx, at_x, lambda p: dkxs, dkxr, kx_s, kx_r)
    dkxr[mx] = dkxs[...]
    send_back(1)

    own_gate = shard_of(gate)
    lefts, rights = pairs3(grad_squeeze * scale, shard_of(own(pooled)))
    dse1_ref[...] = lax.dot_general(lefts, rights, TN_DIMS, preferred_element_type=F32)[0:64]
    lefts, rights = pairs3(squeeze_act, shard_of(own(excite)) * scale)
    dse2_ref[...] = lax.dot_general(lefts, rights, TN_DIMS, preferred_element_type=F32)[0:64]
    gate_wide = lax.dot_general(split3(own_gate * scale), ones, TN_DIMS, preferred_element_type=F32)
    projected(0, x_ref, xf.at[0:H, 0:W], out_ref)
    whole(0, gacc.at[0:S])
    dwp_ref[...] = gacc[0:S] * gate_wide
    gathered(xn, mx, at_x, lambda p: dkxs, dkxr, kx_s, kx_r)
    dk_ref[...] = summed(dkxr)[0:9, 0:S] * scale
    whole(1, gacc.at[S:2 * S])
    dwe_ref[...] = gacc[S:2 * S] * scale


def settle(*refs):
    count = (len(refs) - 1) // 2
    moves = [pltpu.make_async_copy(refs[k], refs[count + k], refs[-1].at[k]) for k in range(count)]
    for move in moves:
        move.start()
    for move in moves:
        move.wait()


def per_device(inputs, w_expand, kernel, w_se1, w_se2, w_project, cotangent):
    rows_n, ch_n = lax.axis_size("rows"), lax.axis_size("ch")
    zn = CHIPS_Z if rows_n % CHIPS_Z == 0 else 2
    xn, yn = rows_n // zn, ch_n // 2
    ce = S * yn
    nt = ce // 128
    zr = S // (zn // 2)
    grad_scale = 1.0 / math.sqrt(rows_n * H * ch_n * W)
    vmem, dma = pltpu.VMEM, pltpu.SemaphoreType.DMA
    scratch = [
        vmem((H, W, C), BF16), vmem((S, C), BF16), vmem((9, S), BF16), vmem((64, S), BF16), vmem((64, S), BF16),
        vmem((S, C), BF16), vmem((H, W, C), BF16),
        vmem((H, W, C), BF16), vmem((H, W, C), BF16),
        vmem((2, 3 * W, C), BF16), vmem((2, 2, 3 * W, C), BF16),
        vmem((3 * H, C), BF16), vmem((2, 3, 3 * H, C), BF16),
        vmem((yn, S, C), BF16), vmem((yn, S, C), BF16),
        vmem((S, 128), BF16), vmem((2, yn, S, 128), BF16),
        vmem((16, 256), BF16), vmem((yn, 16, 256), BF16),
        vmem((H + 4, PW, C), F32), vmem((H + 2, PW, C), F32),
        vmem(((H + 4) * PW, C), BF16), vmem(((H + 2) * PW, C), BF16),
        vmem((H, 64, C), BF16), vmem((H, 64, C), BF16),
        vmem((nt, H + 4, PW, 128), F32), vmem((nt, H + 4, PW, 128), F32),
        vmem((nt, H + 2, PW, 128), F32), vmem((nt, H + 2, PW, 128), F32),
        vmem((nt, H, 64, 128), F32), vmem((nt, H, 64, 128), F32),
        vmem((H, 64, ce), BF16), vmem((H, 64, ce), BF16),
        vmem((nt, 16, 128), F32), vmem((ce, C), F32), vmem((nt, 16, 128), F32),
        vmem((16, 128), F32), vmem((zn, 16, 128), F32), vmem((xn, 16, 128), F32), vmem((ch_n, 16, 128), F32),
        vmem((2, 8, 128), F32),
        vmem((2, yn, S, C), BF16), vmem((2, yn, S, C), BF16),
        vmem((2, zn, zr, 128), BF16), vmem((2, zn, zr, 128), BF16),
        vmem((2, xn, zr, 128), BF16), vmem((2, 2, zr, 128), BF16), vmem((2, zn, zr, 128), BF16),
        vmem((16, ce), BF16), vmem((yn, 16, ce), BF16),
        vmem((zn, 16, 256), BF16), vmem((16, 256), BF16), vmem((xn, 16, 256), BF16), vmem((16, 256), BF16),
        vmem((2, H, W, C), BF16), vmem((2, H, W, C), BF16),
        dma((7,)), dma((2,)), dma((2,)), dma((2, 2)), dma((2, 2)), dma((3, 2)), dma((2, 3)),
        dma((yn,)), dma((yn,)), dma((yn,)), dma((yn,)),
        dma((yn,)), dma((yn,)), dma((1,)), dma((2,)), dma((yn,)), dma((yn,)),
        dma((zn,)), dma((zn,)), dma((xn,)), dma((xn,)), dma((ch_n,)), dma((ch_n,)),
        dma((2, yn)), dma((2, yn)), dma((2, zn)), dma((2, zn)), dma((2, xn)), dma((2, xn)), dma((2, zn)), dma((2, zn)),
        dma((yn,)), dma((yn,)), dma((zn,)), dma((zn,)), dma((xn,)), dma((xn,)),
        dma((2,)), dma((2,)),
    ]
    anywhere = pl.BlockSpec(memory_space=pl.ANY)
    in_vmem = pl.BlockSpec(memory_space=pltpu.VMEM)
    shapes = (
        jax.ShapeDtypeStruct((1, H, W, C), BF16), jax.ShapeDtypeStruct((1, H, W, C), BF16),
        jax.ShapeDtypeStruct((S, C), F32), jax.ShapeDtypeStruct((9, S), F32),
        jax.ShapeDtypeStruct((64, S), F32), jax.ShapeDtypeStruct((64, S), F32),
        jax.ShapeDtypeStruct((S, C), F32))
    results = pl.pallas_call(
        functools.partial(fused, rows_n, ch_n, grad_scale),
        out_shape=shapes,
        in_specs=[anywhere] * 7,
        out_specs=(in_vmem,) * 7,
        scratch_shapes=scratch,
        compiler_params=pltpu.CompilerParams(
            collective_id=0, has_side_effects=True, vmem_limit_bytes=56 * 1024 * 1024),
    )(inputs, w_expand.T, kernel, w_se1.T, w_se2, w_project, cotangent)
    output, d_input, d_expand_t, d_taps, d_se1_t, d_se2, d_project = pl.pallas_call(
        settle,
        out_shape=shapes,
        in_specs=[anywhere] * 7,
        out_specs=(in_vmem,) * 7,
        scratch_shapes=[dma((7,))],
    )(*results)
    return output, d_input, d_expand_t.T, d_taps, d_se1_t.T, d_se2, d_project


def solution(mesh):
    return jax.shard_map(
        per_device,
        mesh=mesh,
        in_specs=(
            P(None, "rows", "ch", None),
            P(None, "ch"),
            P(None, "ch"),
            P("ch", None),
            P(None, "ch"),
            P("ch", None),
            P(None, "rows", "ch", None),
        ),
        out_specs=(
            P(None, "rows", "ch", None),
            P(None, "rows", "ch", None),
            P(None, "ch"),
            P(None, "ch"),
            P("ch", None),
            P(None, "ch"),
            P("ch", None),
        ),
        check_vma=False,
    )
```
